128 devices in a mesh: row: 4 (over x), col: 8 (over z, core), depth: 4 (over y).
Axes of the slice: x: 4, y: 4, z: 4, core: 2. Of those that a mesh axis runs over, the one named last changes fastest.
Arguments:
- policy_states: bfloat16 [1024, 5120], P(('col', 'depth'), 'row'), may hold values from -40 to 40
- reference_states: bfloat16 [1024, 5120], P(('row', 'col', 'depth')), may hold values from -40 to 40
- policy_weight: bfloat16 [5120, 81920], P('row', ('col', 'depth'))
- reference_weight: bfloat16 [5120, 81920], P(None, ('row', 'col', 'depth'))
- targets: int32 [1024], replicated, may hold values from 0 to 81919
- response_mask: int32 [1024], replicated, may hold values from 0 to 1, as said below
- pair_index: int32 [8], replicated, may hold values from 0 to 3, as said below
- chosen_flag: int32 [8], replicated, may hold values from 0 to 1, as said below
Outputs:
- loss: float32 [], replicated
- grad_states: float32 [1024, 5120], P(('col', 'depth'), 'row')
- grad_weight: float32 [5120, 81920], P('row', ('col', 'depth'))
The draws below stay inside these ranges and needn't reach their ends.
Inputs may be any that keep to these rules, and one draw needn't show every extreme that they name: `response_mask`: in each sequence of 128 tokens the ones form one run of at least 32 tokens that begins at or after position 16. `pair_index`: each pair names exactly two sequences. `chosen_flag`: the two sequences of a pair have flags 1 and 0.
All inputs are finite; a program needn't handle non-finite values.
Results may differ from the reference program's by a relative error of at most 0.0022.
Values may be sent and summed in bfloat16 or wider, within the bound.
A program may use at most 128 MiB of HBM per device.

```python
import math
import jax
import jax.numpy as jnp
import numpy as np
from jax import lax

D = 5120
VOCAB = 81920
PAIRS = 4
LEN = 128
SEQS = 8
TOKENS = 1024


def column_block(key, columns):

    def one_column(column):
        return jnp.clip(jax.random.normal(jax.random.fold_in(key, column), (D,), jnp.float32), -6.0, 6.0)
    return jax.vmap(one_column, out_axes=1)(columns) * (3.0 / math.sqrt(D))


def policy_columns(key, columns):
    return column_block(jax.random.fold_in(key, 101), columns)


def reference_columns(key, columns):
    return column_block(jax.random.fold_in(key, 202), columns)


def draw_policy_states(key, part):
    key = jax.random.fold_in(key, 1)
    keys = jax.random.split(key, 1)
    base = jax.random.normal(keys[0], (TOKENS, D), jnp.float32)
    return jnp.clip(base, -40.0, 40.0).astype(jnp.bfloat16)


def draw_reference_states(key, part):
    key = jax.random.fold_in(key, 2)
    keys = jax.random.split(key, 1)
    base = jax.random.normal(keys[0], (TOKENS, D), jnp.float32)
    return jnp.clip(base, -40.0, 40.0).astype(jnp.bfloat16)


def draw_policy_weight(key, part):
    return policy_columns(key, jnp.arange(VOCAB, dtype=jnp.int32)).astype(jnp.bfloat16)


def draw_reference_weight(key, part):
    return reference_columns(key, jnp.arange(VOCAB, dtype=jnp.int32)).astype(jnp.bfloat16)


def draw_response_mask(key, part):
    key = jax.random.fold_in(key, 3)
    keys = jax.random.split(key, 2)
    starts = jax.random.randint(keys[0], (SEQS, 1), LEN // 8, LEN // 2)
    ends = jax.random.randint(keys[1], (SEQS, 1), 3 * LEN // 4, LEN + 1)
    positions = jnp.arange(LEN, dtype=jnp.int32)[None, :]
    inside = (positions >= starts) & (positions < ends)
    return inside.astype(jnp.int32).reshape(TOKENS)


def pairing(key):
    return jax.random.permutation(jax.random.fold_in(key, 5), SEQS)


def draw_pair_index(key, part):
    order = pairing(key)
    return (order // 2).astype(jnp.int32)


def draw_chosen_flag(key, part):
    order = pairing(key)
    return (order % 2).astype(jnp.int32)


def place_ends(drawn, stream_key, low, top_value):
    extent = drawn.shape
    spot = [jax.random.randint(jax.random.fold_in(stream_key, axis), (), 0, extent[axis]) for axis in range(len(extent))]
    drawn = drawn.at[tuple(spot)].set(low)
    longest = extent.index(max(extent))
    spot[longest] = (spot[longest] + 1) % extent[longest]
    return drawn.at[tuple(spot)].set(top_value)


def skewed_wide(key, shape, count, skew):
    weights = [min(1 << octave, count + 1 - (1 << octave)) * (1 << 20) // math.isqrt((1 << octave) ** skew) + 1 for octave in range((count + 1).bit_length()) if 1 << octave <= count]
    deviation = 1 + sum(weights) // (1 << 30)
    table = np.cumsum(np.array([max(1, weight // deviation) for weight in weights]))
    ticket = jax.random.randint(jax.random.fold_in(key, 1), shape, 0, int(table[len(weights) - 1]))
    start = jnp.left_shift(1, jnp.searchsorted(jnp.asarray(table, jnp.int32), ticket, side="right").astype(jnp.int32))
    standing = start - 1 + jax.random.randint(jax.random.fold_in(key, 4), shape, 0, 1 << 30) % jnp.minimum(start, count + 1 - start)
    return jax.random.permutation(jax.random.fold_in(key, 2), count)[standing].astype(jnp.int32)


def setup_inputs(seed: int = 0) -> dict:
    streams_of = jax.random.split(jax.random.key(seed), 9)
    return {
        "policy_states": draw_policy_states(jax.random.fold_in(streams_of[8], 71), 0),
        "reference_states": draw_reference_states(jax.random.fold_in(streams_of[8], 71), 0),
        "policy_weight": draw_policy_weight(jax.random.fold_in(streams_of[8], 71), 0),
        "reference_weight": draw_reference_weight(jax.random.fold_in(streams_of[8], 71), 0),
        "targets": place_ends(skewed_wide(streams_of[4], (TOKENS,), VOCAB, 2), jax.random.fold_in(streams_of[4], 3), 0, VOCAB - 1).astype(jnp.int32),
        "response_mask": draw_response_mask(jax.random.fold_in(streams_of[8], 71), 0),
        "pair_index": draw_pair_index(jax.random.fold_in(streams_of[8], 71), 0),
        "chosen_flag": draw_chosen_flag(jax.random.fold_in(streams_of[8], 71), 0),
    }


beta_value = 0.1
loss_scale = 256.0


def preference(ratio, pair_index, chosen_flag):
    sign = (2 * chosen_flag - 1).astype(jnp.float32)
    member = pair_index[:, None] == jnp.arange(PAIRS, dtype=jnp.int32)[None, :]
    margin = jnp.sum(jnp.where(member, (sign * ratio)[:, None], 0.0), axis=0)
    loss = -jnp.mean(jax.nn.log_sigmoid(beta_value * margin))
    slope = (-loss_scale * beta_value / PAIRS) * jax.nn.sigmoid(-beta_value * margin)
    weights = sign * jnp.sum(jnp.where(member, slope[None, :], 0.0), axis=1)
    return loss, weights


def vocabulary_logp(states, weight, targets):
    blocks = states.reshape(SEQS, LEN, D)
    wanted_blocks = targets.reshape(SEQS, LEN)

    def one_block(pair):
        block, wanted = pair
        logits = jnp.dot(block, weight, preferred_element_type=jnp.float32)
        peak = jnp.max(logits, axis=1)
        normalizer = peak + jnp.log(jnp.sum(jnp.exp(logits - peak[:, None]), axis=1))
        picked = jnp.take_along_axis(logits, wanted[:, None].astype(jnp.int32), axis=1)[:, 0]
        return picked - normalizer, normalizer

    logp, normalizer = lax.map(one_block, (blocks, wanted_blocks))
    return logp.reshape(TOKENS), normalizer.reshape(TOKENS)


def reference(policy_states, reference_states, policy_weight, reference_weight, targets, response_mask, pair_index, chosen_flag):
    policy_logp, normalizer = vocabulary_logp(policy_states, policy_weight, targets)
    reference_logp = vocabulary_logp(reference_states, reference_weight, targets)[0]
    mask_all = response_mask.astype(jnp.float32)
    ratio = jnp.sum(((policy_logp - reference_logp) * mask_all).reshape(SEQS, LEN), axis=1)
    loss, weights = preference(ratio, pair_index, chosen_flag)
    token_weight = jnp.repeat(weights, LEN) * mask_all
    entries = jnp.arange(VOCAB, dtype=jnp.int32)

    def grad_block(carry, pair):
        block, wanted, scale, norm_rows = pair
        logits = jnp.dot(block, policy_weight, preferred_element_type=jnp.float32)
        softmax_rows = jnp.exp(logits - norm_rows[:, None])
        hits = entries[None, :] == wanted[:, None]
        grad_logits = (scale[:, None] * (hits.astype(jnp.float32) - softmax_rows)).astype(jnp.bfloat16)
        carry = carry + jnp.dot(block.T, grad_logits, preferred_element_type=jnp.float32)
        return carry, jnp.dot(grad_logits, policy_weight.T, preferred_element_type=jnp.float32)

    grad_weight, state_blocks = lax.scan(
        grad_block,
        jnp.zeros((D, VOCAB), jnp.float32),
        (policy_states.reshape(SEQS, LEN, D), targets.reshape(SEQS, LEN),
         token_weight.reshape(SEQS, LEN), normalizer.reshape(SEQS, LEN)))
    return loss, state_blocks.reshape(TOKENS, D), grad_weight
```

```python
import functools

import jax
import jax.numpy as jnp
from jax import lax
from jax.experimental import pallas as pl
from jax.experimental.pallas import tpu as pltpu
from jax.sharding import PartitionSpec as P

PAIRS = 4
LEN = 128
SEQS = 8
SKIP = 16
KEEP = LEN - SKIP

beta_value = 0.1
loss_scale = 256.0

MESH = pl.DeviceIdType.MESH
VMEM_LIMIT = 56 * 1024 * 1024
ROWS = 16


def preference(ratio, pair_index, chosen_flag):
    sign = (2 * chosen_flag - 1).astype(jnp.float32)
    member = pair_index[:, None] == jnp.arange(PAIRS, dtype=jnp.int32)[None, :]
    margin = jnp.sum(jnp.where(member, (sign * ratio)[:, None], 0.0), axis=0)
    loss = -jnp.mean(jax.nn.log_sigmoid(beta_value * margin))
    slope = -loss_scale * beta_value / PAIRS * jax.nn.sigmoid(-beta_value * margin)
    weights = sign * jnp.sum(jnp.where(member, slope[None, :], 0.0), axis=1)
    return (loss, weights)


class Place:
    def __init__(self):
        self.x = lax.axis_index("row")
        col = lax.axis_index("col")
        self.z = col // 2
        self.c = col % 2
        self.y = lax.axis_index("depth")

    def on_x(self, step):
        return ((self.x + step) % 4, self.z * 2 + self.c, self.y)

    def on_y(self, step):
        return (self.x, self.z * 2 + self.c, (self.y + step) % 4)

    def on_z(self, step):
        return (self.x, ((self.z + step) % 4) * 2 + self.c, self.y)

    def other_core(self):
        return (self.x, self.z * 2 + 1 - self.c, self.y)


def greet(peers):
    barrier = pltpu.get_barrier_semaphore()
    for peer in peers:
        pl.semaphore_signal(barrier, inc=1, device_id=peer, device_id_type=MESH)
    pl.semaphore_wait(barrier, len(peers))


class Mover:
    def __init__(self, send, recv):
        self.send, self.recv, self.used, self.all = send, recv, 0, []

    def start(self, src, dst, peer):
        k = self.used
        self.used += 1
        copy = pltpu.make_async_remote_copy(
            src_ref=src,
            dst_ref=dst,
            send_sem=self.send.at[k],
            recv_sem=self.recv.at[k],
            device_id=peer,
            device_id_type=MESH,
        )
        copy.start()
        self.all.append(copy)
        return copy

    def finish(self):
        for copy in self.all:
            copy.wait_send()


class Ring:
    def __init__(self, mover, me, view, peer):
        self.mover, self.me, self.view, self.peer = mover, me, view, peer

    def begin(self):
        own = self.view(self.me, None)
        self.right = self.mover.start(own, own, self.peer(1))
        self.left = self.mover.start(own, own, self.peer(3))

    def forward(self):
        self.right.wait_recv()
        part = self.view((self.me + 3) % 4, 0)
        self.far_right = self.mover.start(part, part, self.peer(1))
        self.left.wait_recv()
        part = self.view((self.me + 1) % 4, 1)
        self.far_left = self.mover.start(part, part, self.peer(3))

    def end(self):
        self.far_right.wait_recv()
        self.far_left.wait_recv()


def gather_kernel(own_ref, out, send, recv):
    at = Place()
    z, c, y = at.z, at.c, at.y
    greet([at.on_y(1), at.on_y(3), at.on_z(1), at.on_z(3), at.other_core()])
    move = Mover(send, recv)
    width = own_ref.shape[1] // 2
    low, high = pl.ds(0, width), pl.ds(width, width)
    out[z, c, y] = own_ref[...]

    def halves(half, count):
        return slice(None) if half is None else pl.ds(half * (count // 2), count // 2)

    rows = own_ref.shape[0]
    first_y = Ring(move, y, lambda i, h: out.at[z, c, i, halves(h, rows), low], at.on_y)
    first_z = Ring(move, z, lambda i, h: out.at[i, c, y, halves(h, rows), high], at.on_z)
    then_z = Ring(move, z, lambda i, h: out.at[i, c, halves(h, 4), :, low], at.on_z)
    then_y = Ring(move, y, lambda i, h: out.at[halves(h, 4), c, i, :, high], at.on_y)
    first_y.begin()
    first_z.begin()
    first_y.forward()
    first_z.forward()
    first_y.end()
    then_z.begin()
    first_z.end()
    then_y.begin()
    then_z.forward()
    then_y.forward()
    then_z.end()
    half = out.at[:, c, :, :, low]
    one = move.start(half, half, at.other_core())
    then_y.end()
    half = out.at[:, c, :, :, high]
    two = move.start(half, half, at.other_core())
    one.wait_recv()
    two.wait_recv()
    move.finish()


def gather_states(block):
    rows, width = block.shape
    out = pl.pallas_call(
        gather_kernel,
        name="gather_states",
        out_shape=jax.ShapeDtypeStruct((4, 2, 4, rows, width), block.dtype),
        in_specs=[pl.BlockSpec(memory_space=pltpu.VMEM)],
        out_specs=pl.BlockSpec(memory_space=pltpu.VMEM),
        scratch_shapes=[pltpu.SemaphoreType.DMA((18,)), pltpu.SemaphoreType.DMA((18,))],
        compiler_params=pltpu.CompilerParams(
            collective_id=0, has_side_effects=True, vmem_limit_bytes=VMEM_LIMIT
        ),
    )(block)
    return out.reshape(32 * rows, width)


def logits_kernel(
    states, weight, targets, out, stats, partial, qsend, qrecv, ssend, srecv, column, send, recv
):
    at = Place()
    x = at.x
    greet([at.on_x(1), at.on_x(3)])
    move = Mover(send, recv)
    share, width = partial.shape[1], partial.shape[2]
    half = width // 2
    tile = 512
    padded = column.shape[0]

    def product(owner):
        rows = pl.ds(pl.multiple_of(owner * share, 16), share)

        @pl.loop(0, width // tile)
        def _(j):
            cols = pl.ds(pl.multiple_of(j * tile, tile), tile)
            partial[owner, :, cols] = jnp.dot(
                states[rows, :], weight[:, cols], preferred_element_type=jnp.float32
            )

    def scale_column(k):
        row = jnp.broadcast_to(srecv[k, 0:1, :], (128, padded))
        return jnp.transpose(row)

    def pack(k, owner, side, peer, add=None):
        cols = pl.ds(side * half, half)
        if add is not None:
            column[...] = scale_column(add)

        @pl.loop(0, share // ROWS)
        def _(r):
            rows = pl.ds(pl.multiple_of(r * ROWS, ROWS), ROWS)
            value = partial[owner, rows, cols]
            if add is not None:
                value += qrecv[add, rows, :].astype(jnp.int32).astype(jnp.float32) * column[rows, 0:1]
            top = jnp.maximum(jnp.max(jnp.abs(value), axis=1, keepdims=True), 1e-30)
            step = top * (1.0 / 32767.0)
            code = jnp.round(value * (1.0 / step)).astype(jnp.int32)
            qsend[k, rows, :] = code.astype(jnp.int16)
            column[rows, :] = jnp.broadcast_to(step, (ROWS, 128))

        ssend[k] = jnp.transpose(column[...])[0:8]
        return (
            move.start(ssend.at[k], srecv.at[k], peer),
            move.start(qsend.at[k], qrecv.at[k], peer),
        )

    def arrived(pair):
        pair[0].wait_recv()
        pair[1].wait_recv()

    right, left = at.on_x(1), at.on_x(3)
    after, before, across = (x + 1) % 4, (x + 3) % 4, (x + 2) % 4
    column[...] = jnp.zeros_like(column)
    product(across)
    r0 = pack(0, across, 0, right)
    l0 = pack(3, across, 1, left)
    product(after)
    r1 = pack(1, after, 1, right)
    product(before)
    l1 = pack(4, before, 0, left)
    product(x)
    arrived(r0)
    r2 = pack(2, after, 0, right, add=0)
    arrived(l0)
    l2 = pack(5, before, 1, left, add=3)

    def add_in(k, side):
        cols = pl.ds(side * half, half)
        column[...] = scale_column(k)

        @pl.loop(0, share // ROWS)
        def _(r):
            rows = pl.ds(pl.multiple_of(r * ROWS, ROWS), ROWS)
            partial[x, rows, cols] += (
                qrecv[k, rows, :].astype(jnp.int32).astype(jnp.float32) * column[rows, 0:1]
            )

    arrived(r1)
    add_in(1, 1)
    arrived(l1)
    add_in(4, 0)
    arrived(r2)
    add_in(2, 0)
    arrived(l2)
    add_in(5, 1)

    first = (lax.axis_index("col") * 4 + lax.axis_index("depth")) * width

    @pl.loop(0, share // ROWS)
    def _(r):
        rows = pl.ds(pl.multiple_of(r * ROWS, ROWS), ROWS)
        logits = partial[x, rows, :]
        peak = jnp.max(logits, axis=1, keepdims=True)
        spread = jnp.exp(logits - peak)
        out[x, rows, :] = spread.astype(jnp.bfloat16)
        total = jnp.sum(spread, axis=1, keepdims=True)
        wanted = targets[pl.ds(pl.multiple_of(x * share, 16) + r * ROWS, ROWS), :]
        hits = lax.broadcasted_iota(jnp.int32, (ROWS, width), 1) + first == wanted
        picked = jnp.sum(jnp.where(hits, logits, 0.0), axis=1, keepdims=True)
        lane = lax.broadcasted_iota(jnp.int32, (ROWS, 128), 1)
        column[rows, :] = jnp.where(lane == 0, peak, jnp.where(lane == 1, total, picked))

    def part(i, side):
        return out.at[i] if side is None else out.at[i, :, pl.ds(side * half, half)]

    ring = Ring(move, x, part, at.on_x)
    ring.begin()
    stats[...] = jnp.transpose(column[...])[0:8]
    ring.forward()
    ring.end()
    move.finish()


def spread_logits(states, weight, targets):
    tokens, width = states.shape[0], weight.shape[1]
    share = tokens // 4
    padded = 256
    vmem = pl.BlockSpec(memory_space=pltpu.VMEM)
    return pl.pallas_call(
        logits_kernel,
        name="spread_logits",
        out_shape=(
            jax.ShapeDtypeStruct((4, share, width), jnp.bfloat16),
            jax.ShapeDtypeStruct((8, padded), jnp.float32),
        ),
        in_specs=[vmem] * 3,
        out_specs=(vmem, vmem),
        scratch_shapes=[
            pltpu.VMEM((4, share, width), jnp.float32),
            pltpu.VMEM((6, share, width // 2), jnp.int16),
            pltpu.VMEM((6, share, width // 2), jnp.int16),
            pltpu.VMEM((6, 8, padded), jnp.float32),
            pltpu.VMEM((6, 8, padded), jnp.float32),
            pltpu.VMEM((padded, 128), jnp.float32),
            pltpu.SemaphoreType.DMA((16,)),
            pltpu.SemaphoreType.DMA((16,)),
        ],
        compiler_params=pltpu.CompilerParams(
            collective_id=1, has_side_effects=True, vmem_limit_bytes=VMEM_LIMIT
        ),
    )(states, weight, targets)


def merge(a, b):
    peak = jnp.maximum(a[..., 0:1, :], b[..., 0:1, :])
    total = a[..., 1:2, :] * jnp.exp(a[..., 0:1, :] - peak) + b[..., 1:2, :] * jnp.exp(
        b[..., 0:1, :] - peak
    )
    return jnp.concatenate([peak, total, a[..., 2:3, :] + b[..., 2:3, :], a[..., 3:, :]], axis=-2)


def stats_kernel(policy, other, out, first, held, got, send, recv):
    at = Place()
    x = at.x
    ways = [at.on_x, at.on_y, at.on_z]
    greet([way(i) for way in ways for i in (1, 2, 3)] + [at.other_core()])
    move = Mover(send, recv)
    copies = [
        move.start(other.at[(x + i) % 4], first.at[i - 1], at.on_x(i)) for i in (1, 2, 3)
    ]
    mine = other[x]
    for i in (0, 1, 2):
        copies[i].wait_recv()
        mine = merge(mine, first[i])
    both = jnp.stack([policy[...], mine])
    stages = [[at.other_core()], [at.on_y(i) for i in (1, 2, 3)], [at.on_z(i) for i in (1, 2, 3)]]
    slot = 0
    for s, peers in enumerate(stages):
        held[s] = both
        copies = []
        for peer in peers:
            copies.append((slot, move.start(held.at[s], got.at[slot], peer)))
            slot += 1
        for k, copy in copies:
            copy.wait_recv()
            both = merge(both, got[k])
    out[x] = both
    copies = [move.start(out.at[x], out.at[x], at.on_x(i)) for i in (1, 2, 3)]
    for copy in copies:
        copy.wait_recv()
    move.finish()


def combine_stats(policy, other):
    vmem = pl.BlockSpec(memory_space=pltpu.VMEM)
    padded = policy.shape[1]
    return pl.pallas_call(
        stats_kernel,
        name="combine_stats",
        out_shape=jax.ShapeDtypeStruct((4, 2, 8, padded), jnp.float32),
        in_specs=[vmem] * 2,
        out_specs=vmem,
        scratch_shapes=[
            pltpu.VMEM((3, 8, padded), jnp.float32),
            pltpu.VMEM((3, 2, 8, padded), jnp.float32),
            pltpu.VMEM((7, 2, 8, padded), jnp.float32),
            pltpu.SemaphoreType.DMA((13,)),
            pltpu.SemaphoreType.DMA((13,)),
        ],
        compiler_params=pltpu.CompilerParams(
            collective_id=2, has_side_effects=True, vmem_limit_bytes=VMEM_LIMIT
        ),
    )(policy, other)


def rows_kernel(part, out, core, by_z, by_y, sum_z, sum_y, send, recv):
    at = Place()
    z, c, y = at.z, at.c, at.y
    ways = [at.on_y, at.on_z]
    greet([way(i) for way in ways for i in (1, 2, 3)] + [at.other_core()])
    move = Mover(send, recv)
    width = part.shape[4] // 2
    sides = (pl.ds(0, width), pl.ds(width, width))
    first = [
        move.start(part.at[:, 1 - c, :, :, side], core.at[i], at.other_core())
        for i, side in enumerate(sides)
    ]
    first[0].wait_recv()
    first[1].wait_recv()

    @pl.loop(0, 16)
    def _(k):
        core[0, k // 4, k % 4] += part[k // 4, c, k % 4, :, sides[0]]
        core[1, k // 4, k % 4] += part[k // 4, c, k % 4, :, sides[1]]

    a = [move.start(core.at[0, (z + i) % 4], by_z.at[i - 1], at.on_z(i)) for i in (1, 3, 2)]
    b = [move.start(core.at[1, :, (y + i) % 4], by_y.at[i - 1], at.on_y(i)) for i in (1, 3, 2)]
    for copy in a:
        copy.wait_recv()

    @pl.loop(0, 4)
    def _(k):
        sum_z[k] = core[0, z, k] + by_z[0, k] + by_z[1, k] + by_z[2, k]

    a = [
        move.start(sum_z.at[(y + i) % 4], by_z.at[3, i - 1], at.on_y(i)) for i in (1, 3, 2)
    ]
    for copy in b:
        copy.wait_recv()

    @pl.loop(0, 4)
    def _(k):
        sum_y[k] = core[1, k, y] + by_y[0, k] + by_y[1, k] + by_y[2, k]

    b = [
        move.start(sum_y.at[(z + i) % 4], by_y.at[3, i - 1], at.on_z(i)) for i in (1, 3, 2)
    ]
    for copy in a:
        copy.wait_recv()
    out[:, sides[0]] = sum_z[y] + by_z[3, 0] + by_z[3, 1] + by_z[3, 2]
    for copy in b:
        copy.wait_recv()
    out[:, sides[1]] = sum_y[z] + by_y[3, 0] + by_y[3, 1] + by_y[3, 2]
    move.finish()


def scatter_rows(part):
    vmem = pl.BlockSpec(memory_space=pltpu.VMEM)
    rows, width = part.shape[0] // 32, part.shape[1]
    half = width // 2
    return pl.pallas_call(
        rows_kernel,
        name="scatter_rows",
        out_shape=jax.ShapeDtypeStruct((rows, width), jnp.float32),
        in_specs=[vmem],
        out_specs=vmem,
        scratch_shapes=[
            pltpu.VMEM((2, 4, 4, rows, half), jnp.float32),
            pltpu.VMEM((4, 4, rows, half), jnp.float32),
            pltpu.VMEM((4, 4, rows, half), jnp.float32),
            pltpu.VMEM((4, rows, half), jnp.float32),
            pltpu.VMEM((4, rows, half), jnp.float32),
            pltpu.SemaphoreType.DMA((14,)),
            pltpu.SemaphoreType.DMA((14,)),
        ],
        compiler_params=pltpu.CompilerParams(
            collective_id=3, has_side_effects=True, vmem_limit_bytes=VMEM_LIMIT
        ),
    )(part.reshape(4, 2, 4, rows, width))


def on_device(
    policy_states,
    reference_states,
    policy_weight,
    reference_weight,
    targets,
    response_mask,
    pair_index,
    chosen_flag,
):
    width = policy_weight.shape[1]
    reference_width = reference_weight.shape[1]
    mask_all = response_mask.astype(jnp.float32)
    others = lax.all_gather(reference_states, ("row", "col", "depth"), axis=0, tiled=True)

    gathered = gather_states(policy_states)
    tokens = SEQS * KEEP
    states = gathered.reshape(SEQS, LEN, -1)[:, SKIP:].reshape(tokens, -1)
    kept_targets = targets.reshape(SEQS, LEN)[:, SKIP:].reshape(tokens, 1)
    kept_mask = mask_all.reshape(SEQS, LEN)[:, SKIP:].reshape(tokens)
    sequence = jnp.arange(tokens, dtype=jnp.int32) // KEEP
    spread, policy_stats = spread_logits(states, policy_weight, kept_targets)

    reference_entries = lax.axis_index(("row", "col", "depth")) * reference_width + jnp.arange(
        reference_width, dtype=jnp.int32
    )
    others, spread = lax.optimization_barrier((others, spread))
    reference_logits = jnp.dot(others, reference_weight, preferred_element_type=jnp.float32)
    reference_peak = jnp.max(reference_logits, axis=1)
    reference_total = jnp.sum(jnp.exp(reference_logits - reference_peak[:, None]), axis=1)
    hits = reference_entries[None, :] == targets[:, None]
    reference_picked = jnp.sum(jnp.where(hits, reference_logits, 0.0), axis=1)
    reference_stats = jnp.zeros((4, 8, 256), jnp.float32)
    reference_stats = reference_stats.at[:, 0].set(reference_peak.reshape(4, 256))
    reference_stats = reference_stats.at[:, 1].set(reference_total.reshape(4, 256))
    reference_stats = reference_stats.at[:, 2].set(reference_picked.reshape(4, 256))

    local_peak = policy_stats[0:1]
    policy_stats = jnp.concatenate([policy_stats[:3], local_peak, policy_stats[4:]], axis=0)
    merged = combine_stats(policy_stats, reference_stats)
    share = tokens // 4
    mine = merged[:, 0, :, :share]
    normalizer = (mine[:, 0] + jnp.log(mine[:, 1])).reshape(tokens)
    policy_logp = mine[:, 2].reshape(tokens) - normalizer
    peak = mine[:, 3].reshape(tokens)
    theirs = merged[:, 1]
    reference_logp = (theirs[:, 2] - theirs[:, 0] - jnp.log(theirs[:, 1])).reshape(SEQS, LEN)
    member = sequence[:, None] == jnp.arange(SEQS, dtype=jnp.int32)[None, :]
    policy_sums = jnp.sum(jnp.where(member, (policy_logp * kept_mask)[:, None], 0.0), axis=0)
    reference_sums = jnp.sum(reference_logp * mask_all.reshape(SEQS, LEN), axis=1)
    loss, weights = preference(policy_sums - reference_sums, pair_index, chosen_flag)
    token_weight = jnp.sum(jnp.where(member, weights[None, :], 0.0), axis=1) * kept_mask

    entries = lax.axis_index(("col", "depth")) * width + jnp.arange(width, dtype=jnp.int32)
    hits = entries[None, :] == kept_targets
    softmax = spread.reshape(tokens, width).astype(jnp.float32) * jnp.exp(peak - normalizer)[:, None]
    grad_logits = (token_weight[:, None] * (hits.astype(jnp.float32) - softmax)).astype(jnp.bfloat16)
    rows_part = lax.dot_general(
        grad_logits, policy_weight, (((1,), (1,)), ((), ())), preferred_element_type=jnp.float32
    )
    rows_part = jnp.pad(rows_part.reshape(SEQS, KEEP, -1), ((0, 0), (SKIP, 0), (0, 0)))
    grad_states = scatter_rows(rows_part.reshape(SEQS * LEN, -1))
    grad_weight = lax.dot_general(
        states, grad_logits, (((0,), (0,)), ((), ())), preferred_element_type=jnp.float32
    )
    return (loss, grad_states, grad_weight)


def solution(mesh):
    in_specs = (
        P(("col", "depth"), "row"),
        P(("row", "col", "depth"), None),
        P("row", ("col", "depth")),
        P(None, ("row", "col", "depth")),
        P(),
        P(),
        P(),
        P(),
    )
    out_specs = (P(), P(("col", "depth"), "row"), P("row", ("col", "depth")))
    return jax.shard_map(
        on_device, mesh=mesh, in_specs=in_specs, out_specs=out_specs, check_vma=False
    )
```

```python
import functools

import jax
import jax.numpy as jnp
from jax import lax
from jax.experimental import pallas as pl
from jax.experimental.pallas import tpu as pltpu
from jax.sharding import PartitionSpec as P

PAIRS = 4
LEN = 128
SEQS = 8
SKIP = 16
KEEP = LEN - SKIP
SIZES = (160, 176, 192, 2 * KEEP)

beta_value = 0.1
loss_scale = 256.0

MESH = pl.DeviceIdType.MESH
VMEM_LIMIT = 62 * 1024 * 1024
ROWS = 16


def preference(ratio, pair_index, chosen_flag):
    sign = (2 * chosen_flag - 1).astype(jnp.float32)
    member = pair_index[:, None] == jnp.arange(PAIRS, dtype=jnp.int32)[None, :]
    margin = jnp.sum(jnp.where(member, (sign * ratio)[:, None], 0.0), axis=0)
    loss = -jnp.mean(jax.nn.log_sigmoid(beta_value * margin))
    slope = -loss_scale * beta_value / PAIRS * jax.nn.sigmoid(-beta_value * margin)
    weights = sign * jnp.sum(jnp.where(member, slope[None, :], 0.0), axis=1)
    return (loss, weights)


class Place:
    def __init__(self):
        self.x = lax.axis_index("row")
        col = lax.axis_index("col")
        self.z = col // 2
        self.c = col % 2
        self.y = lax.axis_index("depth")

    def on_x(self, step):
        return ((self.x + step) % 4, self.z * 2 + self.c, self.y)

    def on_y(self, step):
        return (self.x, self.z * 2 + self.c, (self.y + step) % 4)

    def on_z(self, step):
        return (self.x, ((self.z + step) % 4) * 2 + self.c, self.y)

    def partner_y(self):
        return (self.x, self.z * 2 + self.c, self.y + 1 - 2 * (self.y % 2))

    def other_core(self):
        return (self.x, self.z * 2 + 1 - self.c, self.y)


def greet(peers):
    barrier = pltpu.get_barrier_semaphore()
    for peer in peers:
        pl.semaphore_signal(barrier, inc=1, device_id=peer, device_id_type=MESH)
    pl.semaphore_wait(barrier, len(peers))


class Mover:
    def __init__(self, send, recv):
        self.send, self.recv, self.used, self.all = send, recv, 0, []

    def start(self, src, dst, peer):
        k = self.used
        self.used += 1
        copy = pltpu.make_async_remote_copy(
            src_ref=src,
            dst_ref=dst,
            send_sem=self.send.at[k],
            recv_sem=self.recv.at[k],
            device_id=peer,
            device_id_type=MESH,
        )
        copy.start()
        self.all.append(copy)
        return copy

    def sent(self, copy):
        copy.wait_send()
        self.all = [other for other in self.all if other is not copy]

    def finish(self):
        for copy in self.all:
            copy.wait_send()


class Ring:
    def __init__(self, mover, me, view, peer):
        self.mover, self.me, self.view, self.peer = mover, me, view, peer

    def begin(self):
        own = self.view(self.me, None)
        self.right = self.mover.start(own, own, self.peer(1))
        self.left = self.mover.start(own, own, self.peer(3))

    def forward(self):
        self.right.wait_recv()
        part = self.view((self.me + 3) % 4, 0)
        self.far_right = self.mover.start(part, part, self.peer(1))
        self.left.wait_recv()
        part = self.view((self.me + 1) % 4, 1)
        self.far_left = self.mover.start(part, part, self.peer(3))

    def end(self):
        self.far_right.wait_recv()
        self.far_left.wait_recv()


def merge(a, b):
    peak = jnp.maximum(a[..., 0:1, :], b[..., 0:1, :])
    total = a[..., 1:2, :] * jnp.exp(a[..., 0:1, :] - peak) + b[..., 1:2, :] * jnp.exp(
        b[..., 0:1, :] - peak
    )
    return jnp.concatenate([peak, total, a[..., 2:3, :] + b[..., 2:3, :], a[..., 3:, :]], axis=-2)


def span(half, count):
    return slice(None) if half is None else pl.ds(half * (count // 2), count // 2)


def fused_kernel(
    own,
    ref_own,
    weight,
    ref_weight,
    masks,
    wanted,
    pairs,
    loss,
    rows_out,
    grad_out,
    kept,
    gathered,
    ref_half,
    ref_got,
    refs,
    partial,
    qsend,
    qrecv,
    ssend,
    srecv,
    column,
    spread,
    ref_logits,
    ref_column,
    ref_wanted,
    ref_stats,
    ref_first,
    held,
    got,
    info,
    token_weights,
    grad,
    grad_full,
    rows_all,
    keep,
    core_send,
    core_recv,
    y_send,
    y_recv,
    z_send,
    z_recv,
    z_sum,
    row_ssend,
    row_srecv,
    send,
    recv,
    local,
):
    at = Place()
    x, z, c, y = at.x, at.z, at.c, at.y
    share, width = spread.shape[1], spread.shape[2]
    depth = own.shape[1]
    half = width // 2
    f32, bf16 = jnp.float32, jnp.bfloat16
    ways = [at.on_x, at.on_y, at.on_z]
    greet([way(i) for way in ways for i in (1, 2, 3)] + [at.other_core()])
    move = Mover(send, recv)

    gathered[z, c, y] = own[...]
    low, high = pl.ds(0, depth // 2), pl.ds(depth // 2, depth // 2)
    count = own.shape[0]
    first_y = Ring(move, y, lambda i, h: gathered.at[z, c, i, span(h, count), low], at.on_y)
    first_z = Ring(move, z, lambda i, h: gathered.at[i, c, y, span(h, count), high], at.on_z)
    then_z = Ring(move, z, lambda i, h: gathered.at[i, c, span(h, 4), :, low], at.on_z)
    then_y = Ring(move, y, lambda i, h: gathered.at[span(h, 4), c, i, :, high], at.on_y)
    first_y.begin()
    first_z.begin()

    side, pair = y % 2, y // 2
    ref_depth = ref_own.shape[1]
    quarter = ref_depth // 4
    for k in (0, 1):
        ref_half[k] = ref_own[:, k * 2 * quarter : (k + 1) * 2 * quarter].astype(f32)
    swap = move.start(ref_half.at[1 - side], ref_got, at.partner_y())
    column[...] = jnp.zeros_like(column)
    first_y.forward()
    first_z.forward()
    swap.wait_recv()
    mine, theirs = ref_half[side], ref_got[...]
    block = jnp.concatenate(
        [jnp.where(side == 0, mine, theirs), jnp.where(side == 0, theirs, mine)], axis=0
    ).astype(bf16)
    for f in (0, 1):
        refs[x, z, c, f, pair, side] = block[:, f * quarter : (f + 1) * quarter]
    ref_x = Ring(
        move,
        x,
        lambda i, h: refs.at[i, z, c, slice(None) if h is None else h, pair, side],
        at.on_x,
    )
    ref_y = Ring(move, y, lambda i, h: refs.at[span(h, 4), z, c, 0, i // 2, i % 2], at.on_y)
    ref_z = Ring(move, z, lambda i, h: refs.at[span(h, 4), i, c, 1, pair, side], at.on_z)
    ref_yz = Ring(move, z, lambda i, h: refs.at[span(h, 4), i, c, 0], at.on_z)
    ref_zy = Ring(move, y, lambda i, h: refs.at[span(h, 4), :, c, 1, i // 2, i % 2], at.on_y)
    ref_core = []

    def to_core(ring, i):
        part = ring.view((ring.me + i) % 4, None)
        ref_core.append(move.start(part, part, at.other_core()))

    first_y.end()
    then_z.begin()
    first_z.end()
    then_y.begin()
    ref_x.begin()

    def runs(owner):
        lane = lax.broadcasted_iota(jnp.int32, (1, 2 * LEN), 1)
        mask = masks[owner]
        a = jnp.where(lane < LEN, mask, 0)
        b = jnp.where(lane < LEN, 0, mask)
        return (
            jnp.sum(a, axis=1, keepdims=True),
            jnp.sum(b, axis=1, keepdims=True),
            jnp.min(jnp.where(a > 0, lane, 2 * LEN), axis=1, keepdims=True),
            jnp.min(jnp.where(b > 0, lane, 2 * LEN), axis=1, keepdims=True),
        )

    def source(owner, i):
        len_a, len_b, start_a, start_b = runs(owner)
        second = jnp.where(i < len_a + len_b, start_b + i - len_a, -1)
        return jnp.where(i < len_a, start_a + i, second)

    def kept_masks(owner):
        len_a, len_b, _, _ = runs(owner)
        i = lax.broadcasted_iota(jnp.int32, (1, 2 * LEN), 1)
        a = (i < len_a).astype(f32)
        return a, (i < len_a + len_b).astype(f32) - a

    def to_column(row):
        return jnp.transpose(jnp.broadcast_to(row, (128, row.shape[1])))

    for k in range(4):
        ref_wanted[k] = to_column(wanted[k].astype(f32))

    def kept_source(owner):
        return source(owner, lax.broadcasted_iota(jnp.int32, (share, 1), 0))

    def kept_targets(owner):
        lane = lax.broadcasted_iota(jnp.int32, (share, 2 * LEN), 1)
        return jnp.sum(
            jnp.where(lane == kept_source(owner), wanted[owner].astype(f32), 0.0), axis=1, keepdims=True
        )

    then_z.forward()
    then_y.forward()
    ref_x.forward()
    then_z.end()
    view = gathered.at[:, c, :, :, low]
    one = move.start(view, view, at.other_core())
    then_y.end()
    view = gathered.at[:, c, :, :, high]
    two = move.start(view, view, at.other_core())
    ref_x.end()
    ref_y.begin()
    ref_z.begin()
    one.wait_recv()
    two.wait_recv()

    tile = 512

    def product(owner):
        lane = lax.broadcasted_iota(jnp.int32, (share, 2 * LEN), 1)
        choose = (lane == kept_source(owner)).astype(bf16)
        whole = gathered[owner].reshape(2 * LEN, depth)
        kept[owner] = jnp.dot(choose, whole, preferred_element_type=f32).astype(bf16)

        @pl.loop(0, width // tile)
        def _(j):
            cols = pl.ds(pl.multiple_of(j * tile, tile), tile)
            partial[owner, :, cols] = jnp.dot(
                kept[owner], weight[:, cols], preferred_element_type=f32
            )

    def encode(rows_count, read, write):
        @pl.loop(0, rows_count // ROWS)
        def _(r):
            rows = pl.ds(pl.multiple_of(r * ROWS, ROWS), ROWS)
            value = read(rows)
            top = jnp.maximum(jnp.max(jnp.abs(value), axis=1, keepdims=True), 1e-30)
            step = top * (1.0 / 32767.0)
            write(rows, jnp.round(value * (1.0 / step)).astype(jnp.int32).astype(jnp.int16))
            column[rows, :] = jnp.broadcast_to(step, (ROWS, 128))

        return jnp.transpose(column[...])[0:8]

    def decode(code, rows):
        return code.astype(jnp.int32).astype(f32) * column[rows, 0:1]

    def pack(k, owner, part, peer, add=None):
        cols = pl.ds(part * half, half)
        if add is not None:
            column[...] = to_column(srecv[add, 0:1, :])

        def read(rows):
            value = partial[owner, rows, cols]
            if add is not None:
                value += decode(qrecv[add, rows, :], rows)
            return value

        def write(rows, code):
            qsend[k % 3 % 2 + k // 3 * 2, rows, :] = code

        ssend[k] = encode(share, read, write)
        return (
            move.start(ssend.at[k], srecv.at[k], peer),
            move.start(qsend.at[k % 3 % 2 + k // 3 * 2], qrecv.at[k], peer),
        )

    def arrived(copies):
        for copy in copies:
            copy.wait_recv()

    def add_in(k, part):
        cols = pl.ds(part * half, half)
        column[...] = to_column(srecv[k, 0:1, :])

        @pl.loop(0, share // ROWS)
        def _(r):
            rows = pl.ds(pl.multiple_of(r * ROWS, ROWS), ROWS)
            partial[x, rows, cols] += decode(qrecv[k, rows, :], rows)

    right, left = at.on_x(1), at.on_x(3)
    after, before, across = (x + 1) % 4, (x + 3) % 4, (x + 2) % 4
    product(across)
    r0 = pack(0, across, 0, right)
    l0 = pack(3, across, 1, left)
    ref_y.forward()
    ref_z.forward()
    product(after)
    r1 = pack(1, after, 1, right)
    product(before)
    l1 = pack(4, before, 0, left)
    ref_y.end()
    ref_yz.begin()
    to_core(ref_yz, 0)
    ref_z.end()
    ref_zy.begin()
    to_core(ref_zy, 0)
    product(x)
    arrived(r0)
    move.sent(r0[1])
    r2 = pack(2, after, 0, right, add=0)
    arrived(l0)
    move.sent(l0[1])
    l2 = pack(5, before, 1, left, add=3)
    ref_yz.forward()
    to_core(ref_yz, 1)
    to_core(ref_yz, 3)
    ref_zy.forward()
    to_core(ref_zy, 1)
    to_core(ref_zy, 3)
    arrived(r1)
    add_in(1, 1)
    arrived(l1)
    add_in(4, 0)
    ref_yz.end()
    to_core(ref_yz, 2)
    ref_zy.end()
    to_core(ref_zy, 2)
    arrived(r2)
    add_in(2, 0)
    arrived(l2)
    add_in(5, 1)

    first = (lax.axis_index("col") * 4 + y) * width
    lane = lax.broadcasted_iota(jnp.int32, (ROWS, 128), 1)
    ref_column[0, 0:share, :] = jnp.broadcast_to(kept_targets(x), (share, 128))

    @pl.loop(0, share // ROWS)
    def _(r):
        rows = pl.ds(pl.multiple_of(r * ROWS, ROWS), ROWS)
        logits = partial[x, rows, :]
        peak = jnp.max(logits, axis=1, keepdims=True)
        powers = jnp.exp(logits - peak)
        spread[x, rows, :] = powers.astype(bf16)
        total = jnp.sum(powers, axis=1, keepdims=True)
        entry = (lax.broadcasted_iota(jnp.int32, (ROWS, width), 1) + first).astype(f32)
        picked = jnp.sum(
            jnp.where(entry == ref_column[0, rows, 0:1], logits, 0.0), axis=1, keepdims=True
        )
        column[rows, :] = jnp.where(lane == 0, peak, jnp.where(lane == 1, total, picked))

    ring = Ring(
        move,
        x,
        lambda i, h: spread.at[i] if h is None else spread.at[i, :, pl.ds(h * half, half)],
        at.on_x,
    )
    ring.begin()
    stats = jnp.transpose(column[...])[0:8]
    local_peak = stats[0:1]

    arrived(ref_core)
    ref_width = ref_weight.shape[1]
    ref_entry = lax.axis_index("row") * 32 + lax.axis_index("col") * 4 + y

    @pl.loop(0, 4)
    def _(k):
        for f in (0, 1):
            for h in (0, 1):
                a = refs[:, k, :, f, :, h].reshape(2 * LEN, quarter)
                b = ref_weight[(h * 2 + f) * quarter : (h * 2 + f + 1) * quarter, :]
                d = jnp.dot(a, b, preferred_element_type=f32)
                if f + h == 0:
                    ref_logits[...] = d
                else:
                    ref_logits[...] += d
        for i in range(4):
            rows = pl.ds(i * 64, 64)
            there = pl.ds(pl.multiple_of(k * 64, 64), 64)
            logits = ref_logits[rows, :]
            peak = jnp.max(logits, axis=1, keepdims=True)
            total = jnp.sum(jnp.exp(logits - peak), axis=1, keepdims=True)
            entry = (
                lax.broadcasted_iota(jnp.int32, (64, ref_width), 1) + ref_entry * ref_width
            ).astype(f32)
            picked = jnp.sum(
                jnp.where(entry == ref_wanted[i, there, 0:1], logits, 0.0), axis=1, keepdims=True
            )
            lanes = lax.broadcasted_iota(jnp.int32, (64, 128), 1)
            ref_column[i, there, :] = jnp.where(
                lanes == 0, peak, jnp.where(lanes == 1, total, picked)
            )

    for i in range(4):
        ref_stats[i] = jnp.transpose(ref_column[i])[0:8]
    copies = [
        move.start(ref_stats.at[(x + i) % 4], ref_first.at[i - 1], at.on_x(i)) for i in (1, 2, 3)
    ]
    ring.forward()
    arrived(copies)
    mine = ref_stats[x]
    for i in (0, 1, 2):
        mine = merge(mine, ref_first[i])
    both = jnp.stack([stats, mine])
    stages = [[at.other_core()], [at.on_y(i) for i in (1, 2, 3)], [at.on_z(i) for i in (1, 2, 3)]]
    slot = 0
    for s, peers in enumerate(stages):
        held[s] = both
        copies = [move.start(held.at[s], got.at[slot + k], peer) for k, peer in enumerate(peers)]
        arrived(copies)
        for k in range(len(peers)):
            both = merge(both, got[slot + k])
        slot += len(peers)

    def valid(mask, value):
        return jnp.sum(jnp.where(mask > 0, value, 0.0), axis=1, keepdims=True)

    normalizer = both[0, 0:1] + jnp.log(both[0, 1:2])
    logp = both[0, 2:3] - normalizer
    ref_logp = both[1, 2:3] - both[1, 0:1] - jnp.log(both[1, 1:2])
    mask_a, mask_b = kept_masks(x)
    natural = lax.broadcasted_iota(jnp.int32, (1, 2 * LEN), 1)
    mask = masks[x]
    ratio_a = valid(mask_a, logp) - valid(jnp.where(natural < LEN, mask, 0), ref_logp)
    ratio_b = valid(mask_b, logp) - valid(jnp.where(natural < LEN, 0, mask), ref_logp)
    info[x] = jnp.concatenate(
        [
            normalizer,
            local_peak,
            jnp.broadcast_to(ratio_a, (1, 2 * LEN)),
            jnp.broadcast_to(ratio_b, (1, 2 * LEN)),
            jnp.zeros((4, 2 * LEN), f32),
        ],
        axis=0,
    )
    arrived([move.start(info.at[x], info.at[x], at.on_x(i)) for i in (1, 2, 3)])
    margin = jnp.zeros((SEQS, 2 * LEN), f32)
    for s in range(SEQS):
        margin += pairs[:, s : s + 1] * info[s // 2, 2 + s % 2 : 3 + s % 2, :]
    margin *= beta_value
    log_sigmoid = jnp.minimum(margin, 0.0) - jnp.log1p(jnp.exp(-jnp.abs(margin)))
    loss[...] = jnp.broadcast_to(
        jnp.sum(log_sigmoid, axis=0, keepdims=True)[:, 0:128] * (-1.0 / SEQS), (8, 128)
    )
    weights = (
        (-loss_scale * beta_value / PAIRS)
        * jax.nn.sigmoid(-margin)
        * pairs[:, SEQS : SEQS + 1]
    )
    token_weights[...] = weights

    out_copies = []

    def gradient(order, owner):
        slot = order % 2
        mask_a, mask_b = kept_masks(owner)
        weight_a = token_weights[pl.ds(2 * owner, 1), :]
        weight_b = token_weights[pl.ds(2 * owner + 1, 1), :]
        token = mask_a * weight_a + mask_b * weight_b
        factor = jnp.where(
            mask_a + mask_b > 0, token * jnp.exp(info[owner, 1:2, :] - info[owner, 0:1, :]), 0.0
        )
        column[...] = jnp.transpose(
            jnp.concatenate([token, factor, jnp.zeros((126, 2 * LEN), f32)], axis=0)
        )
        ref_column[0, 0:share, :] = jnp.broadcast_to(kept_targets(owner), (share, 128))
        if order >= 2:
            out_copies[order - 2].wait()

        @pl.loop(0, share // ROWS)
        def _(r):
            rows = pl.ds(pl.multiple_of(r * ROWS, ROWS), ROWS)
            entry = (lax.broadcasted_iota(jnp.int32, (ROWS, width), 1) + first).astype(f32)
            hits = jnp.where(entry == ref_column[0, rows, 0:1], column[rows, 0:1], 0.0)
            grad[slot, rows, :] = (
                hits - column[rows, 1:2] * spread[owner, rows, :].astype(f32)
            ).astype(bf16)

        copy = pltpu.make_async_copy(grad.at[slot], grad_out.at[owner], local.at[order])
        copy.start()
        out_copies.append(copy)
        i = lax.broadcasted_iota(jnp.int32, (1, share), 1)
        place = (
            lax.broadcasted_iota(jnp.int32, (2 * LEN, share), 0) == source(owner, i)
        ).astype(bf16)

        @pl.loop(0, width // tile)
        def _(j):
            cols = pl.ds(pl.multiple_of(j * tile, tile), tile)
            grad_full[:, cols] = jnp.dot(
                place, grad[slot, :, cols], preferred_element_type=f32
            ).astype(bf16)

        @pl.loop(0, depth // 256)
        def _(j):
            cols = pl.ds(pl.multiple_of(j * 256, 256), 256)
            rows_all[:, :, cols] = lax.dot_general(
                grad_full[...],
                weight[cols, :],
                (((1,), (1,)), ((), ())),
                preferred_element_type=f32,
            ).reshape(2, LEN, 256)

        keep[slot] = rows_all[c]

        def write(rows, code):
            core_send[order, rows, :] = code

        row_ssend[order] = encode(LEN, lambda rows: rows_all[1 - c, rows, :], write)
        return [
            move.start(row_ssend.at[order], row_srecv.at[order], at.other_core()),
            move.start(core_send.at[order], core_recv.at[order], at.other_core()),
        ]

    def over_cores(order, copies):
        slot = order % 2
        arrived(copies)
        column[...] = to_column(row_srecv[order, 0:1, :])

        def read(rows):
            value = keep[slot, rows, :] + decode(core_recv[order, rows, :], rows)
            keep[slot, rows, :] = value
            return value

        def write(rows, code):
            y_send[order, rows, :] = code

        row_ssend[4 + order] = encode(LEN, read, write)
        copies = []
        for i in (1, 3, 2):
            there = (y + i) % 4
            k = order * 3 + i - 1
            copies.append(
                move.start(row_ssend.at[4 + order], row_srecv.at[4 + k], at.on_y(i))
            )
            part = y_send.at[order, pl.ds(pl.multiple_of(there * count, count), count), :]
            copies.append(move.start(part, y_recv.at[k], at.on_y(i)))
        return copies

    mine_rows = pl.ds(pl.multiple_of(y * count, count), count)

    def over_y(order, owner, copies):
        arrived(copies)
        total = keep[order % 2, mine_rows, :]
        for i in range(3):
            k = order * 3 + i
            column[...] = to_column(row_srecv[4 + k, 0:1, :])
            total += decode(y_recv[k], mine_rows)
        z_sum[pl.ds(pl.multiple_of(owner * count, count), count), :] = total

    a0 = gradient(0, x)
    a1 = gradient(1, before)
    b0 = over_cores(0, a0)
    over_y(0, x, b0)
    a2 = gradient(2, after)
    b1 = over_cores(1, a1)
    over_y(1, before, b1)
    ring.end()
    a3 = gradient(3, across)
    b2 = over_cores(2, a2)
    b3 = over_cores(3, a3)
    over_y(2, after, b2)
    over_y(3, across, b3)

    def write(rows, code):
        z_send[rows, :] = code

    row_ssend[8] = encode(LEN, lambda rows: z_sum[rows, :], write)
    copies = []
    for i in (1, 3, 2):
        there = (z + i) % 4
        copies.append(move.start(row_ssend.at[8], row_srecv.at[16 + i - 1], at.on_z(i)))
        part = z_send.at[pl.ds(pl.multiple_of(there * count, count), count), :]
        copies.append(move.start(part, z_recv.at[i - 1], at.on_z(i)))
    arrived(copies)
    here = pl.ds(pl.multiple_of(z * count, count), count)
    total = z_sum[here, :]
    for i in range(3):
        column[...] = to_column(row_srecv[16 + i, 0:1, :])
        total += decode(z_recv[i], here)
    rows_out[...] = total
    out_copies[2].wait()
    out_copies[3].wait()
    move.finish()


def fused(index, share, states, others, weight, ref_weight, masks, wanted, pairs):
    vmem = pl.BlockSpec(memory_space=pltpu.VMEM)
    count, depth = states.shape
    width = weight.shape[1]
    ref_rows, ref_depth = others.shape
    quarter = ref_depth // 4
    f32, bf16, i16 = jnp.float32, jnp.bfloat16, jnp.int16
    lanes = 2 * LEN
    copies = 120
    return pl.pallas_call(
        fused_kernel,
        name="fused_%d" % share,
        out_shape=(
            jax.ShapeDtypeStruct((8, 128), f32),
            jax.ShapeDtypeStruct((count, depth), f32),
            jax.ShapeDtypeStruct((4, share, width), bf16),
            jax.ShapeDtypeStruct((4, share, depth), bf16),
        ),
        in_specs=[vmem] * 7,
        out_specs=(vmem, vmem, pl.BlockSpec(memory_space=pl.ANY), vmem),
        scratch_shapes=[
            pltpu.VMEM((4, 2, 4, count, depth), bf16),
            pltpu.VMEM((2, ref_rows, ref_depth // 2), f32),
            pltpu.VMEM((ref_rows, ref_depth // 2), f32),
            pltpu.VMEM((4, 4, 2, 2, 2, 2, 2 * ref_rows, quarter), bf16),
            pltpu.VMEM((4, share, width), f32),
            pltpu.VMEM((4, share, width // 2), i16),
            pltpu.VMEM((6, share, width // 2), i16),
            pltpu.VMEM((6, 8, lanes), f32),
            pltpu.VMEM((6, 8, lanes), f32),
            pltpu.VMEM((lanes, 128), f32),
            pltpu.VMEM((4, share, width), bf16),
            pltpu.VMEM((lanes, ref_weight.shape[1]), f32),
            pltpu.VMEM((4, lanes, 128), f32),
            pltpu.VMEM((4, lanes, 128), f32),
            pltpu.VMEM((4, 8, lanes), f32),
            pltpu.VMEM((3, 8, lanes), f32),
            pltpu.VMEM((3, 2, 8, lanes), f32),
            pltpu.VMEM((7, 2, 8, lanes), f32),
            pltpu.VMEM((4, 8, lanes), f32),
            pltpu.VMEM((8, lanes), f32),
            pltpu.VMEM((2, share, width), bf16),
            pltpu.VMEM((lanes, width), bf16),
            pltpu.VMEM((2, LEN, depth), f32),
            pltpu.VMEM((2, LEN, depth), f32),
            pltpu.VMEM((4, LEN, depth), i16),
            pltpu.VMEM((4, LEN, depth), i16),
            pltpu.VMEM((4, LEN, depth), i16),
            pltpu.VMEM((12, count, depth), i16),
            pltpu.VMEM((LEN, depth), i16),
            pltpu.VMEM((3, count, depth), i16),
            pltpu.VMEM((LEN, depth), f32),
            pltpu.VMEM((9, 8, lanes), f32),
            pltpu.VMEM((19, 8, lanes), f32),
            pltpu.SemaphoreType.DMA((copies,)),
            pltpu.SemaphoreType.DMA((copies,)),
            pltpu.SemaphoreType.DMA((4,)),
        ],
        compiler_params=pltpu.CompilerParams(
            collective_id=index, has_side_effects=True, vmem_limit_bytes=VMEM_LIMIT
        ),
    )(states, others, weight, ref_weight, masks, wanted, pairs)


def weight_kernel(states, grad, out, turned):
    @pl.when(pl.program_id(0) == 0)
    def _():
        turned[...] = jnp.transpose(states[...])

    out[...] = jnp.dot(turned[...], grad[...], preferred_element_type=jnp.float32)


def weight_gradient(states, grad):
    tokens, depth = states.shape
    width = grad.shape[1]
    tile = 256
    return pl.pallas_call(
        weight_kernel,
        name="weight_gradient",
        grid=(width // tile,),
        out_shape=jax.ShapeDtypeStruct((depth, width), jnp.float32),
        in_specs=[
            pl.BlockSpec((tokens, depth), lambda j: (0, 0)),
            pl.BlockSpec((tokens, tile), lambda j: (0, j)),
        ],
        out_specs=pl.BlockSpec((depth, tile), lambda j: (0, j)),
        scratch_shapes=[pltpu.VMEM((depth, tokens), states.dtype)],
        compiler_params=pltpu.CompilerParams(vmem_limit_bytes=VMEM_LIMIT),
    )(states, grad)


def on_device(
    policy_states,
    reference_states,
    policy_weight,
    reference_weight,
    targets,
    response_mask,
    pair_index,
    chosen_flag,
):
    masks = response_mask.reshape(4, 1, 2 * LEN)
    wanted = targets.reshape(4, 1, 2 * LEN)
    sign = (2 * chosen_flag - 1).astype(jnp.float32)
    same = (pair_index[:, None] == pair_index[None, :]).astype(jnp.float32)
    pairs = jnp.concatenate(
        [same * sign[None, :], sign[:, None], jnp.zeros((SEQS, 128 - SEQS - 1), jnp.float32)], axis=1
    )

    def run(index):
        def branch(*operands):
            loss, grad_states, grad, states = fused(index, SIZES[index], *operands)
            grad_weight = weight_gradient(
                states.reshape(-1, states.shape[2]), grad.reshape(-1, grad.shape[2])
            )
            return (loss[0, 0], grad_states, grad_weight)

        return branch

    longest = jnp.max(jnp.sum(response_mask.reshape(4, 2 * LEN), axis=1))
    size = sum((longest > s).astype(jnp.int32) for s in SIZES[:-1])
    return lax.switch(
        size,
        [run(i) for i in range(len(SIZES))],
        policy_states,
        reference_states,
        policy_weight,
        reference_weight,
        masks,
        wanted,
        pairs,
    )


def solution(mesh):
    in_specs = (
        P(("col", "depth"), "row"),
        P(("row", "col", "depth"), None),
        P("row", ("col", "depth")),
        P(None, ("row", "col", "depth")),
        P(),
        P(),
        P(),
        P(),
    )
    out_specs = (P(), P(("col", "depth"), "row"), P("row", ("col", "depth")))
    return jax.shard_map(
        on_device, mesh=mesh, in_specs=in_specs, out_specs=out_specs, check_vma=False
    )
```

```python
import functools

import jax
import jax.numpy as jnp
from jax import lax
from jax.experimental import pallas as pl
from jax.experimental.pallas import tpu as pltpu
from jax.sharding import PartitionSpec as P

PAIRS = 4
LEN = 128
SEQS = 8
SKIP = 16
KEEP = LEN - SKIP
SIZES = (176, 2 * KEEP)

beta_value = 0.1
loss_scale = 256.0

MESH = pl.DeviceIdType.MESH
VMEM_LIMIT = 62 * 1024 * 1024
ROWS = 16


def preference(ratio, pair_index, chosen_flag):
    sign = (2 * chosen_flag - 1).astype(jnp.float32)
    member = pair_index[:, None] == jnp.arange(PAIRS, dtype=jnp.int32)[None, :]
    margin = jnp.sum(jnp.where(member, (sign * ratio)[:, None], 0.0), axis=0)
    loss = -jnp.mean(jax.nn.log_sigmoid(beta_value * margin))
    slope = -loss_scale * beta_value / PAIRS * jax.nn.sigmoid(-beta_value * margin)
    weights = sign * jnp.sum(jnp.where(member, slope[None, :], 0.0), axis=1)
    return (loss, weights)


class Place:
    def __init__(self):
        self.x = lax.axis_index("row")
        col = lax.axis_index("col")
        self.z = col // 2
        self.c = col % 2
        self.y = lax.axis_index("depth")

    def on_x(self, step):
        return ((self.x + step) % 4, self.z * 2 + self.c, self.y)

    def on_y(self, step):
        return (self.x, self.z * 2 + self.c, (self.y + step) % 4)

    def on_z(self, step):
        return (self.x, ((self.z + step) % 4) * 2 + self.c, self.y)

    def partner_y(self):
        return (self.x, self.z * 2 + self.c, self.y + 1 - 2 * (self.y % 2))

    def other_core(self):
        return (self.x, self.z * 2 + 1 - self.c, self.y)


def greet(peers):
    barrier = pltpu.get_barrier_semaphore()
    for peer in peers:
        pl.semaphore_signal(barrier, inc=1, device_id=peer, device_id_type=MESH)
    pl.semaphore_wait(barrier, len(peers))


class Mover:
    def __init__(self, send, recv):
        self.send, self.recv, self.used, self.all = send, recv, 0, []

    def make(self, k, src, dst, peer):
        return pltpu.make_async_remote_copy(
            src_ref=src,
            dst_ref=dst,
            send_sem=self.send.at[k],
            recv_sem=self.recv.at[k],
            device_id=peer,
            device_id_type=MESH,
        )

    def start(self, src, dst, peer):
        copy = self.make(self.used, src, dst, peer)
        self.used += 1
        copy.start()
        self.all.append(copy)
        return copy

    def sent(self, copy):
        copy.wait_send()
        self.all = [other for other in self.all if other is not copy]

    def finish(self):
        for copy in self.all:
            copy.wait_send()


class Ring:
    def __init__(self, mover, me, view, peer):
        self.mover, self.me, self.view, self.peer = mover, me, view, peer

    def begin(self):
        own = self.view(self.me, None)
        self.right = self.mover.start(own, own, self.peer(1))
        self.left = self.mover.start(own, own, self.peer(3))

    def forward(self):
        self.right.wait_recv()
        part = self.view((self.me + 3) % 4, 0)
        self.far_right = self.mover.start(part, part, self.peer(1))
        self.left.wait_recv()
        part = self.view((self.me + 1) % 4, 1)
        self.far_left = self.mover.start(part, part, self.peer(3))

    def end(self):
        self.far_right.wait_recv()
        self.far_left.wait_recv()


def merge(a, b):
    peak = jnp.maximum(a[..., 0:1, :], b[..., 0:1, :])
    total = a[..., 1:2, :] * jnp.exp(a[..., 0:1, :] - peak) + b[..., 1:2, :] * jnp.exp(
        b[..., 0:1, :] - peak
    )
    return jnp.concatenate([peak, total, a[..., 2:3, :] + b[..., 2:3, :], a[..., 3:, :]], axis=-2)


def over(count, read, write, unroll):
    def group(steps):
        rows = [pl.ds(pl.multiple_of(step * ROWS, ROWS), ROWS) for step in steps]
        for r, value in zip(rows, [read(r) for r in rows]):
            write(r, value)

    steps = count // ROWS
    whole = steps // unroll

    @pl.loop(0, whole)
    def _(g):
        group([g * unroll + u for u in range(unroll)])

    if steps % unroll:
        group(list(range(whole * unroll, steps)))


def wide(value, width):
    return jnp.concatenate([value] * (width // 128), axis=1)


def fold(op, value):
    parts = [value[:, k : k + 128] for k in range(0, value.shape[1], 128)]
    while len(parts) > 1:
        paired = [op(a, b) for a, b in zip(parts[::2], parts[1::2])]
        parts = paired + parts[len(paired) * 2 :]
    return parts[0]


def to_column(row):
    return jnp.transpose(jnp.broadcast_to(row, (128, row.shape[1])))


def span(half, count):
    return slice(None) if half is None else pl.ds(half * (count // 2), count // 2)


def fused_kernel(
    own,
    ref_own,
    weight_in,
    ref_weight_in,
    masks,
    wanted,
    pairs,
    loss,
    rows_out,
    grad_out,
    kept,
    weight,
    ref_weight,
    gathered,
    ref_half,
    ref_got,
    refs,
    partial,
    qsend,
    qrecv,
    ssend,
    srecv,
    column,
    inverse,
    third,
    kept_wanted,
    choose,
    place,
    kept_mask,
    spread,
    ref_logits,
    ref_column,
    ref_wanted,
    ref_stats,
    ref_first,
    held,
    got,
    info,
    token_weights,
    grad,
    grad_full,
    rows_all,
    core_send,
    core_recv,
    y_send,
    y_recv,
    z_send,
    z_recv,
    z_sum,
    row_ssend,
    row_srecv,
    send,
    recv,
    local,
):
    at = Place()
    x, z, c, y = at.x, at.z, at.c, at.y
    share, width = spread.shape[1], spread.shape[2]
    depth = own.shape[1]
    half = width // 2
    f32, bf16 = jnp.float32, jnp.bfloat16
    fetch = [
        pltpu.make_async_copy(weight_in, weight, local.at[4]),
        pltpu.make_async_copy(ref_weight_in, ref_weight, local.at[5]),
    ]
    for copy in fetch:
        copy.start()
    ways = [at.on_x, at.on_y, at.on_z]
    greet([way(i) for way in ways for i in (1, 2, 3)] + [at.other_core()])
    move = Mover(send, recv)

    gathered[z, c, y] = own[...]
    low, high = pl.ds(0, depth // 2), pl.ds(depth // 2, depth // 2)
    count = own.shape[0]
    first_y = Ring(move, y, lambda i, h: gathered.at[z, c, i, span(h, count), low], at.on_y)
    first_z = Ring(move, z, lambda i, h: gathered.at[i, c, y, span(h, count), high], at.on_z)
    then_z = Ring(move, z, lambda i, h: gathered.at[i, c, span(h, 4), :, low], at.on_z)
    then_y = Ring(move, y, lambda i, h: gathered.at[span(h, 4), c, i, :, high], at.on_y)
    first_y.begin()
    first_z.begin()

    side, pair = y % 2, y // 2
    ref_depth = ref_own.shape[1]
    quarter = ref_depth // 4
    for k in (0, 1):
        ref_half[k] = ref_own[:, k * 2 * quarter : (k + 1) * 2 * quarter].astype(f32)
    swap = move.start(ref_half.at[1 - side], ref_got, at.partner_y())
    column[...] = jnp.zeros_like(column)
    first_y.forward()
    first_z.forward()
    swap.wait_recv()
    mine, theirs = ref_half[side], ref_got[...]
    block = jnp.concatenate(
        [jnp.where(side == 0, mine, theirs), jnp.where(side == 0, theirs, mine)], axis=0
    ).astype(bf16)
    for f in (0, 1):
        refs[x, z, c, f, pair, side] = block[:, f * quarter : (f + 1) * quarter]
    ref_x = Ring(
        move,
        x,
        lambda i, h: refs.at[i, z, c, slice(None) if h is None else h, pair, side],
        at.on_x,
    )
    ref_y = Ring(move, y, lambda i, h: refs.at[span(h, 4), z, c, 0, i // 2, i % 2], at.on_y)
    ref_z = Ring(move, z, lambda i, h: refs.at[span(h, 4), i, c, 1, pair, side], at.on_z)
    ref_yz = Ring(move, z, lambda i, h: refs.at[span(h, 4), i, c, 0], at.on_z)
    ref_zy = Ring(move, y, lambda i, h: refs.at[span(h, 4), :, c, 1, i // 2, i % 2], at.on_y)
    ref_core = []

    def to_core(ring, i):
        part = ring.view((ring.me + i) % 4, None)
        ref_core.append(move.start(part, part, at.other_core()))

    own_core = []

    def share_core(ring, steps):
        for i in steps:
            part = ring.view((ring.me + i) % 4, None)
            own_core.append(move.start(part, part, at.other_core()))

    first_y.end()
    then_z.begin()
    share_core(then_z, (0,))
    first_z.end()
    then_y.begin()
    share_core(then_y, (0,))
    ref_x.begin()

    def runs(owner):
        lane = lax.broadcasted_iota(jnp.int32, (1, 2 * LEN), 1)
        mask = masks[owner]
        a = jnp.where(lane < LEN, mask, 0)
        b = jnp.where(lane < LEN, 0, mask)
        return (
            jnp.sum(a, axis=1, keepdims=True),
            jnp.sum(b, axis=1, keepdims=True),
            jnp.min(jnp.where(a > 0, lane, 2 * LEN), axis=1, keepdims=True),
            jnp.min(jnp.where(b > 0, lane, 2 * LEN), axis=1, keepdims=True),
        )

    def source(owner, i):
        len_a, len_b, start_a, start_b = runs(owner)
        second = jnp.where(i < len_a + len_b, start_b + i - len_a, -1)
        return jnp.where(i < len_a, start_a + i, second)

    def kept_masks(owner):
        len_a, len_b, _, _ = runs(owner)
        i = lax.broadcasted_iota(jnp.int32, (1, 2 * LEN), 1)
        a = (i < len_a).astype(f32)
        return a, (i < len_a + len_b).astype(f32) - a

    for k in range(4):
        ref_wanted[k] = to_column(wanted[k].astype(f32))

    @pl.loop(0, 4)
    def _(o):
        to = source(o, lax.broadcasted_iota(jnp.int32, (share, 1), 0))
        here = lax.broadcasted_iota(jnp.int32, (share, 2 * LEN), 1) == to
        choose[o] = here.astype(bf16)
        target = jnp.sum(jnp.where(here, wanted[o].astype(f32), 0.0), axis=1, keepdims=True)
        kept_wanted[o] = jnp.broadcast_to(target, (share, 128))
        to = source(o, lax.broadcasted_iota(jnp.int32, (1, share), 1))
        place[o] = (lax.broadcasted_iota(jnp.int32, (2 * LEN, share), 0) == to).astype(bf16)
        mask_a, mask_b = kept_masks(o)
        kept_mask[o, 0:1, :] = mask_a
        kept_mask[o, 1:2, :] = mask_b

    then_z.forward()
    share_core(then_z, (1, 3))
    then_y.forward()
    share_core(then_y, (1, 3))
    ref_x.forward()
    then_z.end()
    share_core(then_z, (2,))
    then_y.end()
    share_core(then_y, (2,))
    ref_x.end()
    ref_y.begin()
    ref_z.begin()
    fetch[0].wait()
    for copy in own_core:
        copy.wait_recv()

    tile = 256

    def product(owner):
        whole = gathered[owner].reshape(2 * LEN, depth)
        kept[owner] = jnp.dot(choose[owner], whole, preferred_element_type=f32).astype(bf16)

        @pl.loop(0, width // tile)
        def _(j):
            cols = pl.ds(pl.multiple_of(j * tile, tile), tile)
            partial[owner, :, cols] = jnp.dot(
                kept[owner], weight[:, cols], preferred_element_type=f32
            )

    def encode(count, read, write, store=None):
        def top(rows, value):
            if store is not None:
                store(rows, value)
            column[rows, :] = fold(jnp.maximum, jnp.abs(value))

        over(count, read, top, 2)
        peak = jnp.max(column[0:count, :], axis=1, keepdims=True)
        step = jnp.broadcast_to(jnp.maximum(peak, 1e-30) * (1.0 / 32767.0), (count, 128))
        column[0:count, :] = step
        inverse[0:count, :] = 1.0 / step

        def code(rows):
            value = read(rows) if store is None else store(rows)
            value = value * wide(inverse[rows, :], value.shape[1])
            return jnp.round(value).astype(jnp.int32).astype(jnp.int16)

        over(count, code, write, 2)
        return jnp.transpose(column[...])[0:8]

    def decode(code, step):
        return code.astype(jnp.int32).astype(f32) * wide(step, code.shape[1])

    def pack(k, owner, part, peer, add=None):
        cols = pl.ds(part * half, half)
        slot = k % 3 % 2 + k // 3 * 2

        def plain(rows):
            return partial[owner, rows, cols]

        def summed(rows):
            return plain(rows) + decode(qrecv[add, rows, :], third[rows, :])

        def store(rows, value=None):
            if value is None:
                return plain(rows)
            partial[owner, rows, cols] = value

        def write(rows, code):
            qsend[slot, rows, :] = code

        if add is None:
            ssend[k] = encode(share, plain, write)
        else:
            third[...] = to_column(srecv[add, 0:1, :])
            ssend[k] = encode(share, summed, write, store)
        return (
            move.start(ssend.at[k], srecv.at[k], peer),
            move.start(qsend.at[slot], qrecv.at[k], peer),
        )

    def arrived(copies):
        for copy in copies:
            copy.wait_recv()

    def add_in(k, part):
        cols = pl.ds(part * half, half)
        column[...] = to_column(srecv[k, 0:1, :])

        def read(rows):
            return partial[x, rows, cols] + decode(qrecv[k, rows, :], column[rows, :])

        def write(rows, value):
            partial[x, rows, cols] = value

        over(share, read, write, 2)

    right, left = at.on_x(1), at.on_x(3)
    after, before, across = (x + 1) % 4, (x + 3) % 4, (x + 2) % 4
    product(across)
    r0 = pack(0, across, 0, right)
    l0 = pack(3, across, 1, left)
    ref_y.forward()
    ref_z.forward()
    product(after)
    r1 = pack(1, after, 1, right)
    product(before)
    l1 = pack(4, before, 0, left)
    ref_y.end()
    ref_yz.begin()
    to_core(ref_yz, 0)
    ref_z.end()
    ref_zy.begin()
    to_core(ref_zy, 0)
    product(x)
    arrived(r0)
    move.sent(r0[1])
    r2 = pack(2, after, 0, right, add=0)
    arrived(l0)
    move.sent(l0[1])
    l2 = pack(5, before, 1, left, add=3)
    ref_yz.forward()
    to_core(ref_yz, 1)
    to_core(ref_yz, 3)
    ref_zy.forward()
    to_core(ref_zy, 1)
    to_core(ref_zy, 3)
    arrived(r1)
    add_in(1, 1)
    arrived(l1)
    add_in(4, 0)
    ref_yz.end()
    to_core(ref_yz, 2)
    ref_zy.end()
    to_core(ref_zy, 2)
    arrived(r2)
    arrived(l2)
    column[...] = to_column(srecv[2, 0:1, :])
    third[...] = to_column(srecv[5, 0:1, :])
    first = (lax.axis_index("col") * 4 + y) * width

    def entries(rows_count):
        lane = lax.broadcasted_iota(jnp.int32, (rows_count, width), 1)
        return (lane + first).astype(f32)

    def read(rows):
        codes = (decode(qrecv[2, rows, :], column[rows, :]), decode(qrecv[5, rows, :], third[rows, :]))
        return partial[x, rows, :] + jnp.concatenate(codes, axis=1)

    def write(rows, value):
        partial[x, rows, :] = value
        hits = entries(ROWS) == wide(kept_wanted[x, rows, :], width)
        column[rows, :] = fold(jnp.maximum, value)
        third[rows, :] = fold(jnp.add, jnp.where(hits, value, 0.0))

    over(share, read, write, 1)
    peak = jnp.broadcast_to(jnp.max(column[0:share, :], axis=1, keepdims=True), (share, 128))
    column[0:share, :] = peak

    def read(rows):
        return jnp.exp(partial[x, rows, :] - wide(column[rows, :], width))

    def write(rows, value):
        spread[x, rows, :] = value.astype(bf16)
        inverse[rows, :] = fold(jnp.add, value)

    over(share, read, write, 1)
    ring = Ring(
        move,
        x,
        lambda i, h: spread.at[i] if h is None else spread.at[i, :, pl.ds(h * half, half)],
        at.on_x,
    )
    ring.begin()
    total = jnp.sum(inverse[0:share, :], axis=1, keepdims=True)
    picked = jnp.sum(third[0:share, :], axis=1, keepdims=True)
    lane = lax.broadcasted_iota(jnp.int32, (share, 128), 1)
    column[0:share, :] = jnp.where(
        lane == 0, column[0:share, :], jnp.where(lane == 1, total, picked)
    )
    stats = jnp.transpose(column[...])[0:8]
    local_peak = stats[0:1]

    arrived(ref_core)
    fetch[1].wait()
    ref_width = ref_weight.shape[1]
    ref_entry = lax.axis_index("row") * 32 + lax.axis_index("col") * 4 + y

    @pl.loop(0, 4)
    def _(k):
        for f in (0, 1):
            for h in (0, 1):
                a = refs[:, k, :, f, :, h].reshape(2 * LEN, quarter)
                b = ref_weight[(h * 2 + f) * quarter : (h * 2 + f + 1) * quarter, :]
                d = jnp.dot(a, b, preferred_element_type=f32)
                if f + h == 0:
                    ref_logits[...] = d
                else:
                    ref_logits[...] += d
        for i in range(4):
            rows = pl.ds(i * 64, 64)
            there = pl.ds(pl.multiple_of(k * 64, 64), 64)
            logits = ref_logits[rows, :]
            peak = jnp.max(logits, axis=1, keepdims=True)
            total = jnp.sum(jnp.exp(logits - peak), axis=1, keepdims=True)
            entry = (
                lax.broadcasted_iota(jnp.int32, (64, ref_width), 1) + ref_entry * ref_width
            ).astype(f32)
            picked = jnp.sum(
                jnp.where(entry == ref_wanted[i, there, 0:1], logits, 0.0), axis=1, keepdims=True
            )
            lanes = lax.broadcasted_iota(jnp.int32, (64, 128), 1)
            ref_column[i, there, :] = jnp.where(
                lanes == 0, peak, jnp.where(lanes == 1, total, picked)
            )

    for i in range(4):
        ref_stats[i] = jnp.transpose(ref_column[i])[0:8]
    copies = [
        move.start(ref_stats.at[(x + i) % 4], ref_first.at[i - 1], at.on_x(i)) for i in (1, 2, 3)
    ]
    ring.forward()
    arrived(copies)
    mine = ref_stats[x]
    for i in (0, 1, 2):
        mine = merge(mine, ref_first[i])
    both = jnp.stack([stats, mine])
    stages = [[at.other_core()], [at.on_y(i) for i in (1, 2, 3)], [at.on_z(i) for i in (1, 2, 3)]]
    slot = 0
    for s, peers in enumerate(stages):
        held[s] = both
        copies = [move.start(held.at[s], got.at[slot + k], peer) for k, peer in enumerate(peers)]
        arrived(copies)
        for k in range(len(peers)):
            both = merge(both, got[slot + k])
        slot += len(peers)

    def valid(mask, value):
        return jnp.sum(jnp.where(mask > 0, value, 0.0), axis=1, keepdims=True)

    normalizer = both[0, 0:1] + jnp.log(both[0, 1:2])
    logp = both[0, 2:3] - normalizer
    ref_logp = both[1, 2:3] - both[1, 0:1] - jnp.log(both[1, 1:2])
    mask_a, mask_b = kept_mask[x, 0:1, :], kept_mask[x, 1:2, :]
    natural = lax.broadcasted_iota(jnp.int32, (1, 2 * LEN), 1)
    mask = masks[x]
    ratio_a = valid(mask_a, logp) - valid(jnp.where(natural < LEN, mask, 0), ref_logp)
    ratio_b = valid(mask_b, logp) - valid(jnp.where(natural < LEN, 0, mask), ref_logp)
    info[x] = jnp.concatenate(
        [
            normalizer,
            local_peak,
            jnp.broadcast_to(ratio_a, (1, 2 * LEN)),
            jnp.broadcast_to(ratio_b, (1, 2 * LEN)),
            jnp.zeros((4, 2 * LEN), f32),
        ],
        axis=0,
    )
    arrived([move.start(info.at[x], info.at[x], at.on_x(i)) for i in (1, 2, 3)])
    margin = jnp.zeros((SEQS, 2 * LEN), f32)
    for s in range(SEQS):
        margin += pairs[:, s : s + 1] * info[s // 2, 2 + s % 2 : 3 + s % 2, :]
    margin *= beta_value
    log_sigmoid = jnp.minimum(margin, 0.0) - jnp.log1p(jnp.exp(-jnp.abs(margin)))
    loss[...] = jnp.broadcast_to(
        jnp.sum(log_sigmoid, axis=0, keepdims=True)[:, 0:128] * (-1.0 / SEQS), (8, 128)
    )
    weights = (
        (-loss_scale * beta_value / PAIRS)
        * jax.nn.sigmoid(-margin)
        * pairs[:, SEQS : SEQS + 1]
    )
    token_weights[...] = weights

    core_at, y_at = move.used, move.used + 8
    move.used += 32

    def core_copies(t):
        return [
            move.make(core_at + 2 * t, row_ssend.at[t], row_srecv.at[t], at.other_core()),
            move.make(core_at + 2 * t + 1, core_send.at[t % 2], core_recv.at[t], at.other_core()),
        ]

    def y_copies(t):
        copies = []
        for i in (1, 3, 2):
            k = t * 3 + i - 1
            there = (y + i) % 4
            part = y_send.at[t % 2, pl.ds(pl.multiple_of(there * count, count), count), :]
            copies.append(
                move.make(y_at + 2 * k, row_ssend.at[4 + t], row_srecv.at[4 + k], at.on_y(i))
            )
            copies.append(move.make(y_at + 2 * k + 1, part, y_recv.at[k], at.on_y(i)))
        return copies

    def out_copy(t, owner):
        return pltpu.make_async_copy(grad.at[t % 2], grad_out.at[owner], local.at[t])

    def sent(copies):
        for copy in copies:
            copy.wait_send()

    def owner_of(t):
        return (x + t + t // 2 - 2 * (t // 3)) % 4

    mine_rows = pl.ds(pl.multiple_of(y * count, count), count)

    def rows_of(owner):
        return pl.ds(pl.multiple_of(owner * count, count), count)

    @pl.loop(0, 6)
    def _(t):
        @pl.when(t == 3)
        def _():
            ring.end()

        @pl.when((t >= 2) & (t < 4))
        def _():
            sent(core_copies(t - 2))
            out_copy(t - 2, owner_of(t - 2)).wait()

        @pl.when(t < 4)
        def _():
            slot = t % 2
            owner = owner_of(t)
            mask_a, mask_b = kept_mask[owner, 0:1, :], kept_mask[owner, 1:2, :]
            weight_a = token_weights[pl.ds(2 * owner, 1), :]
            weight_b = token_weights[pl.ds(2 * owner + 1, 1), :]
            token = mask_a * weight_a + mask_b * weight_b
            factor = jnp.where(
                mask_a + mask_b > 0, token * jnp.exp(info[owner, 1:2, :] - info[owner, 0:1, :]), 0.0
            )
            column[...] = to_column(token)
            third[...] = to_column(factor)

            def read(rows):
                hits = entries(ROWS) == wide(kept_wanted[owner, rows, :], width)
                return (
                    jnp.where(hits, wide(column[rows, :], width), 0.0)
                    - wide(third[rows, :], width) * spread[owner, rows, :].astype(f32)
                ).astype(bf16)

            def write(rows, value):
                grad[slot, rows, :] = value

            over(share, read, write, 1)
            out_copy(t, owner).start()

            @pl.loop(0, width // tile)
            def _(j):
                cols = pl.ds(pl.multiple_of(j * tile, tile), tile)
                grad_full[:, cols] = jnp.dot(
                    place[owner], grad[slot, :, cols], preferred_element_type=f32
                ).astype(bf16)

            @pl.loop(0, depth // 256)
            def _(j):
                cols = pl.ds(pl.multiple_of(j * 256, 256), 256)
                rows_all[slot, :, :, cols] = lax.dot_general(
                    grad_full[...],
                    weight[cols, :],
                    (((1,), (1,)), ((), ())),
                    preferred_element_type=f32,
                ).reshape(2, LEN, 256)

            def write(rows, code):
                core_send[slot, rows, :] = code

            row_ssend[t] = encode(LEN, lambda rows: rows_all[slot, 1 - c, rows, :], write)
            for copy in core_copies(t):
                copy.start()

        @pl.when((t >= 3) & (t < 5))
        def _():
            sent(y_copies(t - 3))

        @pl.when((t >= 1) & (t < 5))
        def _():
            u = t - 1
            slot = u % 2
            for copy in core_copies(u):
                copy.wait_recv()
            third[...] = to_column(row_srecv[u, 0:1, :])

            def read(rows):
                return rows_all[slot, c, rows, :] + decode(core_recv[u, rows, :], third[rows, :])

            def store(rows, value=None):
                if value is None:
                    return rows_all[slot, c, rows, :]
                rows_all[slot, c, rows, :] = value

            def write(rows, code):
                y_send[slot, rows, :] = code

            row_ssend[4 + u] = encode(LEN, read, write, store)
            for copy in y_copies(u):
                copy.start()
            z_sum[rows_of(owner_of(u)), :] = rows_all[slot, c, mine_rows, :]

        @pl.when(t >= 2)
        def _():
            v = t - 2
            for copy in y_copies(v):
                copy.wait_recv()
            total = z_sum[rows_of(owner_of(v)), :]
            for i in range(3):
                k = v * 3 + i
                column[...] = to_column(row_srecv[4 + k, 0:1, :])
                total += decode(y_recv[k], column[mine_rows, :])
            z_sum[rows_of(owner_of(v)), :] = total

    for t in (2, 3):
        sent(core_copies(t))
        sent(y_copies(t))
        out_copy(t, owner_of(t)).wait()

    def write(rows, code):
        z_send[rows, :] = code

    row_ssend[8] = encode(LEN, lambda rows: z_sum[rows, :], write)
    copies = []
    for i in (1, 3, 2):
        there = (z + i) % 4
        copies.append(move.start(row_ssend.at[8], row_srecv.at[16 + i - 1], at.on_z(i)))
        part = z_send.at[pl.ds(pl.multiple_of(there * count, count), count), :]
        copies.append(move.start(part, z_recv.at[i - 1], at.on_z(i)))
    arrived(copies)
    here = pl.ds(pl.multiple_of(z * count, count), count)
    total = z_sum[here, :]
    for i in range(3):
        column[...] = to_column(row_srecv[16 + i, 0:1, :])
        total += decode(z_recv[i], column[here, :])
    rows_out[...] = total
    move.finish()


def fused(index, share, states, others, weight, ref_weight, masks, wanted, pairs):
    vmem = pl.BlockSpec(memory_space=pltpu.VMEM)
    count, depth = states.shape
    width = weight.shape[1]
    ref_rows, ref_depth = others.shape
    quarter = ref_depth // 4
    f32, bf16, i16 = jnp.float32, jnp.bfloat16, jnp.int16
    lanes = 2 * LEN
    copies = 128
    return pl.pallas_call(
        fused_kernel,
        name="fused_%d" % share,
        out_shape=(
            jax.ShapeDtypeStruct((8, 128), f32),
            jax.ShapeDtypeStruct((count, depth), f32),
            jax.ShapeDtypeStruct((4, share, width), bf16),
            jax.ShapeDtypeStruct((4, share, depth), bf16),
        ),
        in_specs=[vmem, vmem, pl.BlockSpec(memory_space=pl.ANY), pl.BlockSpec(memory_space=pl.ANY)]
        + [vmem] * 3,
        out_specs=(vmem, vmem, pl.BlockSpec(memory_space=pl.ANY), vmem),
        scratch_shapes=[
            pltpu.VMEM(weight.shape, bf16),
            pltpu.VMEM(ref_weight.shape, bf16),
            pltpu.VMEM((4, 2, 4, count, depth), bf16),
            pltpu.VMEM((2, ref_rows, ref_depth // 2), f32),
            pltpu.VMEM((ref_rows, ref_depth // 2), f32),
            pltpu.VMEM((4, 4, 2, 2, 2, 2, 2 * ref_rows, quarter), bf16),
            pltpu.VMEM((4, share, width), f32),
            pltpu.VMEM((4, share, width // 2), i16),
            pltpu.VMEM((6, share, width // 2), i16),
            pltpu.VMEM((6, 8, lanes), f32),
            pltpu.VMEM((6, 8, lanes), f32),
            pltpu.VMEM((lanes, 128), f32),
            pltpu.VMEM((lanes, 128), f32),
            pltpu.VMEM((lanes, 128), f32),
            pltpu.VMEM((4, share, 128), f32),
            pltpu.VMEM((4, share, lanes), bf16),
            pltpu.VMEM((4, lanes, share), bf16),
            pltpu.VMEM((4, 8, lanes), f32),
            pltpu.VMEM((4, share, width), bf16),
            pltpu.VMEM((lanes, ref_weight.shape[1]), f32),
            pltpu.VMEM((4, lanes, 128), f32),
            pltpu.VMEM((4, lanes, 128), f32),
            pltpu.VMEM((4, 8, lanes), f32),
            pltpu.VMEM((3, 8, lanes), f32),
            pltpu.VMEM((3, 2, 8, lanes), f32),
            pltpu.VMEM((7, 2, 8, lanes), f32),
            pltpu.VMEM((4, 8, lanes), f32),
            pltpu.VMEM((8, lanes), f32),
            pltpu.VMEM((2, share, width), bf16),
            pltpu.VMEM((lanes, width), bf16),
            pltpu.VMEM((2, 2, LEN, depth), f32),
            pltpu.VMEM((2, LEN, depth), i16),
            pltpu.VMEM((4, LEN, depth), i16),
            pltpu.VMEM((2, LEN, depth), i16),
            pltpu.VMEM((12, count, depth), i16),
            pltpu.VMEM((LEN, depth), i16),
            pltpu.VMEM((3, count, depth), i16),
            pltpu.VMEM((LEN, depth), f32),
            pltpu.VMEM((9, 8, lanes), f32),
            pltpu.VMEM((19, 8, lanes), f32),
            pltpu.SemaphoreType.DMA((copies,)),
            pltpu.SemaphoreType.DMA((copies,)),
            pltpu.SemaphoreType.DMA((6,)),
        ],
        compiler_params=pltpu.CompilerParams(
            collective_id=index, has_side_effects=True, vmem_limit_bytes=VMEM_LIMIT
        ),
    )(states, others, weight, ref_weight, masks, wanted, pairs)


def weight_kernel(states, grad, out, turned):
    @pl.when(pl.program_id(0) == 0)
    def _():
        turned[...] = jnp.transpose(states[...])

    out[...] = jnp.dot(turned[...], grad[...], preferred_element_type=jnp.float32)


def weight_gradient(states, grad):
    tokens, depth = states.shape
    width = grad.shape[1]
    tile = 512
    return pl.pallas_call(
        weight_kernel,
        name="weight_gradient",
        grid=(width // tile,),
        out_shape=jax.ShapeDtypeStruct((depth, width), jnp.float32),
        in_specs=[
            pl.BlockSpec((tokens, depth), lambda j: (0, 0)),
            pl.BlockSpec((tokens, tile), lambda j: (0, j)),
        ],
        out_specs=pl.BlockSpec((depth, tile), lambda j: (0, j)),
        scratch_shapes=[pltpu.VMEM((depth, tokens), states.dtype)],
        compiler_params=pltpu.CompilerParams(vmem_limit_bytes=VMEM_LIMIT),
    )(states, grad)


def on_device(
    policy_states,
    reference_states,
    policy_weight,
    reference_weight,
    targets,
    response_mask,
    pair_index,
    chosen_flag,
):
    masks = response_mask.reshape(4, 1, 2 * LEN)
    wanted = targets.reshape(4, 1, 2 * LEN)
    sign = (2 * chosen_flag - 1).astype(jnp.float32)
    same = (pair_index[:, None] == pair_index[None, :]).astype(jnp.float32)
    pairs = jnp.concatenate(
        [same * sign[None, :], sign[:, None], jnp.zeros((SEQS, 128 - SEQS - 1), jnp.float32)], axis=1
    )

    def run(index):
        def branch(*operands):
            loss, grad_states, grad, states = fused(index, SIZES[index], *operands)
            grad_weight = weight_gradient(
                states.reshape(-1, states.shape[2]), grad.reshape(-1, grad.shape[2])
            )
            return (loss[0, 0], grad_states, grad_weight)

        return branch

    longest = jnp.max(jnp.sum(response_mask.reshape(4, 2 * LEN), axis=1))
    size = sum((longest > s).astype(jnp.int32) for s in SIZES[:-1])
    return lax.switch(
        size,
        [run(i) for i in range(len(SIZES))],
        policy_states,
        reference_states,
        policy_weight,
        reference_weight,
        masks,
        wanted,
        pairs,
    )


def solution(mesh):
    in_specs = (
        P(("col", "depth"), "row"),
        P(("row", "col", "depth"), None),
        P("row", ("col", "depth")),
        P(None, ("row", "col", "depth")),
        P(),
        P(),
        P(),
        P(),
    )
    out_specs = (P(), P(("col", "depth"), "row"), P("row", ("col", "depth")))
    return jax.shard_map(
        on_device, mesh=mesh, in_specs=in_specs, out_specs=out_specs, check_vma=False
    )
```

```python
import functools

import jax
import jax.numpy as jnp
from jax import lax
from jax.experimental import pallas as pl
from jax.experimental.pallas import tpu as pltpu
from jax.sharding import PartitionSpec as P

PAIRS = 4
LEN = 128
SEQS = 8
SKIP = 16
KEEP = LEN - SKIP
SIZES = (176, 2 * KEEP)

beta_value = 0.1
loss_scale = 256.0

MESH = pl.DeviceIdType.MESH
VMEM_LIMIT = 62 * 1024 * 1024
ROWS = 16


class Place:
    def __init__(self):
        self.x = lax.axis_index("row")
        col = lax.axis_index("col")
        self.z = col // 2
        self.c = col % 2
        self.y = lax.axis_index("depth")

    def on_x(self, step):
        return ((self.x + step) % 4, self.z * 2 + self.c, self.y)

    def on_y(self, step):
        return (self.x, self.z * 2 + self.c, (self.y + step) % 4)

    def on_z(self, step):
        return (self.x, ((self.z + step) % 4) * 2 + self.c, self.y)

    def partner_y(self):
        return (self.x, self.z * 2 + self.c, self.y + 1 - 2 * (self.y % 2))

    def other_core(self):
        return (self.x, self.z * 2 + 1 - self.c, self.y)


def greet(peers):
    barrier = pltpu.get_barrier_semaphore()
    for peer in peers:
        pl.semaphore_signal(barrier, inc=1, device_id=peer, device_id_type=MESH)
    pl.semaphore_wait(barrier, len(peers))


class Mover:
    def __init__(self, send, recv):
        self.send, self.recv, self.used, self.all = send, recv, 0, []

    def make(self, k, src, dst, peer):
        return pltpu.make_async_remote_copy(
            src_ref=src,
            dst_ref=dst,
            send_sem=self.send.at[k],
            recv_sem=self.recv.at[k],
            device_id=peer,
            device_id_type=MESH,
        )

    def start(self, src, dst, peer):
        copy = self.make(self.used, src, dst, peer)
        self.used += 1
        copy.start()
        self.all.append(copy)
        return copy

    def sent(self, copy):
        copy.wait_send()
        self.all = [other for other in self.all if other is not copy]

    def finish(self):
        for copy in self.all:
            copy.wait_send()


class Ring:
    def __init__(self, mover, me, view, peer):
        self.mover, self.me, self.view, self.peer = mover, me, view, peer

    def begin(self):
        own = self.view(self.me, None)
        self.right = self.mover.start(own, own, self.peer(1))
        self.left = self.mover.start(own, own, self.peer(3))

    def forward(self):
        self.right.wait_recv()
        part = self.view((self.me + 3) % 4, 0)
        self.far_right = self.mover.start(part, part, self.peer(1))
        self.left.wait_recv()
        part = self.view((self.me + 1) % 4, 1)
        self.far_left = self.mover.start(part, part, self.peer(3))

    def copies(self):
        return [self.right, self.left, self.far_right, self.far_left]

    def end(self):
        self.far_right.wait_recv()
        self.far_left.wait_recv()


def merge(a, b):
    peak = jnp.maximum(a[..., 0:1, :], b[..., 0:1, :])
    total = a[..., 1:2, :] * jnp.exp(a[..., 0:1, :] - peak) + b[..., 1:2, :] * jnp.exp(
        b[..., 0:1, :] - peak
    )
    return jnp.concatenate([peak, total, a[..., 2:3, :] + b[..., 2:3, :], a[..., 3:, :]], axis=-2)


def over(count, read, write, unroll):
    def group(steps):
        rows = [pl.ds(pl.multiple_of(step * ROWS, ROWS), ROWS) for step in steps]
        for r, value in zip(rows, [read(r) for r in rows]):
            write(r, value)

    steps = count // ROWS
    whole = steps // unroll

    @pl.loop(0, whole)
    def _(g):
        group([g * unroll + u for u in range(unroll)])

    if steps % unroll:
        group(list(range(whole * unroll, steps)))


def wide(value, width):
    return jnp.concatenate([value] * (width // 128), axis=1)


def fold(op, value):
    parts = [value[:, k : k + 128] for k in range(0, value.shape[1], 128)]
    while len(parts) > 1:
        paired = [op(a, b) for a, b in zip(parts[::2], parts[1::2])]
        parts = paired + parts[len(paired) * 2 :]
    return parts[0]


def to_column(row):
    return jnp.transpose(jnp.broadcast_to(row, (128, row.shape[1])))


def span(half, count):
    return slice(None) if half is None else pl.ds(half * (count // 2), count // 2)


def fused_kernel(
    own,
    ref_own,
    weight_in,
    ref_weight_in,
    masks,
    wanted,
    pair_index,
    chosen_flag,
    loss,
    rows_out,
    grad_out,
    turned_out,
    kept,
    pairs,
    turned,
    weight,
    ref_weight,
    gathered,
    refs,
    partial,
    qsend,
    qrecv,
    ssend,
    srecv,
    column,
    inverse,
    third,
    kept_wanted,
    choose,
    place,
    kept_mask,
    spread,
    ref_logits,
    ref_column,
    ref_stats,
    held,
    got,
    info,
    token_weights,
    grad_full,
    rows_all,
    y_send,
    z_recv,
    z_sum,
    row_ssend,
    row_srecv,
    send,
    recv,
    local,
):
    at = Place()
    x, z, c, y = at.x, at.z, at.c, at.y
    share, width = spread.shape[1], spread.shape[2]
    depth = own.shape[1]
    half = width // 2
    f32, bf16 = jnp.float32, jnp.bfloat16
    fetch = [
        pltpu.make_async_copy(weight_in, weight, local.at[10]),
        pltpu.make_async_copy(ref_weight_in, ref_weight, local.at[11]),
    ]
    for copy in fetch:
        copy.start()
    ways = [at.on_x, at.on_y, at.on_z]
    greet([way(i) for way in ways for i in (1, 2, 3)] + [at.other_core()])
    move = Mover(send, recv)

    gathered[z, c, y] = own[...]
    low, high = pl.ds(0, depth // 2), pl.ds(depth // 2, depth // 2)
    count = own.shape[0]
    first_y = Ring(move, y, lambda i, h: gathered.at[z, c, i, span(h, count), low], at.on_y)
    first_z = Ring(move, z, lambda i, h: gathered.at[i, c, y, span(h, count), high], at.on_z)
    then_z = Ring(move, z, lambda i, h: gathered.at[i, c, span(h, 4), :, low], at.on_z)
    then_y = Ring(move, y, lambda i, h: gathered.at[span(h, 4), c, i, :, high], at.on_y)
    first_y.begin()
    first_z.begin()

    side, pair = y % 2, y // 2
    ref_depth = ref_own.shape[1]
    quarter = ref_depth // 4
    for k in range(4):
        z_sum[8 * k : 8 * k + 8, :] = ref_own[:, k * quarter : (k + 1) * quarter].astype(f32)
    swap = move.start(
        z_sum.at[pl.ds(pl.multiple_of(16 - 16 * side, 16), 16), :],
        z_sum.at[32:48, :],
        at.partner_y(),
    )
    column[...] = jnp.zeros_like(column)
    first_y.forward()
    first_z.forward()
    swap.wait_recv()
    mine, theirs = z_sum[pl.ds(pl.multiple_of(16 * side, 16), 16), :], z_sum[32:48, :]
    for f in (0, 1):
        a, b = mine[8 * f : 8 * f + 8], theirs[8 * f : 8 * f + 8]
        block = [jnp.where(side == 0, a, b), jnp.where(side == 0, b, a)]
        refs[x, z, c, f, pair, side] = jnp.concatenate(block, axis=0).astype(bf16)
    move.sent(swap)
    ref_x = Ring(
        move,
        x,
        lambda i, h: refs.at[i, z, c, slice(None) if h is None else h, pair, side],
        at.on_x,
    )
    ref_y = Ring(move, y, lambda i, h: refs.at[span(h, 4), z, c, 0, i // 2, i % 2], at.on_y)
    ref_z = Ring(move, z, lambda i, h: refs.at[span(h, 4), i, c, 1, pair, side], at.on_z)
    ref_yz = Ring(move, z, lambda i, h: refs.at[span(h, 4), i, c, 0], at.on_z)
    ref_zy = Ring(move, y, lambda i, h: refs.at[span(h, 4), :, c, 1, i // 2, i % 2], at.on_y)
    ref_core = []
    ref_rings = [ref_x, ref_y, ref_z, ref_yz, ref_zy]

    def to_core(ring, i):
        part = ring.view((ring.me + i) % 4, None)
        ref_core.append(move.start(part, part, at.other_core()))

    own_core = []

    def share_core(ring, steps):
        for i in steps:
            part = ring.view((ring.me + i) % 4, None)
            own_core.append(move.start(part, part, at.other_core()))

    first_y.end()
    then_z.begin()
    share_core(then_z, (0,))
    first_z.end()
    then_y.begin()
    share_core(then_y, (0,))
    ref_x.begin()

    def runs(owner):
        lane = lax.broadcasted_iota(jnp.int32, (1, 2 * LEN), 1)
        mask = masks[owner]
        a = jnp.where(lane < LEN, mask, 0)
        b = jnp.where(lane < LEN, 0, mask)
        return (
            jnp.sum(a, axis=1, keepdims=True),
            jnp.sum(b, axis=1, keepdims=True),
            jnp.min(jnp.where(a > 0, lane, 2 * LEN), axis=1, keepdims=True),
            jnp.min(jnp.where(b > 0, lane, 2 * LEN), axis=1, keepdims=True),
        )

    def source(owner, i):
        len_a, len_b, start_a, start_b = runs(owner)
        second = jnp.where(i < len_a + len_b, start_b + i - len_a, -1)
        return jnp.where(i < len_a, start_a + i, second)

    def kept_masks(owner):
        len_a, len_b, _, _ = runs(owner)
        i = lax.broadcasted_iota(jnp.int32, (1, 2 * LEN), 1)
        a = (i < len_a).astype(f32)
        return a, (i < len_a + len_b).astype(f32) - a

    for k in range(4):
        ref_column[k] = to_column(wanted[k].astype(f32))

    lane = lax.broadcasted_iota(jnp.int32, (1, 128), 1)
    signs = [(2 * chosen_flag[s] - 1).astype(f32) for s in range(SEQS)]
    for s in range(SEQS):
        row = jnp.where(lane == SEQS, signs[s], 0.0)
        for other in range(SEQS):
            sign = jnp.where(pair_index[s] == pair_index[other], signs[other], 0.0)
            row += jnp.where(lane == other, sign, 0.0)
        pairs[s : s + 1, :] = row

    @pl.loop(0, 4)
    def _(o):
        to = source(o, lax.broadcasted_iota(jnp.int32, (share, 1), 0))
        here = lax.broadcasted_iota(jnp.int32, (share, 2 * LEN), 1) == to
        choose[o] = here.astype(bf16)
        target = jnp.sum(jnp.where(here, wanted[o].astype(f32), 0.0), axis=1, keepdims=True)
        kept_wanted[o] = jnp.broadcast_to(target, (share, 128))
        to = source(o, lax.broadcasted_iota(jnp.int32, (1, share), 1))
        row = lax.broadcasted_iota(jnp.int32, (2 * KEEP, share), 0) + SKIP
        place[o] = (row + jnp.where(row >= LEN, SKIP, 0) == to).astype(bf16)
        mask_a, mask_b = kept_masks(o)
        kept_mask[o, 0:1, :] = mask_a
        kept_mask[o, 1:2, :] = mask_b

    then_z.forward()
    share_core(then_z, (1, 3))
    then_y.forward()
    share_core(then_y, (1, 3))
    ref_x.forward()
    then_z.end()
    share_core(then_z, (2,))
    ref_x.end()
    ref_y.begin()
    ref_z.begin()
    then_y.end()
    share_core(then_y, (2,))
    ref_logits[...] = jnp.zeros_like(ref_logits)
    rows_all[:, :, 0:SKIP, :] = jnp.zeros((2, 2, SKIP, depth), f32)
    ref_y.forward()
    ref_z.forward()
    fetch[0].wait()
    for copy in own_core:
        copy.wait_recv()

    tile = 256

    def product(owner):
        whole = gathered[owner].reshape(2 * LEN, depth)
        kept[owner] = jnp.dot(choose[owner], whole, preferred_element_type=f32).astype(bf16)

        @pl.loop(0, width // tile)
        def _(j):
            cols = pl.ds(pl.multiple_of(j * tile, tile), tile)
            partial[owner, :, cols] = jnp.dot(
                kept[owner], weight[:, cols], preferred_element_type=f32
            )

    def encode(count, read, write, store=None):
        def top(rows, value):
            if store is not None:
                store(rows, value)
            column[rows, :] = fold(jnp.maximum, jnp.abs(value))

        over(count, read, top, 2)
        peak = jnp.max(column[0:count, :], axis=1, keepdims=True)
        step = jnp.broadcast_to(jnp.maximum(peak, 1e-30) * (1.0 / 32767.0), (count, 128))
        column[0:count, :] = step
        inverse[0:count, :] = 1.0 / step

        def code(rows):
            value = read(rows) if store is None else store(rows)
            value = value * wide(inverse[rows, :], value.shape[1])
            return jnp.round(value).astype(jnp.int32).astype(jnp.int16)

        over(count, code, write, 2)
        return jnp.transpose(column[...])[0:8]

    def decode(code, step):
        return code.astype(jnp.int32).astype(f32) * wide(step, code.shape[1])

    def pack(k, owner, part, peer, add=None):
        cols = pl.ds(part * half, half)
        slot = k % 3 % 2 + k // 3 * 2

        def plain(rows):
            return partial[owner, rows, cols]

        def summed(rows):
            return plain(rows) + decode(qrecv[add, rows, :], third[rows, :])

        def store(rows, value=None):
            if value is None:
                return plain(rows)
            partial[owner, rows, cols] = value

        def write(rows, code):
            qsend[slot, rows, :] = code

        if add is None:
            ssend[k] = encode(share, plain, write)
        else:
            third[...] = to_column(srecv[add, 0:1, :])
            ssend[k] = encode(share, summed, write, store)
        return (
            move.start(ssend.at[k], srecv.at[k], peer),
            move.start(qsend.at[slot], qrecv.at[k], peer),
        )

    def arrived(copies):
        for copy in copies:
            copy.wait_recv()

    def add_in(k, part):
        cols = pl.ds(part * half, half)
        column[...] = to_column(srecv[k, 0:1, :])

        def read(rows):
            return partial[x, rows, cols] + decode(qrecv[k, rows, :], column[rows, :])

        def write(rows, value):
            partial[x, rows, cols] = value

        over(share, read, write, 2)

    right, left = at.on_x(1), at.on_x(3)
    after, before, across = (x + 1) % 4, (x + 3) % 4, (x + 2) % 4
    product(across)
    r0 = pack(0, across, 0, right)
    l0 = pack(3, across, 1, left)
    ref_y.end()
    ref_yz.begin()
    to_core(ref_yz, 0)
    ref_z.end()
    ref_zy.begin()
    to_core(ref_zy, 0)
    product(after)
    r1 = pack(1, after, 1, right)
    product(before)
    l1 = pack(4, before, 0, left)
    product(x)

    def ref_product(e):
        step = e + e // 2 - 2 * (e // 3)
        plane, row = (z + step) % 4, (y + step) % 4
        part = jnp.zeros((2 * LEN, ref_weight.shape[1]), f32)
        for h in (0, 1):
            part += jnp.dot(
                refs[:, plane, :, 0, :, h].reshape(2 * LEN, quarter),
                ref_weight[2 * h * quarter : (2 * h + 1) * quarter, :],
                preferred_element_type=f32,
            )
        ref_logits[:, plane] += part.reshape(4, 2, 2, 16, ref_weight.shape[1])
        there = pl.ds(pl.multiple_of((row % 2 * 2 + 1) * quarter, quarter), quarter)

        @pl.loop(0, 2)
        def _(i):
            half_x = pl.ds(2 * i, 2)
            part = jnp.dot(
                refs[half_x, :, :, 1, row // 2, row % 2].reshape(2 * LEN, quarter),
                ref_weight[there, :],
                preferred_element_type=f32,
            )
            ref_logits[half_x, :, :, row // 2] += part.reshape(2, 4, 2, 16, ref_weight.shape[1])

    fetch[1].wait()
    arrived(ref_core[0:2])
    ref_product(0)
    arrived(r0)
    move.sent(r0[1])
    r2 = pack(2, after, 0, right, add=0)
    arrived(l0)
    move.sent(l0[1])
    l2 = pack(5, before, 1, left, add=3)
    ref_yz.forward()
    to_core(ref_yz, 1)
    to_core(ref_yz, 3)
    ref_zy.forward()
    to_core(ref_zy, 1)
    to_core(ref_zy, 3)
    arrived(r1)
    add_in(1, 1)
    arrived(l1)
    add_in(4, 0)
    ref_yz.end()
    to_core(ref_yz, 2)
    ref_zy.end()
    to_core(ref_zy, 2)
    arrived(ref_core[2:6])

    @pl.loop(1, 3)
    def _(e):
        ref_product(e)

    arrived(r2)
    arrived(l2)
    column[...] = to_column(srecv[2, 0:1, :])
    third[...] = to_column(srecv[5, 0:1, :])
    first = (lax.axis_index("col") * 4 + y) * width

    def entries(rows_count):
        lane = lax.broadcasted_iota(jnp.int32, (rows_count, width), 1)
        return (lane + first).astype(f32)

    def read(rows):
        codes = (decode(qrecv[2, rows, :], column[rows, :]), decode(qrecv[5, rows, :], third[rows, :]))
        return partial[x, rows, :] + jnp.concatenate(codes, axis=1)

    def write(rows, value):
        partial[x, rows, :] = value
        hits = entries(ROWS) == wide(kept_wanted[x, rows, :], width)
        column[rows, :] = fold(jnp.maximum, value)
        third[rows, :] = fold(jnp.add, jnp.where(hits, value, 0.0))

    over(share, read, write, 1)
    peak = jnp.broadcast_to(jnp.max(column[0:share, :], axis=1, keepdims=True), (share, 128))
    column[0:share, :] = peak

    def read(rows):
        return jnp.exp(partial[x, rows, :] - wide(column[rows, :], width))

    def write(rows, value):
        spread[x, rows, :] = value.astype(bf16)
        inverse[rows, :] = fold(jnp.add, value)

    over(share, read, write, 1)
    ring = Ring(
        move,
        x,
        lambda i, h: spread.at[i] if h is None else spread.at[i, :, pl.ds(h * half, half)],
        at.on_x,
    )
    ring.begin()
    total = jnp.sum(inverse[0:share, :], axis=1, keepdims=True)
    picked = jnp.sum(third[0:share, :], axis=1, keepdims=True)
    lane = lax.broadcasted_iota(jnp.int32, (share, 128), 1)
    column[0:share, :] = jnp.where(
        lane == 0, column[0:share, :], jnp.where(lane == 1, total, picked)
    )
    stats = jnp.transpose(column[...])[0:8]
    local_peak = stats[0:1]

    arrived(ref_core[6:8])
    ref_product(3)
    ref_width = ref_weight.shape[1]
    ref_entry = lax.axis_index("row") * 32 + lax.axis_index("col") * 4 + y

    @pl.loop(0, 16)
    def _(k):
        i, j = k // 4, k % 4
        rows = pl.ds(pl.multiple_of(j * 64, 64), 64)
        logits = ref_logits[i, j].reshape(64, ref_width)
        peak = jnp.max(logits, axis=1, keepdims=True)
        total = jnp.sum(jnp.exp(logits - peak), axis=1, keepdims=True)
        entry = (
            lax.broadcasted_iota(jnp.int32, (64, ref_width), 1) + ref_entry * ref_width
        ).astype(f32)
        picked = jnp.sum(
            jnp.where(entry == ref_column[i, rows, 0:1], logits, 0.0), axis=1, keepdims=True
        )
        lanes = lax.broadcasted_iota(jnp.int32, (64, 128), 1)
        ref_column[i, rows, :] = jnp.where(lanes == 0, peak, jnp.where(lanes == 1, total, picked))

    for i in range(4):
        ref_stats[i] = jnp.transpose(ref_column[i])[0:8]
    for copy in ref_core + [ring_copy for r in ref_rings for ring_copy in r.copies()]:
        move.sent(copy)

    for copies in (r1, l1, r2, l2):
        move.sent(copies[1])

    every = jnp.concatenate([stats[None], ref_stats[...]], axis=0)
    stages = [[at.other_core()], [at.on_y(i) for i in (1, 2, 3)], [at.on_z(i) for i in (1, 2, 3)]]
    slot = 0
    for s, peers in enumerate(stages):
        held[s] = every
        copies = [move.start(held.at[s], got.at[slot + k], peer) for k, peer in enumerate(peers)]
        arrived(copies)
        for k in range(len(peers)):
            every = merge(every, got[slot + k])
        slot += len(peers)

    def valid(mask, value):
        return jnp.sum(jnp.where(mask > 0, value, 0.0), axis=-1, keepdims=True)

    normalizer = every[0, 0:1] + jnp.log(every[0, 1:2])
    logp = every[0, 2:3] - normalizer
    info[x, 0] = jnp.concatenate(
        [
            normalizer,
            local_peak,
            jnp.broadcast_to(valid(kept_mask[x, 0:1, :], logp), (1, 2 * LEN)),
            jnp.broadcast_to(valid(kept_mask[x, 1:2, :], logp), (1, 2 * LEN)),
            jnp.zeros((4, 2 * LEN), f32),
        ],
        axis=0,
    )
    info[x, 1:5] = every[1:5]
    info_copies = [move.start(info.at[x], info.at[x], at.on_x(i)) for i in (1, 2, 3)]
    ring.forward()
    arrived(info_copies)
    merged = info[0, 1:5]
    for i in (1, 2, 3):
        merged = merge(merged, info[i, 1:5])
    ref_logp = merged[:, 2:3] - merged[:, 0:1] - jnp.log(merged[:, 1:2])
    natural = lax.broadcasted_iota(jnp.int32, (4, 1, 2 * LEN), 2)
    mask = masks[...]
    ref_sums = (
        valid(jnp.where(natural < LEN, mask, 0), ref_logp),
        valid(jnp.where(natural < LEN, 0, mask), ref_logp),
    )
    margin = jnp.zeros((SEQS, 2 * LEN), f32)
    for s in range(SEQS):
        ratio = info[s // 2, 0, 2 + s % 2 : 3 + s % 2, :] - ref_sums[s % 2][s // 2]
        margin += pairs[:, s : s + 1] * ratio
    margin *= beta_value
    log_sigmoid = jnp.minimum(margin, 0.0) - jnp.log1p(jnp.exp(-jnp.abs(margin)))
    loss[...] = jnp.broadcast_to(
        jnp.sum(log_sigmoid, axis=0, keepdims=True)[:, 0:128] * (-1.0 / SEQS), (8, 128)
    )
    weights = (
        (-loss_scale * beta_value / PAIRS)
        * jax.nn.sigmoid(-margin)
        * pairs[:, SEQS : SEQS + 1]
    )
    token_weights[...] = weights

    core_at, y_at, z_at = move.used, move.used + 8, move.used + 32
    move.used += 38

    def z_copies():
        copies = []
        for i in (1, 3, 2):
            there = (z + i) % 4
            k = z_at + 2 * i - 2
            copies.append(move.make(k, row_ssend.at[8], row_srecv.at[16 + i - 1], at.on_z(i)))
            part = y_send.at[0, pl.ds(pl.multiple_of(there * count, count), count), :]
            copies.append(move.make(k + 1, part, z_recv.at[i - 1], at.on_z(i)))
        return copies

    def core_copies(t):
        return [
            move.make(core_at + 2 * t, row_ssend.at[t], row_srecv.at[t], at.other_core()),
            move.make(core_at + 2 * t + 1, qrecv.at[4 + t % 2, 0:LEN, :], qrecv.at[t, 0:LEN, :], at.other_core()),
        ]

    def y_copies(t):
        copies = []
        for i in (1, 3, 2):
            k = t * 3 + i - 1
            there = (y + i) % 4
            part = y_send.at[t % 2, pl.ds(pl.multiple_of(there * count, count), count), :]
            copies.append(
                move.make(y_at + 2 * k, row_ssend.at[4 + t], row_srecv.at[4 + k], at.on_y(i))
            )
            into = qsend.at[t, (i - 1) * count : i * count, :]
            copies.append(move.make(y_at + 2 * k + 1, part, into, at.on_y(i)))
        return copies

    def grad_part(owner, f, cols):
        return refs[owner, :, :, f, :, 0, :, cols].reshape(2 * LEN, -1)[0:share]

    def out_copies(owner):
        return [
            pltpu.make_async_copy(
                refs.at[owner, :, :, f, :, 0],
                grad_out.at[owner, :, :, :, :, pl.ds(f * quarter, quarter)],
                local.at[2 * owner + f],
            )
            for f in (0, 1)
        ]

    def turned_copy(k):
        rows = pl.ds(pl.multiple_of(k * 2 * LEN, 2 * LEN), 2 * LEN)
        return pltpu.make_async_copy(
            turned, turned_out.at[rows, :], local.at[8]
        )

    def turn(k):
        rows = pl.ds(pl.multiple_of(k * 2 * LEN, 2 * LEN), 2 * LEN)

        @pl.when(k >= 1)
        def _():
            turned_copy(k - 1).wait()

        turned[...] = jnp.transpose(kept[:, :, rows].reshape(4 * share, 2 * LEN))
        turned_copy(k).start()

    def sent(copies):
        for copy in copies:
            copy.wait_send()

    def owner_of(t):
        return (x + t + t // 2 - 2 * (t // 3)) % 4

    mine_rows = pl.ds(pl.multiple_of(y * count, count), count)

    def rows_of(owner):
        return pl.ds(pl.multiple_of(owner * count, count), count)

    @pl.loop(0, 6)
    def _(t):
        @pl.when(t == 3)
        def _():
            ring.end()

        @pl.when((t >= 2) & (t < 4))
        def _():
            sent(core_copies(t - 2))

        @pl.when(t < 4)
        def _():
            slot = t % 2
            owner = owner_of(t)
            mask_a, mask_b = kept_mask[owner, 0:1, :], kept_mask[owner, 1:2, :]
            weight_a = token_weights[pl.ds(2 * owner, 1), :]
            weight_b = token_weights[pl.ds(2 * owner + 1, 1), :]
            token = mask_a * weight_a + mask_b * weight_b
            factor = jnp.where(
                mask_a + mask_b > 0, token * jnp.exp(info[owner, 0, 1:2, :] - info[owner, 0, 0:1, :]), 0.0
            )
            column[...] = to_column(token)
            third[...] = to_column(factor)

            def read(rows):
                hits = entries(ROWS) == wide(kept_wanted[owner, rows, :], width)
                return (
                    jnp.where(hits, wide(column[rows, :], width), 0.0)
                    - wide(third[rows, :], width) * spread[owner, rows, :].astype(f32)
                ).astype(bf16)

            @pl.loop(0, share // ROWS)
            def _(r):
                value = read(pl.ds(pl.multiple_of(r * ROWS, ROWS), ROWS))
                refs[owner, r // 4, r // 2 % 2, 0, r % 2, 0] = value[:, 0:half]
                refs[owner, r // 4, r // 2 % 2, 1, r % 2, 0] = value[:, half:]

            for copy in out_copies(owner):
                copy.start()

            for f in (0, 1):

                @pl.loop(0, half // tile)
                def _(j):
                    cols = pl.ds(pl.multiple_of(j * tile, tile), tile)
                    there = pl.ds(pl.multiple_of(f * half + j * tile, tile), tile)
                    grad_full[:, there] = jnp.dot(
                        place[owner], grad_part(owner, f, cols), preferred_element_type=f32
                    ).astype(bf16)

            @pl.loop(0, depth // 256)
            def _(j):
                cols = pl.ds(pl.multiple_of(j * 256, 256), 256)
                rows_all[slot, :, SKIP:LEN, cols] = lax.dot_general(
                    grad_full[...],
                    weight[cols, :],
                    (((1,), (1,)), ((), ())),
                    preferred_element_type=f32,
                ).reshape(2, KEEP, 256)

            def write(rows, code):
                qrecv[4 + slot, rows, :] = code

            row_ssend[t] = encode(LEN, lambda rows: rows_all[slot, 1 - c, rows, :], write)
            for copy in core_copies(t):
                copy.start()

        @pl.when((t >= 3) & (t < 5))
        def _():
            sent(y_copies(t - 3))

        @pl.when((t >= 1) & (t < 5))
        def _():
            u = t - 1
            slot = u % 2
            for copy in core_copies(u):
                copy.wait_recv()
            third[...] = to_column(row_srecv[u, 0:1, :])

            def read(rows):
                return rows_all[slot, c, rows, :] + decode(qrecv[u, rows, :], third[rows, :])

            def store(rows, value=None):
                if value is None:
                    return rows_all[slot, c, rows, :]
                rows_all[slot, c, rows, :] = value

            def write(rows, code):
                y_send[slot, rows, :] = code

            row_ssend[4 + u] = encode(LEN, read, write, store)
            for copy in y_copies(u):
                copy.start()
            z_sum[rows_of(owner_of(u)), :] = rows_all[slot, c, mine_rows, :]

        @pl.when(t >= 2)
        def _():
            v = t - 2
            for copy in y_copies(v):
                copy.wait_recv()
            total = z_sum[rows_of(owner_of(v)), :]
            for i in range(3):
                k = v * 3 + i
                column[...] = to_column(row_srecv[4 + k, 0:1, :])
                code = qsend[v, i * count : (i + 1) * count, :]
                total += decode(code, column[mine_rows, :])
            z_sum[rows_of(owner_of(v)), :] = total

        @pl.when(t == 5)
        def _():
            for u in (2, 3):
                sent(core_copies(u))
                sent(y_copies(u))

            def write(rows, code):
                y_send[0, rows, :] = code

            row_ssend[8] = encode(LEN, lambda rows: z_sum[rows, :], write)
            for copy in z_copies():
                copy.start()

        @pl.when(t >= 3)
        def _():
            start = 2 * (t - 3)

            @pl.loop(start, jnp.minimum(start + 2, depth // (2 * LEN)))
            def _(k):
                turn(k)

    for copy in z_copies():
        copy.wait_recv()
    here = pl.ds(pl.multiple_of(z * count, count), count)
    total = z_sum[here, :]
    for i in range(3):
        column[...] = to_column(row_srecv[16 + i, 0:1, :])
        total += decode(z_recv[i], column[here, :])
    rows_out[...] = total
    sent(z_copies())
    turned_copy(depth // (2 * LEN) - 1).wait()
    for owner in range(4):
        for copy in out_copies(owner):
            copy.wait()
    move.finish()


def fused(index, share, states, others, weight, ref_weight, masks, wanted, pair_index, chosen):
    vmem = pl.BlockSpec(memory_space=pltpu.VMEM)
    count, depth = states.shape
    width = weight.shape[1]
    ref_rows, ref_depth = others.shape
    quarter = ref_depth // 4
    f32, bf16, i16 = jnp.float32, jnp.bfloat16, jnp.int16
    lanes = 2 * LEN
    copies = 128
    return pl.pallas_call(
        fused_kernel,
        name="fused_%d" % share,
        out_shape=(
            jax.ShapeDtypeStruct((8, 128), f32),
            jax.ShapeDtypeStruct((count, depth), f32),
            jax.ShapeDtypeStruct((4, 4, 2, 2, 2 * ref_rows, width), bf16),
            jax.ShapeDtypeStruct((depth, 4 * share), bf16),
        ),
        in_specs=[vmem] * 2
        + [pl.BlockSpec(memory_space=pl.ANY)] * 2
        + [vmem] * 2
        + [pl.BlockSpec(memory_space=pltpu.SMEM)] * 2,
        out_specs=(vmem, vmem, pl.BlockSpec(memory_space=pl.ANY), pl.BlockSpec(memory_space=pl.ANY)),
        scratch_shapes=[
            pltpu.VMEM((4, share, depth), bf16),
            pltpu.VMEM((8, 128), f32),
            pltpu.VMEM((lanes, 4 * share), bf16),
            pltpu.VMEM(weight.shape, bf16),
            pltpu.VMEM(ref_weight.shape, bf16),
            pltpu.VMEM((4, 2, 4, count, depth), bf16),
            pltpu.VMEM((4, 4, 2, 2, 2, 2, 2 * ref_rows, quarter), bf16),
            pltpu.VMEM((4, share, width), f32),
            pltpu.VMEM((4, share, width // 2), i16),
            pltpu.VMEM((6, share, width // 2), i16),
            pltpu.VMEM((6, 8, lanes), f32),
            pltpu.VMEM((6, 8, lanes), f32),
            pltpu.VMEM((lanes, 128), f32),
            pltpu.VMEM((lanes, 128), f32),
            pltpu.VMEM((lanes, 128), f32),
            pltpu.VMEM((4, share, 128), f32),
            pltpu.VMEM((4, share, lanes), bf16),
            pltpu.VMEM((4, 2 * KEEP, share), bf16),
            pltpu.VMEM((4, 8, lanes), f32),
            pltpu.VMEM((4, share, width), bf16),
            pltpu.VMEM((4, 4, 2, 2, 2 * ref_rows, ref_weight.shape[1]), f32),
            pltpu.VMEM((4, lanes, 128), f32),
            pltpu.VMEM((4, 8, lanes), f32),
            pltpu.VMEM((3, 5, 8, lanes), f32),
            pltpu.VMEM((7, 5, 8, lanes), f32),
            pltpu.VMEM((4, 5, 8, lanes), f32),
            pltpu.VMEM((8, lanes), f32),
            pltpu.VMEM((2 * KEEP, width), bf16),
            pltpu.VMEM((2, 2, LEN, depth), f32),
            pltpu.VMEM((2, LEN, depth), i16),
            pltpu.VMEM((3, count, depth), i16),
            pltpu.VMEM((LEN, depth), f32),
            pltpu.VMEM((9, 8, lanes), f32),
            pltpu.VMEM((19, 8, lanes), f32),
            pltpu.SemaphoreType.DMA((copies,)),
            pltpu.SemaphoreType.DMA((copies,)),
            pltpu.SemaphoreType.DMA((12,)),
        ],
        compiler_params=pltpu.CompilerParams(
            collective_id=index, has_side_effects=True, vmem_limit_bytes=VMEM_LIMIT
        ),
    )(states, others, weight, ref_weight, masks, wanted, pair_index, chosen)


def weight_kernel(turned, grad, out):
    whole = jnp.concatenate([grad[owner] for owner in range(4)], axis=0)
    out[...] = jnp.dot(turned[...], whole, preferred_element_type=jnp.float32)


def weight_gradient(turned, grad):
    depth, tokens = turned.shape
    width = grad.shape[2]
    tile = 512
    return pl.pallas_call(
        weight_kernel,
        name="weight_gradient",
        grid=(width // tile,),
        out_shape=jax.ShapeDtypeStruct((depth, width), jnp.float32),
        in_specs=[
            pl.BlockSpec((depth, tokens), lambda j: (0, 0)),
            pl.BlockSpec((4, tokens // 4, tile), lambda j: (0, 0, j)),
        ],
        out_specs=pl.BlockSpec((depth, tile), lambda j: (0, j)),
        compiler_params=pltpu.CompilerParams(vmem_limit_bytes=VMEM_LIMIT),
    )(turned, grad)


def on_device(
    policy_states,
    reference_states,
    policy_weight,
    reference_weight,
    targets,
    response_mask,
    pair_index,
    chosen_flag,
):
    masks = response_mask.reshape(4, 1, 2 * LEN)
    wanted = targets.reshape(4, 1, 2 * LEN)

    def run(index):
        def branch(*operands):
            loss, grad_states, grad, turned = fused(index, SIZES[index], *operands)
            grad_weight = weight_gradient(turned, grad.reshape(4, 2 * LEN, -1))
            return (loss[0, 0], grad_states, grad_weight)

        return branch

    longest = jnp.max(jnp.sum(response_mask.reshape(4, 2 * LEN), axis=1))
    size = sum((longest > s).astype(jnp.int32) for s in SIZES[:-1])
    return lax.switch(
        size,
        [run(i) for i in range(len(SIZES))],
        policy_states,
        reference_states,
        policy_weight,
        reference_weight,
        masks,
        wanted,
        pair_index,
        chosen_flag,
    )


def solution(mesh):
    in_specs = (
        P(("col", "depth"), "row"),
        P(("row", "col", "depth"), None),
        P("row", ("col", "depth")),
        P(None, ("row", "col", "depth")),
        P(),
        P(),
        P(),
        P(),
    )
    out_specs = (P(), P(("col", "depth"), "row"), P("row", ("col", "depth")))
    return jax.shard_map(
        on_device, mesh=mesh, in_specs=in_specs, out_specs=out_specs, check_vma=False
    )
```

```python
import functools

import jax
import jax.numpy as jnp
from jax import lax
from jax.experimental import pallas as pl
from jax.experimental.pallas import tpu as pltpu
from jax.sharding import PartitionSpec as P

PAIRS = 4
LEN = 128
SEQS = 8
SKIP = 16
KEEP = LEN - SKIP
SIZES = (176, 192, 2 * KEEP)

beta_value = 0.1
loss_scale = 256.0

MESH = pl.DeviceIdType.MESH
VMEM_LIMIT = 62 * 1024 * 1024
ROWS = 16


class Place:
    def __init__(self):
        self.x = lax.axis_index("row")
        col = lax.axis_index("col")
        self.z = col // 2
        self.c = col % 2
        self.y = lax.axis_index("depth")

    def on_x(self, step):
        return ((self.x + step) % 4, self.z * 2 + self.c, self.y)

    def on_y(self, step):
        return (self.x, self.z * 2 + self.c, (self.y + step) % 4)

    def on_z(self, step):
        return (self.x, ((self.z + step) % 4) * 2 + self.c, self.y)

    def partner_y(self):
        return (self.x, self.z * 2 + self.c, self.y + 1 - 2 * (self.y % 2))

    def other_core(self):
        return (self.x, self.z * 2 + 1 - self.c, self.y)


def greet(peers):
    barrier = pltpu.get_barrier_semaphore()
    for peer in peers:
        pl.semaphore_signal(barrier, inc=1, device_id=peer, device_id_type=MESH)
    pl.semaphore_wait(barrier, len(peers))


class Mover:
    def __init__(self, send, recv):
        self.send, self.recv, self.used, self.all = send, recv, 0, []

    def make(self, k, src, dst, peer):
        return pltpu.make_async_remote_copy(
            src_ref=src,
            dst_ref=dst,
            send_sem=self.send.at[k],
            recv_sem=self.recv.at[k],
            device_id=peer,
            device_id_type=MESH,
        )

    def start(self, src, dst, peer):
        copy = self.make(self.used, src, dst, peer)
        self.used += 1
        copy.start()
        self.all.append(copy)
        return copy

    def sent(self, copy):
        copy.wait_send()
        self.all = [other for other in self.all if other is not copy]

    def finish(self):
        for copy in self.all:
            copy.wait_send()


class Ring:
    def __init__(self, mover, me, view, peer):
        self.mover, self.me, self.view, self.peer = mover, me, view, peer

    def begin(self):
        own = self.view(self.me, None)
        self.right = self.mover.start(own, own, self.peer(1))
        self.left = self.mover.start(own, own, self.peer(3))

    def forward(self):
        self.right.wait_recv()
        part = self.view((self.me + 3) % 4, 0)
        self.far_right = self.mover.start(part, part, self.peer(1))
        self.left.wait_recv()
        part = self.view((self.me + 1) % 4, 1)
        self.far_left = self.mover.start(part, part, self.peer(3))

    def copies(self):
        return [self.right, self.left, self.far_right, self.far_left]

    def end(self):
        self.far_right.wait_recv()
        self.far_left.wait_recv()


def merge(a, b):
    peak = jnp.maximum(a[0], b[0])
    total = a[1] * jnp.exp(a[0] - peak) + b[1] * jnp.exp(b[0] - peak)
    return jnp.stack([peak, total, a[2] + b[2]])


def over(count, read, write, unroll):
    def group(steps):
        rows = [pl.ds(pl.multiple_of(step * ROWS, ROWS), ROWS) for step in steps]
        for r, value in zip(rows, [read(r) for r in rows]):
            write(r, value)

    steps = count // ROWS
    whole = steps // unroll

    @pl.loop(0, whole)
    def _(g):
        group([g * unroll + u for u in range(unroll)])

    if steps % unroll:
        group(list(range(whole * unroll, steps)))


def wide(value, width):
    return jnp.concatenate([value] * (width // 128), axis=1)


def fold(op, value):
    parts = [value[:, k : k + 128] for k in range(0, value.shape[1], 128)]
    while len(parts) > 1:
        paired = [op(a, b) for a, b in zip(parts[::2], parts[1::2])]
        parts = paired + parts[len(paired) * 2 :]
    return parts[0]


def to_column(row):
    return jnp.transpose(jnp.broadcast_to(row, (128, row.shape[1])))


def span(half, count):
    return slice(None) if half is None else pl.ds(half * (count // 2), count // 2)


def fused_kernel(
    own,
    ref_own,
    weight_in,
    ref_weight_in,
    masks,
    wanted,
    pair_index,
    chosen_flag,
    loss,
    rows_out,
    grad_out,
    turned_out,
    kept,
    pairs,
    turned,
    weight,
    ref_weight,
    gathered,
    refs,
    partial,
    qsend,
    qrecv,
    ssend,
    srecv,
    column,
    inverse,
    third,
    kept_wanted,
    choose,
    place,
    kept_mask,
    spread,
    ref_logits,
    ref_column,
    ref_stats,
    held,
    got,
    info,
    token_weights,
    grad_full,
    rows_all,
    y_send,
    z_recv,
    z_sum,
    row_ssend,
    row_srecv,
    send,
    recv,
    local,
):
    at = Place()
    x, z, c, y = at.x, at.z, at.c, at.y
    share, width = spread.shape[1], spread.shape[2]
    depth = own.shape[1]
    half = width // 2
    f32, bf16 = jnp.float32, jnp.bfloat16
    fetch = [
        pltpu.make_async_copy(weight_in, weight, local.at[10]),
        pltpu.make_async_copy(ref_weight_in, ref_weight, local.at[11]),
    ]
    for copy in fetch:
        copy.start()
    def arrived(copies):
        for copy in copies:
            copy.wait_recv()

    ways = [at.on_x, at.on_y, at.on_z]
    greet([way(i) for way in ways for i in (1, 2, 3)] + [at.other_core()])
    move = Mover(send, recv)

    gathered[z, c, y] = own[...]
    low, high = pl.ds(0, depth // 2), pl.ds(depth // 2, depth // 2)
    count = own.shape[0]
    first_y = [(gathered.at[z, c, y, :, low], at.on_y(i)) for i in (1, 3, 2)]
    first_z = [(gathered.at[z, c, y, :, high], at.on_z(i)) for i in (1, 3, 2)]
    then_z = Ring(move, z, lambda i, h: gathered.at[i, c, span(h, 4), :, low], at.on_z)
    then_y = Ring(move, y, lambda i, h: gathered.at[span(h, 4), c, i, :, high], at.on_y)
    first_y = [move.start(part, part, peer) for part, peer in first_y]
    first_z = [move.start(part, part, peer) for part, peer in first_z]

    side, pair = y % 2, y // 2
    ref_depth = ref_own.shape[1]
    quarter = ref_depth // 4
    for k in range(4):
        z_sum[8 * k : 8 * k + 8, :] = ref_own[:, k * quarter : (k + 1) * quarter].astype(f32)
    swap = move.start(
        z_sum.at[pl.ds(pl.multiple_of(16 - 16 * side, 16), 16), :],
        z_sum.at[32:48, :],
        at.partner_y(),
    )
    column[...] = jnp.zeros_like(column)
    swap.wait_recv()
    mine, theirs = z_sum[pl.ds(pl.multiple_of(16 * side, 16), 16), :], z_sum[32:48, :]
    for f in (0, 1):
        a, b = mine[8 * f : 8 * f + 8], theirs[8 * f : 8 * f + 8]
        block = [jnp.where(side == 0, a, b), jnp.where(side == 0, b, a)]
        refs[x, z, c, f, pair, side] = jnp.concatenate(block, axis=0).astype(bf16)
    move.sent(swap)
    ref_x = Ring(
        move,
        x,
        lambda i, h: refs.at[i, z, c, slice(None) if h is None else h, pair, side],
        at.on_x,
    )
    ref_y = Ring(move, y, lambda i, h: refs.at[span(h, 4), z, c, 0, i // 2, i % 2], at.on_y)
    ref_z = Ring(move, z, lambda i, h: refs.at[span(h, 4), i, c, 1, pair, side], at.on_z)
    ref_yz = Ring(move, z, lambda i, h: refs.at[span(h, 4), i, c, 0], at.on_z)
    ref_zy = Ring(move, y, lambda i, h: refs.at[span(h, 4), :, c, 1, i // 2, i % 2], at.on_y)
    ref_core = []
    ref_rings = [ref_x, ref_y, ref_z, ref_yz, ref_zy]

    def to_core(ring, i):
        part = ring.view((ring.me + i) % 4, None)
        ref_core.append(move.start(part, part, at.other_core()))

    own_core = []

    def share_core(ring, steps):
        for i in steps:
            part = ring.view((ring.me + i) % 4, None)
            own_core.append(move.start(part, part, at.other_core()))

    arrived(first_y)
    then_z.begin()
    share_core(then_z, (0,))
    arrived(first_z)
    then_y.begin()
    share_core(then_y, (0,))
    ref_x.begin()

    def runs(owner):
        lane = lax.broadcasted_iota(jnp.int32, (1, 2 * LEN), 1)
        mask = masks[owner]
        a = jnp.where(lane < LEN, mask, 0)
        b = jnp.where(lane < LEN, 0, mask)
        return (
            jnp.sum(a, axis=1, keepdims=True),
            jnp.sum(b, axis=1, keepdims=True),
            jnp.min(jnp.where(a > 0, lane, 2 * LEN), axis=1, keepdims=True),
            jnp.min(jnp.where(b > 0, lane, 2 * LEN), axis=1, keepdims=True),
        )

    def source(owner, i):
        len_a, len_b, start_a, start_b = runs(owner)
        second = jnp.where(i < len_a + len_b, start_b + i - len_a, -1)
        return jnp.where(i < len_a, start_a + i, second)

    def kept_masks(owner):
        len_a, len_b, _, _ = runs(owner)
        i = lax.broadcasted_iota(jnp.int32, (1, 2 * LEN), 1)
        a = (i < len_a).astype(f32)
        return a, (i < len_a + len_b).astype(f32) - a

    for k in range(4):
        ref_column[k] = to_column(wanted[k].astype(f32))

    lane = lax.broadcasted_iota(jnp.int32, (1, 128), 1)
    signs = [(2 * chosen_flag[s] - 1).astype(f32) for s in range(SEQS)]
    for s in range(SEQS):
        row = jnp.where(lane == SEQS, signs[s], 0.0)
        for other in range(SEQS):
            sign = jnp.where(pair_index[s] == pair_index[other], signs[other], 0.0)
            row += jnp.where(lane == other, sign, 0.0)
        pairs[s : s + 1, :] = row

    @pl.loop(0, 4)
    def _(o):
        to = source(o, lax.broadcasted_iota(jnp.int32, (share, 1), 0))
        here = lax.broadcasted_iota(jnp.int32, (share, 2 * LEN), 1) == to
        choose[o] = here.astype(bf16)
        target = jnp.sum(jnp.where(here, wanted[o].astype(f32), 0.0), axis=1, keepdims=True)
        kept_wanted[o] = jnp.broadcast_to(target, (share, 128))
        to = source(o, lax.broadcasted_iota(jnp.int32, (1, share), 1))
        row = lax.broadcasted_iota(jnp.int32, (2 * KEEP, share), 0) + SKIP
        place[o] = (row + jnp.where(row >= LEN, SKIP, 0) == to).astype(bf16)
        mask_a, mask_b = kept_masks(o)
        kept_mask[o, 0:1, :] = mask_a
        kept_mask[o, 1:2, :] = mask_b

    then_z.forward()
    share_core(then_z, (1, 3))
    then_y.forward()
    share_core(then_y, (1, 3))
    ref_x.forward()
    then_z.end()
    share_core(then_z, (2,))
    ref_x.end()
    ref_y.begin()
    ref_z.begin()
    then_y.end()
    share_core(then_y, (2,))
    ref_logits[...] = jnp.zeros_like(ref_logits)
    rows_all[:, :, 0:SKIP, :] = jnp.zeros((2, 2, SKIP, depth), f32)
    ref_y.forward()
    ref_z.forward()
    fetch[0].wait()
    for copy in own_core:
        copy.wait_recv()

    tile = 640

    def product(owner):
        whole = gathered[owner].reshape(2 * LEN, depth)
        kept[owner] = jnp.dot(choose[owner], whole, preferred_element_type=f32).astype(bf16)

        @pl.loop(0, width // tile)
        def _(j):
            cols = pl.ds(pl.multiple_of(j * tile, tile), tile)
            partial[owner, :, cols] = jnp.dot(
                kept[owner], weight[:, cols], preferred_element_type=f32
            )

    def encode(count, read, write, store=None):
        def top(rows, value):
            if store is not None:
                store(rows, value)
            column[rows, :] = fold(jnp.maximum, jnp.abs(value))

        over(count, read, top, 2)
        peak = jnp.max(column[0:count, :], axis=1, keepdims=True)
        step = jnp.broadcast_to(jnp.maximum(peak, 1e-30) * (1.0 / 32767.0), (count, 128))
        column[0:count, :] = step
        inverse[0:count, :] = 1.0 / step

        def code(rows):
            value = read(rows) if store is None else store(rows)
            value = value * wide(inverse[rows, :], value.shape[1])
            return jnp.round(value).astype(jnp.int32).astype(jnp.int16)

        over(count, code, write, 2)
        return jnp.transpose(column[...])[0:8]

    def decode(code, step):
        return code.astype(jnp.int32).astype(f32) * wide(step, code.shape[1])

    def pack(k, owner, part, peer, add=None):
        cols = pl.ds(part * half, half)
        slot = k % 3 % 2 + k // 3 * 2

        def plain(rows):
            return partial[owner, rows, cols]

        def summed(rows):
            return plain(rows) + decode(qrecv[add, rows, :], third[rows, :])

        def store(rows, value=None):
            if value is None:
                return plain(rows)
            partial[owner, rows, cols] = value

        def write(rows, code):
            qsend[slot, rows, :] = code

        if add is None:
            ssend[k] = encode(share, plain, write)
        else:
            third[...] = to_column(srecv[add, 0:1, :])
            ssend[k] = encode(share, summed, write, store)
        return (
            move.start(ssend.at[k], srecv.at[k], peer),
            move.start(qsend.at[slot], qrecv.at[k], peer),
        )

    def add_in(k, part):
        cols = pl.ds(part * half, half)
        column[...] = to_column(srecv[k, 0:1, :])

        def read(rows):
            return partial[x, rows, cols] + decode(qrecv[k, rows, :], column[rows, :])

        def write(rows, value):
            partial[x, rows, cols] = value

        over(share, read, write, 2)

    right, left = at.on_x(1), at.on_x(3)
    after, before, across = (x + 1) % 4, (x + 3) % 4, (x + 2) % 4
    product(across)
    r0 = pack(0, across, 0, right)
    l0 = pack(3, across, 1, left)
    ref_y.end()
    ref_yz.begin()
    to_core(ref_yz, 0)
    ref_z.end()
    ref_zy.begin()
    to_core(ref_zy, 0)
    product(after)
    r1 = pack(1, after, 1, right)
    product(before)
    l1 = pack(4, before, 0, left)
    product(x)

    def ref_product(e):
        step = e + e // 2 - 2 * (e // 3)
        plane, row = (z + step) % 4, (y + step) % 4
        part = jnp.zeros((2 * LEN, ref_weight.shape[1]), f32)
        for h in (0, 1):
            part += jnp.dot(
                refs[:, plane, :, 0, :, h].reshape(2 * LEN, quarter),
                ref_weight[2 * h * quarter : (2 * h + 1) * quarter, :],
                preferred_element_type=f32,
            )
        ref_logits[:, plane] += part.reshape(4, 2, 2, 16, ref_weight.shape[1])
        there = pl.ds(pl.multiple_of((row % 2 * 2 + 1) * quarter, quarter), quarter)

        @pl.loop(0, 2)
        def _(i):
            half_x = pl.ds(2 * i, 2)
            part = jnp.dot(
                refs[half_x, :, :, 1, row // 2, row % 2].reshape(2 * LEN, quarter),
                ref_weight[there, :],
                preferred_element_type=f32,
            )
            ref_logits[half_x, :, :, row // 2] += part.reshape(2, 4, 2, 16, ref_weight.shape[1])

    fetch[1].wait()
    arrived(ref_core[0:2])
    ref_product(0)
    arrived(r0)
    move.sent(r0[1])
    r2 = pack(2, after, 0, right, add=0)
    arrived(l0)
    move.sent(l0[1])
    l2 = pack(5, before, 1, left, add=3)
    ref_yz.forward()
    to_core(ref_yz, 1)
    to_core(ref_yz, 3)
    ref_zy.forward()
    to_core(ref_zy, 1)
    to_core(ref_zy, 3)
    arrived(r1)
    add_in(1, 1)
    arrived(l1)
    add_in(4, 0)
    ref_yz.end()
    to_core(ref_yz, 2)
    ref_zy.end()
    to_core(ref_zy, 2)
    arrived(ref_core[2:6])

    @pl.loop(1, 3)
    def _(e):
        ref_product(e)

    arrived(r2)
    arrived(l2)
    column[...] = to_column(srecv[2, 0:1, :])
    third[...] = to_column(srecv[5, 0:1, :])
    first = (lax.axis_index("col") * 4 + y) * width

    def entries(rows_count):
        lane = lax.broadcasted_iota(jnp.int32, (rows_count, width), 1)
        return (lane + first).astype(f32)

    def read(rows):
        codes = (decode(qrecv[2, rows, :], column[rows, :]), decode(qrecv[5, rows, :], third[rows, :]))
        return partial[x, rows, :] + jnp.concatenate(codes, axis=1)

    def write(rows, value):
        partial[x, rows, :] = value
        hits = entries(ROWS) == wide(kept_wanted[x, rows, :], width)
        column[rows, :] = fold(jnp.maximum, value)
        third[rows, :] = fold(jnp.add, jnp.where(hits, value, 0.0))

    over(share, read, write, 1)
    peak = jnp.broadcast_to(jnp.max(column[0:share, :], axis=1, keepdims=True), (share, 128))
    column[0:share, :] = peak

    def read(rows):
        return jnp.exp(partial[x, rows, :] - wide(column[rows, :], width))

    def write(rows, value):
        spread[x, rows, :] = value.astype(bf16)
        inverse[rows, :] = fold(jnp.add, value)

    over(share, read, write, 1)
    ring = Ring(
        move,
        x,
        lambda i, h: spread.at[i] if h is None else spread.at[i, :, pl.ds(h * half, half)],
        at.on_x,
    )
    ring.begin()
    total = jnp.sum(inverse[0:share, :], axis=1, keepdims=True)
    picked = jnp.sum(third[0:share, :], axis=1, keepdims=True)
    lane = lax.broadcasted_iota(jnp.int32, (share, 128), 1)
    column[0:share, :] = jnp.where(
        lane == 0, column[0:share, :], jnp.where(lane == 1, total, picked)
    )
    stats = jnp.transpose(column[...])[0:8]
    local_peak = stats[0:1]

    arrived(ref_core[6:8])
    ref_product(3)
    ref_width = ref_weight.shape[1]
    ref_entry = lax.axis_index("row") * 32 + lax.axis_index("col") * 4 + y

    @pl.loop(0, 16)
    def _(k):
        i, j = k // 4, k % 4
        rows = pl.ds(pl.multiple_of(j * 64, 64), 64)
        logits = ref_logits[i, j].reshape(64, ref_width)
        peak = jnp.max(logits, axis=1, keepdims=True)
        total = jnp.sum(jnp.exp(logits - peak), axis=1, keepdims=True)
        entry = (
            lax.broadcasted_iota(jnp.int32, (64, ref_width), 1) + ref_entry * ref_width
        ).astype(f32)
        picked = jnp.sum(
            jnp.where(entry == ref_column[i, rows, 0:1], logits, 0.0), axis=1, keepdims=True
        )
        lanes = lax.broadcasted_iota(jnp.int32, (64, 128), 1)
        ref_column[i, rows, :] = jnp.where(lanes == 0, peak, jnp.where(lanes == 1, total, picked))

    for i in range(4):
        ref_stats[i] = jnp.transpose(ref_column[i])[0:8]
    for copy in ref_core + [ring_copy for r in ref_rings for ring_copy in r.copies()]:
        move.sent(copy)

    for copies in (r1, l1, r2, l2):
        move.sent(copies[1])

    zeros = jnp.zeros((3, 2 * LEN), f32)
    every = jnp.stack(
        [
            jnp.concatenate(
                [stats[i : i + 1]] + [ref_stats[o, i : i + 1, :] for o in range(4)] + [zeros], axis=0
            )
            for i in range(3)
        ]
    )
    stages = [[at.other_core()], [at.on_y(i) for i in (1, 2, 3)], [at.on_z(i) for i in (1, 2, 3)]]
    slot = 0
    for s, peers in enumerate(stages):
        held[s] = every
        copies = [move.start(held.at[s], got.at[slot + k], peer) for k, peer in enumerate(peers)]
        arrived(copies)
        for k in range(len(peers)):
            every = merge(every, got[slot + k])
        slot += len(peers)

    def valid(mask, value):
        return jnp.sum(jnp.where(mask > 0, value, 0.0), axis=-1, keepdims=True)

    normalizer = every[0, 0:1] + jnp.log(every[1, 0:1])
    logp = every[2, 0:1] - normalizer
    sums = [
        jnp.broadcast_to(valid(kept_mask[x, i : i + 1, :], logp), (1, 2 * LEN)) for i in (0, 1)
    ]
    info[x, 0] = jnp.concatenate([normalizer, every[0, 1:5], local_peak, zeros[0:2]], axis=0)
    info[x, 1] = jnp.concatenate([sums[0], every[1, 1:8]], axis=0)
    info[x, 2] = jnp.concatenate([sums[1], every[2, 1:8]], axis=0)
    info_copies = [move.start(info.at[x], info.at[x], at.on_x(i)) for i in (1, 2, 3)]
    ring.forward()
    arrived(info_copies)
    merged = info[0]
    for i in (1, 2, 3):
        merged = merge(merged, info[i])

    def ref_sum(s):
        o = s // 2
        lane = lax.broadcasted_iota(jnp.int32, (1, 2 * LEN), 1)
        mask = jnp.where(lane // LEN == s % 2, masks[o], 0)
        peak, total, picked = (merged[i, 1 + o : 2 + o] for i in range(3))
        return valid(mask, picked - peak - jnp.log(total))

    margin = jnp.zeros((SEQS, 2 * LEN), f32)
    for s in range(SEQS):
        ratio = info[s // 2, 1 + s % 2, 0:1, :] - ref_sum(s)
        margin += pairs[:, s : s + 1] * ratio
    margin *= beta_value
    log_sigmoid = jnp.minimum(margin, 0.0) - jnp.log1p(jnp.exp(-jnp.abs(margin)))
    loss[...] = jnp.broadcast_to(
        jnp.sum(log_sigmoid, axis=0, keepdims=True)[:, 0:128] * (-1.0 / SEQS), (8, 128)
    )
    weights = (
        (-loss_scale * beta_value / PAIRS)
        * jax.nn.sigmoid(-margin)
        * pairs[:, SEQS : SEQS + 1]
    )
    token_weights[...] = weights

    core_at, y_at, z_at = move.used, move.used + 8, move.used + 32
    move.used += 38

    def z_copies():
        copies = []
        for i in (1, 3, 2):
            there = (z + i) % 4
            k = z_at + 2 * i - 2
            copies.append(move.make(k, row_ssend.at[8], row_srecv.at[16 + i - 1], at.on_z(i)))
            part = y_send.at[0, pl.ds(pl.multiple_of(there * count, count), count), :]
            copies.append(move.make(k + 1, part, z_recv.at[i - 1], at.on_z(i)))
        return copies

    def core_copies(t):
        return [
            move.make(core_at + 2 * t, row_ssend.at[t], row_srecv.at[t], at.other_core()),
            move.make(core_at + 2 * t + 1, qrecv.at[4 + t % 2, 0:LEN, :], qrecv.at[t, 0:LEN, :], at.other_core()),
        ]

    def y_copies(t):
        copies = []
        for i in (1, 3, 2):
            k = t * 3 + i - 1
            there = (y + i) % 4
            part = y_send.at[t % 2, pl.ds(pl.multiple_of(there * count, count), count), :]
            copies.append(
                move.make(y_at + 2 * k, row_ssend.at[4 + t], row_srecv.at[4 + k], at.on_y(i))
            )
            into = qsend.at[t, (i - 1) * count : i * count, :]
            copies.append(move.make(y_at + 2 * k + 1, part, into, at.on_y(i)))
        return copies

    def grad_part(owner, f, cols):
        return refs[owner, :, :, f, :, 0, :, cols].reshape(2 * LEN, -1)[0:share]

    def out_copies(owner):
        return [
            pltpu.make_async_copy(
                refs.at[owner, :, :, f, :, 0],
                grad_out.at[owner, :, :, :, :, pl.ds(f * quarter, quarter)],
                local.at[2 * owner + f],
            )
            for f in (0, 1)
        ]

    def turned_copy(k):
        rows = pl.ds(pl.multiple_of(k * 2 * LEN, 2 * LEN), 2 * LEN)
        return pltpu.make_async_copy(
            turned, turned_out.at[rows, :], local.at[8]
        )

    def turn(k):
        rows = pl.ds(pl.multiple_of(k * 2 * LEN, 2 * LEN), 2 * LEN)

        @pl.when(k >= 1)
        def _():
            turned_copy(k - 1).wait()

        turned[...] = jnp.transpose(kept[:, :, rows].reshape(4 * share, 2 * LEN))
        turned_copy(k).start()

    def sent(copies):
        for copy in copies:
            copy.wait_send()

    def owner_of(t):
        return (x + t + t // 2 - 2 * (t // 3)) % 4

    mine_rows = pl.ds(pl.multiple_of(y * count, count), count)

    def rows_of(owner):
        return pl.ds(pl.multiple_of(owner * count, count), count)

    @pl.loop(0, 6)
    def _(t):
        @pl.when(t == 3)
        def _():
            ring.end()

        @pl.when((t >= 2) & (t < 4))
        def _():
            sent(core_copies(t - 2))

        @pl.when(t < 4)
        def _():
            slot = t % 2
            owner = owner_of(t)
            mask_a, mask_b = kept_mask[owner, 0:1, :], kept_mask[owner, 1:2, :]
            weight_a = token_weights[pl.ds(2 * owner, 1), :]
            weight_b = token_weights[pl.ds(2 * owner + 1, 1), :]
            token = mask_a * weight_a + mask_b * weight_b
            factor = jnp.where(
                mask_a + mask_b > 0, token * jnp.exp(info[owner, 0, 5:6, :] - info[owner, 0, 0:1, :]), 0.0
            )
            column[...] = to_column(token)
            third[...] = to_column(factor)

            def read(rows):
                hits = entries(ROWS) == wide(kept_wanted[owner, rows, :], width)
                return (
                    jnp.where(hits, wide(column[rows, :], width), 0.0)
                    - wide(third[rows, :], width) * spread[owner, rows, :].astype(f32)
                ).astype(bf16)

            @pl.loop(0, share // ROWS)
            def _(r):
                value = read(pl.ds(pl.multiple_of(r * ROWS, ROWS), ROWS))
                refs[owner, r // 4, r // 2 % 2, 0, r % 2, 0] = value[:, 0:half]
                refs[owner, r // 4, r // 2 % 2, 1, r % 2, 0] = value[:, half:]

            for copy in out_copies(owner):
                copy.start()

            for f in (0, 1):

                @pl.loop(0, half // tile)
                def _(j):
                    cols = pl.ds(pl.multiple_of(j * tile, tile), tile)
                    there = pl.ds(pl.multiple_of(f * half + j * tile, tile), tile)
                    grad_full[:, there] = jnp.dot(
                        place[owner], grad_part(owner, f, cols), preferred_element_type=f32
                    ).astype(bf16)

            @pl.loop(0, depth // tile)
            def _(j):
                cols = pl.ds(pl.multiple_of(j * tile, tile), tile)
                rows_all[slot, :, SKIP:LEN, cols] = lax.dot_general(
                    grad_full[...],
                    weight[cols, :],
                    (((1,), (1,)), ((), ())),
                    preferred_element_type=f32,
                ).reshape(2, KEEP, tile)

            def write(rows, code):
                qrecv[4 + slot, rows, :] = code

            row_ssend[t] = encode(LEN, lambda rows: rows_all[slot, 1 - c, rows, :], write)
            for copy in core_copies(t):
                copy.start()

        @pl.when((t >= 3) & (t < 5))
        def _():
            sent(y_copies(t - 3))

        @pl.when((t >= 1) & (t < 5))
        def _():
            u = t - 1
            slot = u % 2
            for copy in core_copies(u):
                copy.wait_recv()
            third[...] = to_column(row_srecv[u, 0:1, :])

            def read(rows):
                return rows_all[slot, c, rows, :] + decode(qrecv[u, rows, :], third[rows, :])

            def store(rows, value=None):
                if value is None:
                    return rows_all[slot, c, rows, :]
                rows_all[slot, c, rows, :] = value

            def write(rows, code):
                y_send[slot, rows, :] = code

            row_ssend[4 + u] = encode(LEN, read, write, store)
            for copy in y_copies(u):
                copy.start()
            z_sum[rows_of(owner_of(u)), :] = rows_all[slot, c, mine_rows, :]

        @pl.when(t >= 2)
        def _():
            v = t - 2
            for copy in y_copies(v):
                copy.wait_recv()
            total = z_sum[rows_of(owner_of(v)), :]
            for i in range(3):
                k = v * 3 + i
                column[...] = to_column(row_srecv[4 + k, 0:1, :])
                code = qsend[v, i * count : (i + 1) * count, :]
                total += decode(code, column[mine_rows, :])
            z_sum[rows_of(owner_of(v)), :] = total

        @pl.when(t == 5)
        def _():
            for u in (2, 3):
                sent(core_copies(u))
                sent(y_copies(u))

            def write(rows, code):
                y_send[0, rows, :] = code

            row_ssend[8] = encode(LEN, lambda rows: z_sum[rows, :], write)
            for copy in z_copies():
                copy.start()

        @pl.when(t >= 3)
        def _():
            start = 2 * (t - 3)

            @pl.loop(start, jnp.minimum(start + 2, depth // (2 * LEN)))
            def _(k):
                turn(k)

    for copy in z_copies():
        copy.wait_recv()
    here = pl.ds(pl.multiple_of(z * count, count), count)
    total = z_sum[here, :]
    for i in range(3):
        column[...] = to_column(row_srecv[16 + i, 0:1, :])
        total += decode(z_recv[i], column[here, :])
    rows_out[...] = total
    sent(z_copies())
    turned_copy(depth // (2 * LEN) - 1).wait()
    for owner in range(4):
        for copy in out_copies(owner):
            copy.wait()
    move.finish()


def fused(index, share, states, others, weight, ref_weight, masks, wanted, pair_index, chosen):
    vmem = pl.BlockSpec(memory_space=pltpu.VMEM)
    count, depth = states.shape
    width = weight.shape[1]
    ref_rows, ref_depth = others.shape
    quarter = ref_depth // 4
    f32, bf16, i16 = jnp.float32, jnp.bfloat16, jnp.int16
    lanes = 2 * LEN
    copies = 128
    return pl.pallas_call(
        fused_kernel,
        name="fused_%d" % share,
        out_shape=(
            jax.ShapeDtypeStruct((8, 128), f32),
            jax.ShapeDtypeStruct((count, depth), f32),
            jax.ShapeDtypeStruct((4, 4, 2, 2, 2 * ref_rows, width), bf16),
            jax.ShapeDtypeStruct((depth, 4 * share), bf16),
        ),
        in_specs=[vmem] * 2
        + [pl.BlockSpec(memory_space=pl.ANY)] * 2
        + [vmem] * 2
        + [pl.BlockSpec(memory_space=pltpu.SMEM)] * 2,
        out_specs=(vmem, vmem, pl.BlockSpec(memory_space=pl.ANY), pl.BlockSpec(memory_space=pl.ANY)),
        scratch_shapes=[
            pltpu.VMEM((4, share, depth), bf16),
            pltpu.VMEM((8, 128), f32),
            pltpu.VMEM((lanes, 4 * share), bf16),
            pltpu.VMEM(weight.shape, bf16),
            pltpu.VMEM(ref_weight.shape, bf16),
            pltpu.VMEM((4, 2, 4, count, depth), bf16),
            pltpu.VMEM((4, 4, 2, 2, 2, 2, 2 * ref_rows, quarter), bf16),
            pltpu.VMEM((4, share, width), f32),
            pltpu.VMEM((4, share, width // 2), i16),
            pltpu.VMEM((6, share, width // 2), i16),
            pltpu.VMEM((6, 8, lanes), f32),
            pltpu.VMEM((6, 8, lanes), f32),
            pltpu.VMEM((lanes, 128), f32),
            pltpu.VMEM((lanes, 128), f32),
            pltpu.VMEM((lanes, 128), f32),
            pltpu.VMEM((4, share, 128), f32),
            pltpu.VMEM((4, share, lanes), bf16),
            pltpu.VMEM((4, 2 * KEEP, share), bf16),
            pltpu.VMEM((4, 8, lanes), f32),
            pltpu.VMEM((4, share, width), bf16),
            pltpu.VMEM((4, 4, 2, 2, 2 * ref_rows, ref_weight.shape[1]), f32),
            pltpu.VMEM((4, lanes, 128), f32),
            pltpu.VMEM((4, 8, lanes), f32),
            pltpu.VMEM((3, 3, 8, lanes), f32),
            pltpu.VMEM((7, 3, 8, lanes), f32),
            pltpu.VMEM((4, 3, 8, lanes), f32),
            pltpu.VMEM((8, lanes), f32),
            pltpu.VMEM((2 * KEEP, width), bf16),
            pltpu.VMEM((2, 2, LEN, depth), f32),
            pltpu.VMEM((2, LEN, depth), i16),
            pltpu.VMEM((3, count, depth), i16),
            pltpu.VMEM((LEN, depth), f32),
            pltpu.VMEM((9, 8, lanes), f32),
            pltpu.VMEM((19, 8, lanes), f32),
            pltpu.SemaphoreType.DMA((copies,)),
            pltpu.SemaphoreType.DMA((copies,)),
            pltpu.SemaphoreType.DMA((12,)),
        ],
        compiler_params=pltpu.CompilerParams(
            collective_id=index, has_side_effects=True, vmem_limit_bytes=VMEM_LIMIT
        ),
    )(states, others, weight, ref_weight, masks, wanted, pair_index, chosen)


def weight_kernel(turned, grad, out):
    whole = jnp.concatenate([grad[owner] for owner in range(4)], axis=0)
    out[...] = jnp.dot(turned[...], whole, preferred_element_type=jnp.float32)


def weight_gradient(turned, grad):
    depth, tokens = turned.shape
    width = grad.shape[2]
    tile = 512
    return pl.pallas_call(
        weight_kernel,
        name="weight_gradient",
        grid=(width // tile,),
        out_shape=jax.ShapeDtypeStruct((depth, width), jnp.float32),
        in_specs=[
            pl.BlockSpec((depth, tokens), lambda j: (0, 0)),
            pl.BlockSpec((4, tokens // 4, tile), lambda j: (0, 0, j)),
        ],
        out_specs=pl.BlockSpec((depth, tile), lambda j: (0, j)),
        compiler_params=pltpu.CompilerParams(vmem_limit_bytes=VMEM_LIMIT),
    )(turned, grad)


def on_device(
    policy_states,
    reference_states,
    policy_weight,
    reference_weight,
    targets,
    response_mask,
    pair_index,
    chosen_flag,
):
    masks = response_mask.reshape(4, 1, 2 * LEN)
    wanted = targets.reshape(4, 1, 2 * LEN)

    def run(index):
        def branch(*operands):
            loss, grad_states, grad, turned = fused(index, SIZES[index], *operands)
            grad_weight = weight_gradient(turned, grad.reshape(4, 2 * LEN, -1))
            return (loss[0, 0], grad_states, grad_weight)

        return branch

    longest = jnp.max(jnp.sum(response_mask.reshape(4, 2 * LEN), axis=1))
    size = sum((longest > s).astype(jnp.int32) for s in SIZES[:-1])
    return lax.switch(
        size,
        [run(i) for i in range(len(SIZES))],
        policy_states,
        reference_states,
        policy_weight,
        reference_weight,
        masks,
        wanted,
        pair_index,
        chosen_flag,
    )


def solution(mesh):
    in_specs = (
        P(("col", "depth"), "row"),
        P(("row", "col", "depth"), None),
        P("row", ("col", "depth")),
        P(None, ("row", "col", "depth")),
        P(),
        P(),
        P(),
        P(),
    )
    out_specs = (P(), P(("col", "depth"), "row"), P("row", ("col", "depth")))
    return jax.shard_map(
        on_device, mesh=mesh, in_specs=in_specs, out_specs=out_specs, check_vma=False
    )
```

```python
import functools

import jax
import jax.numpy as jnp
from jax import lax
from jax.experimental import pallas as pl
from jax.experimental.pallas import tpu as pltpu
from jax.sharding import PartitionSpec as P

PAIRS = 4
LEN = 128
SEQS = 8
SKIP = 16
KEEP = LEN - SKIP
SIZES = (192, 2 * KEEP)

beta_value = 0.1
loss_scale = 256.0

MESH = pl.DeviceIdType.MESH
VMEM_LIMIT = 62 * 1024 * 1024
ROWS = 16


class Place:
    def __init__(self):
        self.x = lax.axis_index("row")
        col = lax.axis_index("col")
        self.z = col // 2
        self.c = col % 2
        self.y = lax.axis_index("depth")

    def on_x(self, step):
        return ((self.x + step) % 4, self.z * 2 + self.c, self.y)

    def on_y(self, step):
        return (self.x, self.z * 2 + self.c, (self.y + step) % 4)

    def on_z(self, step):
        return (self.x, ((self.z + step) % 4) * 2 + self.c, self.y)

    def partner_y(self):
        return (self.x, self.z * 2 + self.c, self.y + 1 - 2 * (self.y % 2))

    def other_core(self):
        return (self.x, self.z * 2 + 1 - self.c, self.y)


def greet(peers):
    barrier = pltpu.get_barrier_semaphore()
    for peer in peers:
        pl.semaphore_signal(barrier, inc=1, device_id=peer, device_id_type=MESH)
    pl.semaphore_wait(barrier, len(peers))


class Mover:
    def __init__(self, send, recv):
        self.send, self.recv, self.used, self.all = send, recv, 0, []

    def make(self, k, src, dst, peer):
        return pltpu.make_async_remote_copy(
            src_ref=src,
            dst_ref=dst,
            send_sem=self.send.at[k],
            recv_sem=self.recv.at[k],
            device_id=peer,
            device_id_type=MESH,
        )

    def start(self, src, dst, peer):
        copy = self.make(self.used, src, dst, peer)
        self.used += 1
        copy.start()
        self.all.append(copy)
        return copy

    def sent(self, copy):
        copy.wait_send()
        self.all = [other for other in self.all if other is not copy]

    def finish(self):
        for copy in self.all:
            copy.wait_send()


class Ring:
    def __init__(self, mover, me, view, peer):
        self.mover, self.me, self.view, self.peer = mover, me, view, peer

    def begin(self):
        own = self.view(self.me, None)
        self.right = self.mover.start(own, own, self.peer(1))
        self.left = self.mover.start(own, own, self.peer(3))

    def forward(self):
        self.right.wait_recv()
        part = self.view((self.me + 3) % 4, 0)
        self.far_right = self.mover.start(part, part, self.peer(1))
        self.left.wait_recv()
        part = self.view((self.me + 1) % 4, 1)
        self.far_left = self.mover.start(part, part, self.peer(3))

    def copies(self):
        return [self.right, self.left, self.far_right, self.far_left]

    def end(self):
        self.far_right.wait_recv()
        self.far_left.wait_recv()


def merge(a, b):
    peak = jnp.maximum(a[0], b[0])
    total = a[1] * jnp.exp(a[0] - peak) + b[1] * jnp.exp(b[0] - peak)
    return jnp.stack([peak, total, a[2] + b[2]])


def over(count, read, write, unroll):
    def group(steps):
        rows = [pl.ds(pl.multiple_of(step * ROWS, ROWS), ROWS) for step in steps]
        for r, value in zip(rows, [read(r) for r in rows]):
            write(r, value)

    steps = count // ROWS
    whole = steps // unroll

    @pl.loop(0, whole)
    def _(g):
        group([g * unroll + u for u in range(unroll)])

    if steps % unroll:
        group(list(range(whole * unroll, steps)))


def wide(value, width):
    return jnp.concatenate([value] * (width // 128), axis=1)


def fold(op, value):
    parts = [value[:, k : k + 128] for k in range(0, value.shape[1], 128)]
    while len(parts) > 1:
        paired = [op(a, b) for a, b in zip(parts[::2], parts[1::2])]
        parts = paired + parts[len(paired) * 2 :]
    return parts[0]


def to_column(row):
    return jnp.transpose(jnp.broadcast_to(row, (128, row.shape[1])))


def span(half, count):
    return slice(None) if half is None else pl.ds(half * (count // 2), count // 2)


def fused_kernel(
    own,
    ref_own,
    weight_in,
    ref_weight_in,
    masks,
    wanted,
    pair_index,
    chosen_flag,
    loss,
    rows_out,
    grad_out,
    turned_out,
    kept,
    pairs,
    turned,
    weight,
    ref_weight,
    gathered,
    refs,
    partial,
    qsend,
    qrecv,
    ssend,
    srecv,
    column,
    inverse,
    third,
    kept_wanted,
    choose,
    place,
    kept_mask,
    spread,
    ref_logits,
    ref_column,
    ref_stats,
    held,
    got,
    info,
    token_weights,
    grad_full,
    rows_all,
    y_send,
    z_recv,
    z_sum,
    row_ssend,
    row_srecv,
    send,
    recv,
    local,
):
    at = Place()
    x, z, c, y = at.x, at.z, at.c, at.y
    share, width = spread.shape[1], spread.shape[2]
    depth = own.shape[1]
    half = width // 2
    f32, bf16 = jnp.float32, jnp.bfloat16
    fetch = [
        pltpu.make_async_copy(weight_in, weight, local.at[10]),
        pltpu.make_async_copy(ref_weight_in, ref_weight, local.at[11]),
    ]
    for copy in fetch:
        copy.start()
    def arrived(copies):
        for copy in copies:
            copy.wait_recv()

    ways = [at.on_x, at.on_y, at.on_z]
    greet([way(i) for way in ways for i in (1, 2, 3)] + [at.other_core()])
    move = Mover(send, recv)

    gathered[z, c, y] = own[...]
    low, high = pl.ds(0, depth // 2), pl.ds(depth // 2, depth // 2)
    count = own.shape[0]
    first_y = [(gathered.at[z, c, y, :, low], at.on_y(i)) for i in (1, 3, 2)]
    first_z = [(gathered.at[z, c, y, :, high], at.on_z(i)) for i in (1, 3, 2)]
    then_z = Ring(move, z, lambda i, h: gathered.at[i, c, span(h, 4), :, low], at.on_z)
    then_y = Ring(move, y, lambda i, h: gathered.at[span(h, 4), c, i, :, high], at.on_y)
    first_y = [move.start(part, part, peer) for part, peer in first_y]
    first_z = [move.start(part, part, peer) for part, peer in first_z]

    side, pair = y % 2, y // 2
    ref_depth = ref_own.shape[1]
    quarter = ref_depth // 4
    for k in range(4):
        z_sum[8 * k : 8 * k + 8, :] = ref_own[:, k * quarter : (k + 1) * quarter].astype(f32)
    swap = move.start(
        z_sum.at[pl.ds(pl.multiple_of(16 - 16 * side, 16), 16), :],
        z_sum.at[32:48, :],
        at.partner_y(),
    )
    column[...] = jnp.zeros_like(column)
    swap.wait_recv()
    mine, theirs = z_sum[pl.ds(pl.multiple_of(16 * side, 16), 16), :], z_sum[32:48, :]
    for f in (0, 1):
        a, b = mine[8 * f : 8 * f + 8], theirs[8 * f : 8 * f + 8]
        block = [jnp.where(side == 0, a, b), jnp.where(side == 0, b, a)]
        refs[x, z, c, f, pair, side] = jnp.concatenate(block, axis=0).astype(bf16)
    move.sent(swap)
    ref_x = Ring(
        move,
        x,
        lambda i, h: refs.at[i, z, c, slice(None) if h is None else h, pair, side],
        at.on_x,
    )
    ref_y = Ring(move, y, lambda i, h: refs.at[span(h, 4), z, c, 0, i // 2, i % 2], at.on_y)
    ref_z = Ring(move, z, lambda i, h: refs.at[span(h, 4), i, c, 1, pair, side], at.on_z)
    ref_yz = Ring(move, z, lambda i, h: refs.at[span(h, 4), i, c, 0], at.on_z)
    ref_zy = Ring(move, y, lambda i, h: refs.at[span(h, 4), :, c, 1, i // 2, i % 2], at.on_y)
    ref_core = []
    ref_rings = [ref_x, ref_y, ref_z, ref_yz, ref_zy]

    def to_core(ring, i):
        part = ring.view((ring.me + i) % 4, None)
        ref_core.append(move.start(part, part, at.other_core()))

    own_core = []

    def share_core(ring, steps):
        for i in steps:
            part = ring.view((ring.me + i) % 4, None)
            own_core.append(move.start(part, part, at.other_core()))

    arrived(first_y)
    then_z.begin()
    share_core(then_z, (0,))
    arrived(first_z)
    then_y.begin()
    share_core(then_y, (0,))
    ref_x.begin()

    def runs(owner):
        lane = lax.broadcasted_iota(jnp.int32, (1, 2 * LEN), 1)
        mask = masks[owner]
        a = jnp.where(lane < LEN, mask, 0)
        b = jnp.where(lane < LEN, 0, mask)
        return (
            jnp.sum(a, axis=1, keepdims=True),
            jnp.sum(b, axis=1, keepdims=True),
            jnp.min(jnp.where(a > 0, lane, 2 * LEN), axis=1, keepdims=True),
            jnp.min(jnp.where(b > 0, lane, 2 * LEN), axis=1, keepdims=True),
        )

    def source(owner, i):
        len_a, len_b, start_a, start_b = runs(owner)
        second = jnp.where(i < len_a + len_b, start_b + i - len_a, -1)
        return jnp.where(i < len_a, start_a + i, second)

    def kept_masks(owner):
        len_a, len_b, _, _ = runs(owner)
        i = lax.broadcasted_iota(jnp.int32, (1, 2 * LEN), 1)
        a = (i < len_a).astype(f32)
        return a, (i < len_a + len_b).astype(f32) - a

    for k in range(4):
        ref_column[k] = to_column(wanted[k].astype(f32))

    lane = lax.broadcasted_iota(jnp.int32, (1, 128), 1)
    signs = [(2 * chosen_flag[s] - 1).astype(f32) for s in range(SEQS)]
    for s in range(SEQS):
        row = jnp.where(lane == SEQS, signs[s], 0.0)
        for other in range(SEQS):
            sign = jnp.where(pair_index[s] == pair_index[other], signs[other], 0.0)
            row += jnp.where(lane == other, sign, 0.0)
        pairs[s : s + 1, :] = row

    @pl.loop(0, 4)
    def _(o):
        to = source(o, lax.broadcasted_iota(jnp.int32, (share, 1), 0))
        here = lax.broadcasted_iota(jnp.int32, (share, 2 * LEN), 1) == to
        choose[o] = here.astype(bf16)
        target = jnp.sum(jnp.where(here, wanted[o].astype(f32), 0.0), axis=1, keepdims=True)
        kept_wanted[o] = jnp.broadcast_to(target, (share, 128))
        to = source(o, lax.broadcasted_iota(jnp.int32, (1, share), 1))
        row = lax.broadcasted_iota(jnp.int32, (2 * KEEP, share), 0) + SKIP
        place[o] = (row + jnp.where(row >= LEN, SKIP, 0) == to).astype(bf16)
        mask_a, mask_b = kept_masks(o)
        kept_mask[o, 0:1, :] = mask_a
        kept_mask[o, 1:2, :] = mask_b

    then_z.forward()
    share_core(then_z, (1, 3))
    then_y.forward()
    share_core(then_y, (1, 3))
    ref_x.forward()
    then_z.end()
    share_core(then_z, (2,))
    ref_x.end()
    ref_y.begin()
    ref_z.begin()
    then_y.end()
    share_core(then_y, (2,))
    ref_logits[...] = jnp.zeros_like(ref_logits)
    rows_all[:, :, 0:SKIP, :] = jnp.zeros((2, 2, SKIP, depth), f32)
    ref_y.forward()
    ref_z.forward()
    fetch[0].wait()
    for copy in own_core:
        copy.wait_recv()

    tile = 640

    def product(owner):
        whole = gathered[owner].reshape(2 * LEN, depth)
        kept[owner] = jnp.dot(choose[owner], whole, preferred_element_type=f32).astype(bf16)

        @pl.loop(0, width // tile)
        def _(j):
            cols = pl.ds(pl.multiple_of(j * tile, tile), tile)
            partial[owner, :, cols] = jnp.dot(
                kept[owner], weight[:, cols], preferred_element_type=f32
            )

    def encode(count, read, write, store=None):
        def top(rows, value):
            if store is not None:
                store(rows, value)
            column[rows, :] = fold(jnp.maximum, jnp.abs(value))

        over(count, read, top, 2)
        peak = jnp.max(column[0:count, :], axis=1, keepdims=True)
        step = jnp.broadcast_to(jnp.maximum(peak, 1e-30) * (1.0 / 32767.0), (count, 128))
        column[0:count, :] = step
        inverse[0:count, :] = 1.0 / step

        def code(rows):
            value = read(rows) if store is None else store(rows)
            value = value * wide(inverse[rows, :], value.shape[1])
            return jnp.round(value).astype(jnp.int32).astype(jnp.int16)

        over(count, code, write, 2)
        return jnp.transpose(column[...])[0:8]

    def decode(code, step):
        return code.astype(jnp.int32).astype(f32) * wide(step, code.shape[1])

    def pack(k, owner, part, peer, add=None):
        cols = pl.ds(part * half, half)
        slot = k % 3 % 2 + k // 3 * 2

        def plain(rows):
            return partial[owner, rows, cols]

        def summed(rows):
            return plain(rows) + decode(qrecv[add, rows, :], third[rows, :])

        def store(rows, value=None):
            if value is None:
                return plain(rows)
            partial[owner, rows, cols] = value

        def write(rows, code):
            qsend[slot, rows, :] = code

        if add is None:
            ssend[k] = encode(share, plain, write)
        else:
            third[...] = to_column(srecv[add, 0:1, :])
            ssend[k] = encode(share, summed, write, store)
        return (
            move.start(ssend.at[k], srecv.at[k], peer),
            move.start(qsend.at[slot], qrecv.at[k], peer),
        )

    def add_in(k, part):
        cols = pl.ds(part * half, half)
        column[...] = to_column(srecv[k, 0:1, :])

        def read(rows):
            return partial[x, rows, cols] + decode(qrecv[k, rows, :], column[rows, :])

        def write(rows, value):
            partial[x, rows, cols] = value

        over(share, read, write, 2)

    right, left = at.on_x(1), at.on_x(3)
    after, before, across = (x + 1) % 4, (x + 3) % 4, (x + 2) % 4
    product(across)
    r0 = pack(0, across, 0, right)
    l0 = pack(3, across, 1, left)
    ref_y.end()
    ref_yz.begin()
    to_core(ref_yz, 0)
    ref_z.end()
    ref_zy.begin()
    to_core(ref_zy, 0)
    product(after)
    r1 = pack(1, after, 1, right)
    product(before)
    l1 = pack(4, before, 0, left)
    product(x)

    def ref_product(e):
        step = e + e // 2 - 2 * (e // 3)
        plane, row = (z + step) % 4, (y + step) % 4
        part = jnp.zeros((2 * LEN, ref_weight.shape[1]), f32)
        for h in (0, 1):
            part += jnp.dot(
                refs[:, plane, :, 0, :, h].reshape(2 * LEN, quarter),
                ref_weight[2 * h * quarter : (2 * h + 1) * quarter, :],
                preferred_element_type=f32,
            )
        ref_logits[:, plane] += part.reshape(4, 2, 2, 16, ref_weight.shape[1])
        there = pl.ds(pl.multiple_of((row % 2 * 2 + 1) * quarter, quarter), quarter)

        @pl.loop(0, 2)
        def _(i):
            half_x = pl.ds(2 * i, 2)
            part = jnp.dot(
                refs[half_x, :, :, 1, row // 2, row % 2].reshape(2 * LEN, quarter),
                ref_weight[there, :],
                preferred_element_type=f32,
            )
            ref_logits[half_x, :, :, row // 2] += part.reshape(2, 4, 2, 16, ref_weight.shape[1])

    fetch[1].wait()
    arrived(ref_core[0:2])
    ref_product(0)
    arrived(r0)
    move.sent(r0[1])
    r2 = pack(2, after, 0, right, add=0)
    arrived(l0)
    move.sent(l0[1])
    l2 = pack(5, before, 1, left, add=3)
    ref_yz.forward()
    to_core(ref_yz, 1)
    to_core(ref_yz, 3)
    ref_zy.forward()
    to_core(ref_zy, 1)
    to_core(ref_zy, 3)
    arrived(r1)
    add_in(1, 1)
    arrived(l1)
    add_in(4, 0)
    ref_yz.end()
    to_core(ref_yz, 2)
    ref_zy.end()
    to_core(ref_zy, 2)
    arrived(ref_core[2:6])

    @pl.loop(1, 3)
    def _(e):
        ref_product(e)

    arrived(r2)
    arrived(l2)
    column[...] = to_column(srecv[2, 0:1, :])
    third[...] = to_column(srecv[5, 0:1, :])
    first = (lax.axis_index("col") * 4 + y) * width

    def entries(rows_count):
        lane = lax.broadcasted_iota(jnp.int32, (rows_count, width), 1)
        return (lane + first).astype(f32)

    def read(rows):
        codes = (decode(qrecv[2, rows, :], column[rows, :]), decode(qrecv[5, rows, :], third[rows, :]))
        return partial[x, rows, :] + jnp.concatenate(codes, axis=1)

    def write(rows, value):
        partial[x, rows, :] = value
        hits = entries(ROWS) == wide(kept_wanted[x, rows, :], width)
        column[rows, :] = fold(jnp.maximum, value)
        third[rows, :] = fold(jnp.add, jnp.where(hits, value, 0.0))

    over(share, read, write, 1)
    peak = jnp.broadcast_to(jnp.max(column[0:share, :], axis=1, keepdims=True), (share, 128))
    column[0:share, :] = peak

    def read(rows):
        return jnp.exp(partial[x, rows, :] - wide(column[rows, :], width))

    def write(rows, value):
        spread[x, rows, :] = value.astype(bf16)
        inverse[rows, :] = fold(jnp.add, value)

    over(share, read, write, 1)
    ring = Ring(
        move,
        x,
        lambda i, h: spread.at[i] if h is None else spread.at[i, :, pl.ds(h * half, half)],
        at.on_x,
    )
    ring.begin()
    total = jnp.sum(inverse[0:share, :], axis=1, keepdims=True)
    picked = jnp.sum(third[0:share, :], axis=1, keepdims=True)
    lane = lax.broadcasted_iota(jnp.int32, (share, 128), 1)
    column[0:share, :] = jnp.where(
        lane == 0, column[0:share, :], jnp.where(lane == 1, total, picked)
    )
    stats = jnp.transpose(column[...])[0:8]
    local_peak = stats[0:1]

    arrived(ref_core[6:8])
    ref_product(3)
    ref_width = ref_weight.shape[1]
    ref_entry = lax.axis_index("row") * 32 + lax.axis_index("col") * 4 + y

    @pl.loop(0, 16)
    def _(k):
        i, j = k // 4, k % 4
        rows = pl.ds(pl.multiple_of(j * 64, 64), 64)
        logits = ref_logits[i, j].reshape(64, ref_width)
        peak = jnp.max(logits, axis=1, keepdims=True)
        total = jnp.sum(jnp.exp(logits - peak), axis=1, keepdims=True)
        entry = (
            lax.broadcasted_iota(jnp.int32, (64, ref_width), 1) + ref_entry * ref_width
        ).astype(f32)
        picked = jnp.sum(
            jnp.where(entry == ref_column[i, rows, 0:1], logits, 0.0), axis=1, keepdims=True
        )
        lanes = lax.broadcasted_iota(jnp.int32, (64, 128), 1)
        ref_column[i, rows, :] = jnp.where(lanes == 0, peak, jnp.where(lanes == 1, total, picked))

    for i in range(4):
        ref_stats[i] = jnp.transpose(ref_column[i])[0:8]
    for copy in ref_core + [ring_copy for r in ref_rings for ring_copy in r.copies()]:
        move.sent(copy)

    for copies in (r1, l1, r2, l2):
        move.sent(copies[1])

    zeros = jnp.zeros((3, 2 * LEN), f32)
    every = jnp.stack(
        [
            jnp.concatenate(
                [stats[i : i + 1]] + [ref_stats[o, i : i + 1, :] for o in range(4)] + [zeros], axis=0
            )
            for i in range(3)
        ]
    )
    stages = [[at.other_core()], [at.on_y(i) for i in (1, 2, 3)], [at.on_z(i) for i in (1, 2, 3)]]
    slot = 0
    for s, peers in enumerate(stages):
        held[s] = every
        copies = [move.start(held.at[s], got.at[slot + k], peer) for k, peer in enumerate(peers)]
        arrived(copies)
        for k in range(len(peers)):
            every = merge(every, got[slot + k])
        slot += len(peers)

    def valid(mask, value):
        return jnp.sum(jnp.where(mask > 0, value, 0.0), axis=-1, keepdims=True)

    normalizer = every[0, 0:1] + jnp.log(every[1, 0:1])
    logp = every[2, 0:1] - normalizer
    sums = [
        jnp.broadcast_to(valid(kept_mask[x, i : i + 1, :], logp), (1, 2 * LEN)) for i in (0, 1)
    ]
    info[x, 0] = jnp.concatenate([normalizer, every[0, 1:5], local_peak, zeros[0:2]], axis=0)
    info[x, 1] = jnp.concatenate([sums[0], every[1, 1:8]], axis=0)
    info[x, 2] = jnp.concatenate([sums[1], every[2, 1:8]], axis=0)
    info_copies = [move.start(info.at[x], info.at[x], at.on_x(i)) for i in (1, 2, 3)]
    ring.forward()
    arrived(info_copies)
    merged = info[0]
    for i in (1, 2, 3):
        merged = merge(merged, info[i])

    def ref_sum(s):
        o = s // 2
        lane = lax.broadcasted_iota(jnp.int32, (1, 2 * LEN), 1)
        mask = jnp.where(lane // LEN == s % 2, masks[o], 0)
        peak, total, picked = (merged[i, 1 + o : 2 + o] for i in range(3))
        return valid(mask, picked - peak - jnp.log(total))

    margin = jnp.zeros((SEQS, 2 * LEN), f32)
    for s in range(SEQS):
        ratio = info[s // 2, 1 + s % 2, 0:1, :] - ref_sum(s)
        margin += pairs[:, s : s + 1] * ratio
    margin *= beta_value
    log_sigmoid = jnp.minimum(margin, 0.0) - jnp.log1p(jnp.exp(-jnp.abs(margin)))
    loss[...] = jnp.broadcast_to(
        jnp.sum(log_sigmoid, axis=0, keepdims=True)[:, 0:128] * (-1.0 / SEQS), (8, 128)
    )
    weights = (
        (-loss_scale * beta_value / PAIRS)
        * jax.nn.sigmoid(-margin)
        * pairs[:, SEQS : SEQS + 1]
    )
    token_weights[...] = weights

    core_at, y_at, z_at = move.used, move.used + 8, move.used + 32
    move.used += 38

    def z_copies():
        copies = []
        for i in (1, 3, 2):
            there = (z + i) % 4
            k = z_at + 2 * i - 2
            copies.append(move.make(k, row_ssend.at[8], row_srecv.at[16 + i - 1], at.on_z(i)))
            part = y_send.at[0, pl.ds(pl.multiple_of(there * count, count), count), :]
            copies.append(move.make(k + 1, part, z_recv.at[i - 1], at.on_z(i)))
        return copies

    def core_copies(t):
        return [
            move.make(core_at + 2 * t, row_ssend.at[t], row_srecv.at[t], at.other_core()),
            move.make(core_at + 2 * t + 1, qrecv.at[4 + t % 2, 0:LEN, :], qrecv.at[t, 0:LEN, :], at.other_core()),
        ]

    def y_copies(t):
        copies = []
        for i in (1, 3, 2):
            k = t * 3 + i - 1
            there = (y + i) % 4
            part = y_send.at[t % 2, pl.ds(pl.multiple_of(there * count, count), count), :]
            copies.append(
                move.make(y_at + 2 * k, row_ssend.at[4 + t], row_srecv.at[4 + k], at.on_y(i))
            )
            into = qsend.at[t, (i - 1) * count : i * count, :]
            copies.append(move.make(y_at + 2 * k + 1, part, into, at.on_y(i)))
        return copies

    def grad_part(owner, f, cols):
        return refs[owner, :, :, f, :, 0, :, cols].reshape(2 * LEN, -1)[0:share]

    def out_copies(owner):
        return [
            pltpu.make_async_copy(
                refs.at[owner, :, :, f, :, 0],
                grad_out.at[owner, :, :, :, :, pl.ds(f * quarter, quarter)],
                local.at[2 * owner + f],
            )
            for f in (0, 1)
        ]

    def turned_copy(k):
        rows = pl.ds(pl.multiple_of(k * 2 * LEN, 2 * LEN), 2 * LEN)
        return pltpu.make_async_copy(
            turned, turned_out.at[rows, :], local.at[8]
        )

    def turn(k):
        rows = pl.ds(pl.multiple_of(k * 2 * LEN, 2 * LEN), 2 * LEN)

        @pl.when(k >= 1)
        def _():
            turned_copy(k - 1).wait()

        turned[...] = jnp.transpose(kept[:, :, rows].reshape(4 * share, 2 * LEN))
        turned_copy(k).start()

    def sent(copies):
        for copy in copies:
            copy.wait_send()

    def owner_of(t):
        return (x + t + t // 2 - 2 * (t // 3)) % 4

    mine_rows = pl.ds(pl.multiple_of(y * count, count), count)

    def rows_of(owner):
        return pl.ds(pl.multiple_of(owner * count, count), count)

    @pl.loop(0, 6)
    def _(t):
        @pl.when(t == 3)
        def _():
            ring.end()

        @pl.when((t >= 2) & (t < 4))
        def _():
            sent(core_copies(t - 2))

        @pl.when(t < 4)
        def _():
            slot = t % 2
            owner = owner_of(t)
            mask_a, mask_b = kept_mask[owner, 0:1, :], kept_mask[owner, 1:2, :]
            weight_a = token_weights[pl.ds(2 * owner, 1), :]
            weight_b = token_weights[pl.ds(2 * owner + 1, 1), :]
            token = mask_a * weight_a + mask_b * weight_b
            factor = jnp.where(
                mask_a + mask_b > 0, token * jnp.exp(info[owner, 0, 5:6, :] - info[owner, 0, 0:1, :]), 0.0
            )
            column[...] = to_column(token)
            third[...] = to_column(factor)

            def read(rows):
                hits = entries(ROWS) == wide(kept_wanted[owner, rows, :], width)
                return (
                    jnp.where(hits, wide(column[rows, :], width), 0.0)
                    - wide(third[rows, :], width) * spread[owner, rows, :].astype(f32)
                ).astype(bf16)

            @pl.loop(0, share // ROWS)
            def _(r):
                value = read(pl.ds(pl.multiple_of(r * ROWS, ROWS), ROWS))
                refs[owner, r // 4, r // 2 % 2, 0, r % 2, 0] = value[:, 0:half]
                refs[owner, r // 4, r // 2 % 2, 1, r % 2, 0] = value[:, half:]

            for copy in out_copies(owner):
                copy.start()

            for f in (0, 1):

                @pl.loop(0, half // tile)
                def _(j):
                    cols = pl.ds(pl.multiple_of(j * tile, tile), tile)
                    there = pl.ds(pl.multiple_of(f * half + j * tile, tile), tile)
                    grad_full[:, there] = jnp.dot(
                        place[owner], grad_part(owner, f, cols), preferred_element_type=f32
                    ).astype(bf16)

            @pl.loop(0, depth // tile)
            def _(j):
                cols = pl.ds(pl.multiple_of(j * tile, tile), tile)
                rows_all[slot, :, SKIP:LEN, cols] = lax.dot_general(
                    grad_full[...],
                    weight[cols, :],
                    (((1,), (1,)), ((), ())),
                    preferred_element_type=f32,
                ).reshape(2, KEEP, tile)

            def write(rows, code):
                qrecv[4 + slot, rows, :] = code

            row_ssend[t] = encode(LEN, lambda rows: rows_all[slot, 1 - c, rows, :], write)
            for copy in core_copies(t):
                copy.start()

        @pl.when((t >= 3) & (t < 5))
        def _():
            sent(y_copies(t - 3))

        @pl.when((t >= 1) & (t < 5))
        def _():
            u = t - 1
            slot = u % 2
            for copy in core_copies(u):
                copy.wait_recv()
            third[...] = to_column(row_srecv[u, 0:1, :])

            def read(rows):
                return rows_all[slot, c, rows, :] + decode(qrecv[u, rows, :], third[rows, :])

            def store(rows, value=None):
                if value is None:
                    return rows_all[slot, c, rows, :]
                rows_all[slot, c, rows, :] = value

            def write(rows, code):
                y_send[slot, rows, :] = code

            row_ssend[4 + u] = encode(LEN, read, write, store)
            for copy in y_copies(u):
                copy.start()
            z_sum[rows_of(owner_of(u)), :] = rows_all[slot, c, mine_rows, :]

        @pl.when(t >= 2)
        def _():
            v = t - 2
            for copy in y_copies(v):
                copy.wait_recv()
            total = z_sum[rows_of(owner_of(v)), :]
            for i in range(3):
                k = v * 3 + i
                column[...] = to_column(row_srecv[4 + k, 0:1, :])
                code = qsend[v, i * count : (i + 1) * count, :]
                total += decode(code, column[mine_rows, :])
            z_sum[rows_of(owner_of(v)), :] = total

        @pl.when(t == 5)
        def _():
            for u in (2, 3):
                sent(core_copies(u))
                sent(y_copies(u))

            def write(rows, code):
                y_send[0, rows, :] = code

            row_ssend[8] = encode(LEN, lambda rows: z_sum[rows, :], write)
            for copy in z_copies():
                copy.start()

        @pl.when(t >= 3)
        def _():
            start = 2 * (t - 3)

            @pl.loop(start, jnp.minimum(start + 2, depth // (2 * LEN)))
            def _(k):
                turn(k)

    for copy in z_copies():
        copy.wait_recv()
    here = pl.ds(pl.multiple_of(z * count, count), count)
    total = z_sum[here, :]
    for i in range(3):
        column[...] = to_column(row_srecv[16 + i, 0:1, :])
        total += decode(z_recv[i], column[here, :])
    rows_out[...] = total
    sent(z_copies())
    turned_copy(depth // (2 * LEN) - 1).wait()
    for owner in range(4):
        for copy in out_copies(owner):
            copy.wait()
    move.finish()


def fused(index, share, states, others, weight, ref_weight, masks, wanted, pair_index, chosen):
    vmem = pl.BlockSpec(memory_space=pltpu.VMEM)
    count, depth = states.shape
    width = weight.shape[1]
    ref_rows, ref_depth = others.shape
    quarter = ref_depth // 4
    f32, bf16, i16 = jnp.float32, jnp.bfloat16, jnp.int16
    lanes = 2 * LEN
    copies = 128
    return pl.pallas_call(
        fused_kernel,
        name="fused_%d" % share,
        out_shape=(
            jax.ShapeDtypeStruct((8, 128), f32),
            jax.ShapeDtypeStruct((count, depth), f32),
            jax.ShapeDtypeStruct((4, 4, 2, 2, 2 * ref_rows, width), bf16),
            jax.ShapeDtypeStruct((depth, 4 * share), bf16),
        ),
        in_specs=[vmem] * 2
        + [pl.BlockSpec(memory_space=pl.ANY)] * 2
        + [vmem] * 2
        + [pl.BlockSpec(memory_space=pltpu.SMEM)] * 2,
        out_specs=(vmem, vmem, pl.BlockSpec(memory_space=pl.ANY), pl.BlockSpec(memory_space=pl.ANY)),
        scratch_shapes=[
            pltpu.VMEM((4, share, depth), bf16),
            pltpu.VMEM((8, 128), f32),
            pltpu.VMEM((lanes, 4 * share), bf16),
            pltpu.VMEM(weight.shape, bf16),
            pltpu.VMEM(ref_weight.shape, bf16),
            pltpu.VMEM((4, 2, 4, count, depth), bf16),
            pltpu.VMEM((4, 4, 2, 2, 2, 2, 2 * ref_rows, quarter), bf16),
            pltpu.VMEM((4, share, width), f32),
            pltpu.VMEM((4, share, width // 2), i16),
            pltpu.VMEM((6, share, width // 2), i16),
            pltpu.VMEM((6, 8, lanes), f32),
            pltpu.VMEM((6, 8, lanes), f32),
            pltpu.VMEM((lanes, 128), f32),
            pltpu.VMEM((lanes, 128), f32),
            pltpu.VMEM((lanes, 128), f32),
            pltpu.VMEM((4, share, 128), f32),
            pltpu.VMEM((4, share, lanes), bf16),
            pltpu.VMEM((4, 2 * KEEP, share), bf16),
            pltpu.VMEM((4, 8, lanes), f32),
            pltpu.VMEM((4, share, width), bf16),
            pltpu.VMEM((4, 4, 2, 2, 2 * ref_rows, ref_weight.shape[1]), f32),
            pltpu.VMEM((4, lanes, 128), f32),
            pltpu.VMEM((4, 8, lanes), f32),
            pltpu.VMEM((3, 3, 8, lanes), f32),
            pltpu.VMEM((7, 3, 8, lanes), f32),
            pltpu.VMEM((4, 3, 8, lanes), f32),
            pltpu.VMEM((8, lanes), f32),
            pltpu.VMEM((2 * KEEP, width), bf16),
            pltpu.VMEM((2, 2, LEN, depth), f32),
            pltpu.VMEM((2, LEN, depth), i16),
            pltpu.VMEM((3, count, depth), i16),
            pltpu.VMEM((LEN, depth), f32),
            pltpu.VMEM((9, 8, lanes), f32),
            pltpu.VMEM((19, 8, lanes), f32),
            pltpu.SemaphoreType.DMA((copies,)),
            pltpu.SemaphoreType.DMA((copies,)),
            pltpu.SemaphoreType.DMA((12,)),
        ],
        compiler_params=pltpu.CompilerParams(
            collective_id=index, has_side_effects=True, vmem_limit_bytes=VMEM_LIMIT
        ),
    )(states, others, weight, ref_weight, masks, wanted, pair_index, chosen)


def weight_kernel(turned, grad, out):
    whole = jnp.concatenate([grad[owner] for owner in range(4)], axis=0)
    out[...] = jnp.dot(turned[...], whole, preferred_element_type=jnp.float32)


def weight_gradient(turned, grad):
    depth, tokens = turned.shape
    width = grad.shape[2]
    tile = 512
    return pl.pallas_call(
        weight_kernel,
        name="weight_gradient",
        grid=(width // tile,),
        out_shape=jax.ShapeDtypeStruct((depth, width), jnp.float32),
        in_specs=[
            pl.BlockSpec((depth, tokens), lambda j: (0, 0)),
            pl.BlockSpec((4, tokens // 4, tile), lambda j: (0, 0, j)),
        ],
        out_specs=pl.BlockSpec((depth, tile), lambda j: (0, j)),
        compiler_params=pltpu.CompilerParams(vmem_limit_bytes=VMEM_LIMIT),
    )(turned, grad)


def on_device(
    policy_states,
    reference_states,
    policy_weight,
    reference_weight,
    targets,
    response_mask,
    pair_index,
    chosen_flag,
):
    masks = response_mask.reshape(4, 1, 2 * LEN)
    wanted = targets.reshape(4, 1, 2 * LEN)

    def run(index):
        def branch(*operands):
            loss, grad_states, grad, turned = fused(index, SIZES[index], *operands)
            grad_weight = weight_gradient(turned, grad.reshape(4, 2 * LEN, -1))
            return (loss[0, 0], grad_states, grad_weight)

        return branch

    longest = jnp.max(jnp.sum(response_mask.reshape(4, 2 * LEN), axis=1))
    size = sum((longest > s).astype(jnp.int32) for s in SIZES[:-1])
    return lax.switch(
        size,
        [run(i) for i in range(len(SIZES))],
        policy_states,
        reference_states,
        policy_weight,
        reference_weight,
        masks,
        wanted,
        pair_index,
        chosen_flag,
    )


def solution(mesh):
    in_specs = (
        P(("col", "depth"), "row"),
        P(("row", "col", "depth"), None),
        P("row", ("col", "depth")),
        P(None, ("row", "col", "depth")),
        P(),
        P(),
        P(),
        P(),
    )
    out_specs = (P(), P(("col", "depth"), "row"), P("row", ("col", "depth")))
    return jax.shard_map(
        on_device, mesh=mesh, in_specs=in_specs, out_specs=out_specs, check_vma=False
    )
```
